1024 devices in a mesh: gx: 16 (over y, x), gy: 64 (over z, core).
Axes of the slice: x: 4, y: 4, z: 32, core: 2. Of those that a mesh axis runs over, the one named last changes fastest.
Arguments:
- background: float32 [8, 1024, 2048], P(None, 'gy', 'gx'), may hold values from 1 to 12
- density: float32 [1024, 2048], P('gy', 'gx'), may hold values from 0 to 1
- design_tiles: int32 [8, 16], replicated, may hold values 0 or 1
- material_tiles: int32 [8, 16], replicated, may hold values from 0 to 3
- contrast: float32 [4], replicated, may hold values from 2 to 10
- source: float32 [3, 8, 1024, 2048], P(None, None, 'gy', 'gx'), may hold values from -18 to 18
- adjoint_source: float32 [3, 8, 1024, 2048], P(None, None, 'gy', 'gx'), may hold values from -18 to 18
- field_start: float32 [3, 8, 1024, 2048], P(None, None, 'gy', 'gx'), may hold values from -6 to 6
- adjoint_start: float32 [3, 8, 1024, 2048], P(None, None, 'gy', 'gx'), may hold values from -6 to 6
Outputs:
- field: float32 [3, 8, 1024, 2048], P(None, None, 'gy', 'gx')
- adjoint: float32 [3, 8, 1024, 2048], P(None, None, 'gy', 'gx')
- gradient: float32 [1024, 2048], P('gy', 'gx')
The draws below stay inside these ranges and needn't reach their ends.
All inputs are finite; a program needn't handle non-finite values.
Results may differ from the reference program's by a relative error of at most 0.00019.
Values sent between devices are 32-bit elements; how exact they have to be, the bound alone decides.
No kernel may reach another device: no remote copies, remote signals or barrier semaphores. Data moves between devices by JAX's collectives and lax.ppermute only.
A program may use at most 32 MiB of HBM per device.

```python
import math
import jax
import jax.numpy as jnp
from jax import lax

Z = 8
ITERS = 4
RADIUS = 8
TILE = 128
MATERIALS = 4
NX = 2048
NY = 1024
TX = 16
TY = 8


def set_ends(values, own_key, low, top_value):
    spot = [jax.random.randint(jax.random.fold_in(own_key, axis), (), 0, length) for axis, length in enumerate(values.shape)]
    longest = values.shape.index(max(values.shape))
    beside = spot[:longest] + [(spot[longest] + 1) % values.shape[longest]] + spot[longest + 1:]
    return values.at[tuple(spot)].set(low).at[tuple(beside)].set(top_value)


def steps_of(stream_key, dims, pieces, low, largest):
    def one(dim, blocks):
        draws = jax.random.uniform(jax.random.fold_in(jax.random.fold_in(stream_key, 6), dim), (blocks,), jnp.float32, low / len(pieces), largest / len(pieces))
        return jnp.repeat(jnp.exp(draws), dims[dim] // blocks).reshape((-1,) + (1,) * (len(dims) - dim - 1))

    loudness = one(*pieces[0])
    for cut in pieces[1:]:
        loudness = loudness * one(*cut)
    return loudness


def centred(key, extent, scale, reach, shards=(), kind=jnp.bfloat16):
    values = jax.random.normal(key, extent, jnp.float32) * scale
    if len(shards) > 0:
        values = steps_of(key, extent, shards, -0.22, 0.18) * values
    return jnp.clip(values, min=-reach, max=reach).astype(kind)


def setup_inputs(seed: int = 0) -> dict:
    streams_of = jax.random.split(jax.random.key(seed), 10)
    background = jnp.clip(jnp.exp(math.log(12.0) - 2.4849066 * jax.random.uniform(streams_of[0], (Z, NY, NX), jnp.float32) ** steps_of(streams_of[0], (Z, NY, NX), ((1, 64), (2, 16)), -0.2, 0.2)), 1.0, 12.0)
    density = jnp.clip(1.0 * jax.random.uniform(streams_of[1], (NY, NX), jnp.float32) ** steps_of(streams_of[1], (NY, NX), ((0, 64), (1, 16)), -0.2, 0.2), 0.0, 1.0)
    design_tiles = set_ends((jax.random.randint(streams_of[2], (TY, TX), 0, 2) < 1).astype(jnp.int32), jax.random.fold_in(streams_of[2], 1), 0, 1)
    material_tiles = set_ends(jax.random.randint(streams_of[3], (TY, TX), 0, MATERIALS), jax.random.fold_in(streams_of[3], 1), 0, MATERIALS - 1).astype(jnp.int32)
    contrast = jnp.clip(jnp.exp(jax.random.uniform(streams_of[4], (MATERIALS,), jnp.float32, math.log(2.0), math.log(10.0))), 2.0, 10.0)
    source = centred(streams_of[5], (3, Z, NY, NX), 3.0, 18.0, ((2, 64), (3, 16)), jnp.float32)
    adjoint_source = centred(streams_of[6], (3, Z, NY, NX), 3.0, 18.0, ((2, 64), (3, 16)), jnp.float32)
    field_start = centred(streams_of[7], (3, Z, NY, NX), 1.0, 6.0, ((2, 64), (3, 16)), jnp.float32)
    adjoint_start = centred(streams_of[8], (3, Z, NY, NX), 1.0, 6.0, ((2, 64), (3, 16)), jnp.float32)
    return {"background": background, "density": density, "design_tiles": design_tiles, "material_tiles": material_tiles, "contrast": contrast, "source": source, "adjoint_source": adjoint_source, "field_start": field_start, "adjoint_start": adjoint_start}


wave_square = 0.5
relaxation = 0.5

def cone_weight(row_shift, col_shift):
    return max(0.0, RADIUS + 1 - math.sqrt(row_shift * row_shift + col_shift * col_shift))

def cone_total():
    total = 0.0
    for row_shift in range(-RADIUS, RADIUS + 1):
        for col_shift in range(-RADIUS, RADIUS + 1):
            total = total + cone_weight(row_shift, col_shift)
    return total

def cone_filter(plane):
    rows, cols = plane.shape
    padded = jnp.pad(plane, RADIUS)
    result = jnp.zeros_like(plane)
    for row_shift in range(-RADIUS, RADIUS + 1):
        for col_shift in range(-RADIUS, RADIUS + 1):
            weight = cone_weight(row_shift, col_shift)
            if weight > 0.0:
                result = result + weight * padded[RADIUS + row_shift:RADIUS + row_shift + rows, RADIUS + col_shift:RADIUS + col_shift + cols]
    return result / cone_total()

def take_span(array, axis, chosen, others):
    index = [slice(None)] * array.ndim
    for other in (-3, -2, -1):
        index[other] = others
    index[axis] = chosen
    return array[tuple(index)]

def forward_diff(array, axis):
    return take_span(array, axis, slice(1, None), slice(None, -1)) - take_span(array, axis, slice(None, -1), slice(None, -1))

def backward_diff(array, axis):
    return take_span(array, axis, slice(1, None), slice(1, None)) - take_span(array, axis, slice(None, -1), slice(1, None))

def curl_curl(padded):
    along_x = padded[..., 0, :, :, :]
    along_y = padded[..., 1, :, :, :]
    along_z = padded[..., 2, :, :, :]
    magnet_x = forward_diff(along_z, -2) - forward_diff(along_y, -3)
    magnet_y = forward_diff(along_x, -3) - forward_diff(along_z, -1)
    magnet_z = forward_diff(along_y, -1) - forward_diff(along_x, -2)
    curl_x = backward_diff(magnet_z, -2) - backward_diff(magnet_y, -3)
    curl_y = backward_diff(magnet_x, -3) - backward_diff(magnet_z, -1)
    curl_z = backward_diff(magnet_y, -1) - backward_diff(magnet_x, -2)
    return jnp.stack([curl_x, curl_y, curl_z], axis=-4)

def relax_sweep(fields, padded, sources, permittivity):
    image = curl_curl(padded) + wave_square * permittivity * fields
    return fields + relaxation * (sources - image) / (4.0 + wave_square * permittivity)

def solve_field(start, sources, permittivity):
    fields = start
    for sweep_number in range(ITERS):
        padded = jnp.pad(fields, [(0, 0), (1, 1), (1, 1), (1, 1)])
        fields = relax_sweep(fields, padded, sources, permittivity)
    return fields

def reference(background, density, design_tiles, material_tiles, contrast, source, adjoint_source, field_start, adjoint_start):
    chosen = (material_tiles[:, :, None] == jnp.arange(MATERIALS, dtype=jnp.int32)[None, None, :]).astype(jnp.float32)
    tile_gain = design_tiles.astype(jnp.float32) * lax.optimization_barrier(jnp.sum(chosen * contrast[None, None, :], axis=2))
    gain = jnp.repeat(jnp.repeat(tile_gain, TILE, axis=0), TILE, axis=1)
    filtered = cone_filter(density)
    permittivity = background + (gain * filtered)[None]
    field = solve_field(field_start, source, permittivity)
    adjoint = solve_field(adjoint_start, adjoint_source, permittivity)
    local = -wave_square * gain * lax.optimization_barrier(jnp.sum(adjoint * field, axis=(0, 1)))
    gradient = cone_filter(local)
    return (field, adjoint, gradient)
```

```python
import functools
import math

import jax
import jax.numpy as jnp
from jax import lax
from jax.experimental import pallas as pl
from jax.experimental.pallas import tpu as pltpu
from jax.sharding import PartitionSpec as P

ITERS = 4
RADIUS = 8
TILE = 128
Z = 8
ROWS = 16
LANES = 128
HALO = 4
WRAP = ROWS + 8
GROUPS = 13
WIDTH = 16
SMEM = pltpu.SMEM
VMEM = pltpu.VMEM
LIMIT = 48 * 1024 * 1024


def cone_weight(row_shift, col_shift):
    return max(0.0, RADIUS + 1 - math.sqrt(row_shift * row_shift + col_shift * col_shift))


def cone_total():
    span = range(-RADIUS, RADIUS + 1)
    return math.fsum(cone_weight(a, b) for a in span for b in span)


def lanes_of(rows):
    return lax.broadcasted_iota(jnp.int32, (rows, LANES), 1)


def rows_of(rows):
    return lax.broadcasted_iota(jnp.int32, (rows, LANES), 0)


def turn(value, shift, axis):
    size = value.shape[axis]
    return pltpu.roll(value, shift % size, axis)


def cone(rows_at, rows):
    total = cone_total()
    paired = [rows_at(0)]
    for a in range(1, RADIUS + 1):
        paired.append(rows_at(a) + rows_at(-a))
    result = None
    for b in range(RADIUS + 1):
        column = None
        for a in range(RADIUS + 1):
            weight = cone_weight(a, b)
            if weight > 0.0:
                term = paired[a] * (weight / total)
                column = term if column is None else column + term
        if b > 0:
            column = turn(column, b, 1) + turn(column, -b, 1)
        result = column if result is None else result + column
    return result


def pack_kernel(field, adjoint, source, adjoint_source, background, density, right, left, up, down):
    lane = lanes_of(ROWS)
    low = rows_of(8) < 4
    for g in range(GROUPS):
        planes = background if g == 12 else (field, adjoint, source, adjoint_source)[g // 3].at[g % 3]
        to_right = to_left = None
        for z in range(Z):
            plane = planes[z]
            here_right = turn(plane, 16 * z + 12, 1)
            here_left = turn(plane, 16 * z + 4, 1)
            if z == 0:
                to_right, to_left = here_right, here_left
            else:
                chosen = lane >= 16 * z
                to_right = jnp.where(chosen, here_right, to_right)
                to_left = jnp.where(chosen, here_left, to_left)
        right[g] = to_right
        left[g] = to_left
        for pair in range(Z // 2):
            k = g * (Z // 2) + pair
            down[k] = jnp.where(low, planes[2 * pair, 0:8], turn(planes[2 * pair + 1, 0:8], 4, 0))
            up[k] = jnp.where(low, turn(planes[2 * pair + 1, 8:16], 4, 0), planes[2 * pair, 8:16])
    right[GROUPS] = density[...]
    left[GROUPS] = density[...]
    for part in range(2):
        up[4 * GROUPS + part] = density[8 * part : 8 * part + 8]
        down[4 * GROUPS + part] = density[8 * part : 8 * part + 8]


def strip_kernel(own_right, own_left, from_left, from_right, strips, side, up, down):
    col = lax.axis_index("gx")
    first, last = col == 0, col == lax.axis_size("gx") - 1
    lane = lanes_of(ROWS)
    within = lane % 16
    half = lane % 32 < 16
    low = rows_of(8) < 4
    for g in range(GROUPS):
        here_right = jnp.where(within >= HALO, jnp.where(last, 0.0, from_right[g]), own_left[g])
        here_left = jnp.where(within < 12, jnp.where(first, 0.0, from_left[g]), own_right[g])
        even = jnp.where(half, here_right, turn(here_left, 16, 1))
        odd = jnp.where(half, turn(here_right, -16, 1), here_left)
        strips[g, 0] = even
        strips[g, 1] = odd
        down[g] = jnp.where(low, even[0:8], turn(odd[0:8], 4, 0))
        up[g] = jnp.where(low, turn(odd[8:16], 4, 0), even[8:16])
    beside = jnp.where(
        lane < 64, jnp.where(last, 0.0, from_right[GROUPS]), jnp.where(first, 0.0, from_left[GROUPS])
    )
    side[...] = beside
    for part in range(2):
        up[GROUPS + part] = beside[8 * part : 8 * part + 8]
        down[GROUPS + part] = beside[8 * part : 8 * part + 8]


def unpack(above, below, low, odd):
    if odd:
        return turn(jnp.where(low, below, above), 4, 0)
    return jnp.where(low, above, below)


def main_kernel(
    design, material, contrast, field, adjoint, source, adjoint_source, background, density,
    above, below, strips, side, strip_above, strip_below,
    field_out, adjoint_out, local_up, local_down,
    fields, drive, rate, keep, strip_fields, strip_drive, strip_rate, strip_keep, wide,
):
    col, row = lax.axis_index("gx"), lax.axis_index("gy")
    cols, rows = lax.axis_size("gx"), lax.axis_size("gy")
    first_row, last_row = row == 0, row == rows - 1
    low = rows_of(8) < 4
    lane8, lane24, row24 = lanes_of(8), lanes_of(WRAP), rows_of(WRAP)
    outside8 = (low & last_row) | (jnp.logical_not(low) & first_row)
    outside = ((row24 >= 16) & (row24 < 20) & last_row) | ((row24 >= 20) & first_row)
    j = lane24 % 32
    outside_strip = outside | ((j >= HALO) & (j < 16) & (col == cols - 1)) | ((j >= 16) & (j < 28) & (col == 0))

    tiles_y, tiles_x = design.shape

    def gain_at(first, tile_x):
        tile_y = jnp.clip(first, 0, tiles_y * TILE - 1) // TILE
        tile_x = jnp.clip(tile_x, 0, tiles_x - 1)
        return design[tile_y, tile_x].astype(jnp.float32) * contrast[material[tile_y, tile_x]]

    def gain_rows(tile_x):
        here = gain_at(row * ROWS, tile_x)
        up = gain_at(row * ROWS + ROWS, tile_x)
        down = gain_at(row * ROWS - HALO, tile_x)
        return here, jnp.where(row24 < 16, here, jnp.where(row24 < 20, up, down))

    here_main, gain_main = gain_rows(col)
    here_right, gain_right = gain_rows(col + 1)
    here_left, gain_left = gain_rows(col - 1)

    wide[0:8, 0:LANES] = jnp.where(first_row, 0.0, below[52])
    wide[8:16, 0:LANES] = jnp.where(first_row, 0.0, below[53])
    wide[0:8, LANES : 2 * LANES] = jnp.where(first_row, 0.0, strip_below[13])
    wide[8:16, LANES : 2 * LANES] = jnp.where(first_row, 0.0, strip_below[14])
    wide[16:32, 0:LANES] = density[...]
    wide[16:32, LANES : 2 * LANES] = side[...]
    wide[32:40, 0:LANES] = jnp.where(last_row, 0.0, above[52])
    wide[40:48, 0:LANES] = jnp.where(last_row, 0.0, above[53])
    wide[32:40, LANES : 2 * LANES] = jnp.where(last_row, 0.0, strip_above[13])
    wide[40:48, LANES : 2 * LANES] = jnp.where(last_row, 0.0, strip_above[14])
    filtered = cone(lambda a: wide[8 + a : 40 + a], 32)
    low2 = lax.broadcasted_iota(jnp.int32, (8, 2 * LANES), 0) < 4
    filtered = jnp.concatenate(
        [filtered[8:24], jnp.where(low2, filtered[24:32], filtered[0:8])], axis=0
    )
    design_main = gain_main * filtered[:, :LANES]
    beside = filtered[:, LANES:]
    block = filtered[:, :LANES]
    right_side = jnp.where(lane24 < HALO, turn(block, HALO, 1), turn(beside, HALO, 1))
    left_side = jnp.where(lane24 < 28, turn(beside, 28, 1), turn(block, 28, 1))
    quarter = jnp.where(lane24 < 16, right_side * gain_right, left_side * gain_left)
    quarter = jnp.where((lane24 < HALO) | (lane24 >= 28), turn_edges(right_side, left_side, lane24) * gain_main, quarter)
    quarter = jnp.where(lane24 < 32, quarter, 0.0)
    quarter = quarter + turn(quarter, 32, 1)
    design_strip = quarter + turn(quarter, 64, 1)

    def whole(inner, halo):
        return jnp.concatenate([inner, halo], axis=0)

    for z in range(Z):
        k = 48 + z // 2
        halo = unpack(above[k], below[k], low, z % 2)
        step = 0.5 / (4.0 + 0.5 * (whole(background[z], halo) + design_main))
        step = jnp.where(outside, 0.0, step)
        rate[z] = step
        keep[z] = 0.5 + 4.0 * step
    for t in range(2):
        halo = unpack(strip_above[12], strip_below[12], low, t)
        step = 0.5 / (4.0 + 0.5 * (whole(strips[12, t], halo) + design_strip))
        step = jnp.where(outside_strip, 0.0, step)
        strip_rate[t] = step
        strip_keep[t] = 0.5 + 4.0 * step

    starts = (field, adjoint)
    sources = (source, adjoint_source)
    for f in range(2):
        for c in range(3):
            g = 3 * f + c
            for z in range(Z):
                k = 4 * g + z // 2
                halo = jnp.where(outside8, 0.0, unpack(above[k], below[k], low, z % 2))
                fields[f, c, z] = whole(starts[f][c, z], halo)
                k = 4 * (6 + g) + z // 2
                halo = unpack(above[k], below[k], low, z % 2)
                drive[f, c, z] = rate[z] * whole(sources[f][c, z], halo)
            for t in range(2):
                halo = jnp.where(outside8, 0.0, unpack(strip_above[g], strip_below[g], low, t))
                strip_fields[f, c, t] = whole(strips[g, t], halo)
                halo = unpack(strip_above[6 + g], strip_below[6 + g], low, t)
                strip_drive[f, c, t] = strip_rate[t] * whole(strips[6 + g, t], halo)

    at_last, at_first = lane24 == LANES - 1, lane24 == 0

    def ahead_y(value):
        return turn(value, -1, 0)

    def behind_y(value):
        return turn(value, 1, 0)

    def sweep(_, carry):
        for f in range(2):
            ex, ey, ez = ([strip_fields[f, c, t] for t in range(2)] for c in range(3))

            def above_z(pair):
                return pair[1], jnp.where(lane24 < 96, turn(pair[0], -32, 1), 0.0)

            ex_z, ey_z = above_z(ex), above_z(ey)
            hx, hy, hz = [], [], []
            for t in range(2):
                hx.append((ahead_y(ez[t]) - ez[t]) - (ey_z[t] - ey[t]))
                hy.append((ex_z[t] - ex[t]) - (turn(ez[t], -1, 1) - ez[t]))
                hz.append((turn(ey[t], -1, 1) - ey[t]) - (ahead_y(ex[t]) - ex[t]))
            bottom = lane24 < 32
            hx_z = (jnp.where(bottom, -ey[0], turn(hx[1], 32, 1)), hx[0])
            hy_z = (jnp.where(bottom, ex[0], turn(hy[1], 32, 1)), hy[0])
            for t in range(2):
                curl_x = (hz[t] - behind_y(hz[t])) - (hy[t] - hy_z[t])
                curl_y = (hx[t] - hx_z[t]) - (hz[t] - turn(hz[t], 1, 1))
                curl_z = (hy[t] - turn(hy[t], 1, 1)) - (hx[t] - behind_y(hx[t]))
                step, kept = strip_rate[t], strip_keep[t]
                strip_fields[f, 0, t] = kept * ex[t] + strip_drive[f, 0, t] - step * curl_x
                strip_fields[f, 1, t] = kept * ey[t] + strip_drive[f, 1, t] - step * curl_y
                strip_fields[f, 2, t] = kept * ez[t] + strip_drive[f, 2, t] - step * curl_z

            def ahead_x(value, strip, z):
                return jnp.where(at_last, turn(strip[z % 2], 123 - 32 * (z // 2), 1), turn(value, -1, 1))

            def behind_x(value, strip, z):
                return jnp.where(at_first, turn(strip[z % 2], -(32 * (z // 2) + 27), 1), turn(value, 1, 1))

            mx, my, mz = fields[f, 0, 0], fields[f, 1, 0], fields[f, 2, 0]
            gx_before, gy_before = -my, mx
            for z in range(Z):
                if z < Z - 1:
                    nx, ny, nz = fields[f, 0, z + 1], fields[f, 1, z + 1], fields[f, 2, z + 1]
                else:
                    nx = ny = nz = jnp.zeros_like(mx)
                gx = (ahead_y(mz) - mz) - (ny - my)
                gy = (nx - mx) - (ahead_x(mz, ez, z) - mz)
                gz = (ahead_x(my, ey, z) - my) - (ahead_y(mx) - mx)
                curl_x = (gz - behind_y(gz)) - (gy - gy_before)
                curl_y = (gx - gx_before) - (gz - behind_x(gz, hz, z))
                curl_z = (gy - behind_x(gy, hy, z)) - (gx - behind_y(gx))
                step, kept = rate[z], keep[z]
                fields[f, 0, z] = kept * mx + drive[f, 0, z] - step * curl_x
                fields[f, 1, z] = kept * my + drive[f, 1, z] - step * curl_y
                fields[f, 2, z] = kept * mz + drive[f, 2, z] - step * curl_z
                gx_before, gy_before = gx, gy
                mx, my, mz = nx, ny, nz
        return carry

    lax.fori_loop(0, ITERS, sweep, 0)

    product = jnp.zeros((ROWS, LANES), jnp.float32)
    strip_product = jnp.zeros((ROWS, LANES), jnp.float32)
    for c in range(3):
        for z in range(Z):
            forward, backward = fields[0, c, z, 0:ROWS], fields[1, c, z, 0:ROWS]
            field_out[c, z] = forward
            adjoint_out[c, z] = backward
            product = product + forward * backward
        for t in range(2):
            strip_product = strip_product + strip_fields[0, c, t, 0:ROWS] * strip_fields[1, c, t, 0:ROWS]
    strip_product = strip_product + turn(strip_product, 64, 1)
    strip_product = strip_product + turn(strip_product, 32, 1)
    local = product * (-0.5 * here_main)
    lane = lanes_of(ROWS)
    local_side = jnp.where(
        lane < 64, turn(strip_product, -4, 1) * (-0.5 * here_right), turn(strip_product, 100, 1) * (-0.5 * here_left)
    )
    local_down[:, 0:LANES] = local[0:8]
    local_down[:, LANES : 2 * LANES] = local_side[0:8]
    local_up[:, 0:LANES] = local[8:16]
    local_up[:, LANES : 2 * LANES] = local_side[8:16]


def turn_edges(right_side, left_side, lane):
    return jnp.where(lane < 16, right_side, left_side)


def gradient_kernel(own_up, own_down, above, below, gradient, wide):
    row = lax.axis_index("gy")
    wide[0:8] = jnp.where(row == 0, 0.0, below[...])
    wide[8:16] = own_down[...]
    wide[16:24] = own_up[...]
    wide[24:32] = jnp.where(row == lax.axis_size("gy") - 1, 0.0, above[...])
    gradient[...] = cone(lambda a: wide[8 + a : 24 + a], ROWS)[:, :LANES]


def ring(axis, step):
    size = lax.axis_size(axis)
    return [(i, (i + step) % size) for i in range(size)]


def shape(*dims):
    return jax.ShapeDtypeStruct(dims, jnp.float32)


def call(kernel, outs, smem=0, scratch=()):
    def run(*operands):
        spaces = [SMEM] * smem + [VMEM] * (len(operands) - smem)
        return pl.pallas_call(
            kernel,
            out_shape=outs,
            in_specs=[pl.BlockSpec(memory_space=space) for space in spaces],
            out_specs=jax.tree.map(lambda _: pl.BlockSpec(memory_space=VMEM), outs),
            scratch_shapes=[pltpu.VMEM(dims, jnp.float32) for dims in scratch],
            compiler_params=pltpu.CompilerParams(vmem_limit_bytes=LIMIT),
        )(*operands)

    return run


def on_device(background, density, design_tiles, material_tiles, contrast, source, adjoint_source, field_start, adjoint_start):
    packed = 4 * GROUPS + 2
    right, left, up, down = call(
        pack_kernel,
        [shape(GROUPS + 1, ROWS, LANES), shape(GROUPS + 1, ROWS, LANES), shape(packed, 8, LANES), shape(packed, 8, LANES)],
    )(field_start, adjoint_start, source, adjoint_source, background, density)
    from_left = lax.ppermute(right, "gx", ring("gx", 1))
    from_right = lax.ppermute(left, "gx", ring("gx", -1))
    below = lax.ppermute(up, "gy", ring("gy", 1))
    above = lax.ppermute(down, "gy", ring("gy", -1))
    strips, side, strip_up, strip_down = call(
        strip_kernel,
        [shape(GROUPS, 2, ROWS, LANES), shape(ROWS, LANES), shape(GROUPS + 2, 8, LANES), shape(GROUPS + 2, 8, LANES)],
    )(right, left, from_left, from_right)
    strip_below = lax.ppermute(strip_up, "gy", ring("gy", 1))
    strip_above = lax.ppermute(strip_down, "gy", ring("gy", -1))
    block = shape(3, Z, ROWS, LANES)
    field, adjoint, local_up, local_down = call(
        main_kernel,
        [block, block, shape(8, 2 * LANES), shape(8, 2 * LANES)],
        smem=3,
        scratch=(
            (2, 3, Z, WRAP, LANES),
            (2, 3, Z, WRAP, LANES),
            (Z, WRAP, LANES),
            (Z, WRAP, LANES),
            (2, 3, 2, WRAP, LANES),
            (2, 3, 2, WRAP, LANES),
            (2, WRAP, LANES),
            (2, WRAP, LANES),
            (48, 2 * LANES),
        ),
    )(
        design_tiles, material_tiles, contrast, field_start, adjoint_start, source, adjoint_source, background, density,
        above, below, strips, side, strip_above, strip_below,
    )
    local_below = lax.ppermute(local_up, "gy", ring("gy", 1))
    local_above = lax.ppermute(local_down, "gy", ring("gy", -1))
    gradient = call(gradient_kernel, shape(ROWS, LANES), scratch=((32, 2 * LANES),))(
        local_up, local_down, local_above, local_below
    )
    return (field, adjoint, gradient)


def solution(mesh):
    in_specs = (
        P(None, "gy", "gx"),
        P("gy", "gx"),
        P(),
        P(),
        P(),
        P(None, None, "gy", "gx"),
        P(None, None, "gy", "gx"),
        P(None, None, "gy", "gx"),
        P(None, None, "gy", "gx"),
    )
    out_specs = (P(None, None, "gy", "gx"), P(None, None, "gy", "gx"), P("gy", "gx"))
    return jax.shard_map(on_device, mesh=mesh, in_specs=in_specs, out_specs=out_specs, check_vma=False)
```

```python
import functools
import math

import jax
import jax.numpy as jnp
from jax import lax
from jax.experimental import pallas as pl
from jax.experimental.pallas import tpu as pltpu
from jax.sharding import PartitionSpec as P

ITERS = 4
RADIUS = 8
TILE = 128
Z = 8
ROWS = 16
LANES = 128
HALO = 4
WRAP = ROWS + 8
GROUPS = 13
VMEM = pltpu.VMEM
LIMIT = 48 * 1024 * 1024


def cone_weight(row_shift, col_shift):
    return max(0.0, RADIUS + 1 - math.sqrt(row_shift * row_shift + col_shift * col_shift))


def cone_total():
    span = range(-RADIUS, RADIUS + 1)
    return math.fsum(cone_weight(a, b) for a in span for b in span)


def lanes_of(rows):
    return lax.broadcasted_iota(jnp.int32, (rows, LANES), 1)


def rows_of(rows):
    return lax.broadcasted_iota(jnp.int32, (rows, LANES), 0)


def turn(value, shift, axis):
    size = value.shape[axis]
    return pltpu.roll(value, shift % size, axis)


def cone(rows_at, rows):
    total = cone_total()
    paired = [rows_at(0)]
    for a in range(1, RADIUS + 1):
        paired.append(rows_at(a) + rows_at(-a))
    result = None
    for b in range(RADIUS + 1):
        column = None
        for a in range(RADIUS + 1):
            weight = cone_weight(a, b)
            if weight > 0.0:
                term = paired[a] * (weight / total)
                column = term if column is None else column + term
        if b > 0:
            column = turn(column, b, 1) + turn(column, -b, 1)
        result = column if result is None else result + column
    return result


def edge_kernel(
    design_in, material_in, contrast_in, field_in, adjoint_in, source_in, adjoint_source_in, background_in, density_in,
    right, left, gains,
    design, material, contrast, field, adjoint, source, adjoint_source, background, density, done,
):
    arrays = (
        (field_in, field), (adjoint_in, adjoint), (source_in, source), (adjoint_source_in, adjoint_source),
        (background_in, background), (density_in, density),
        (design_in, design), (material_in, material), (contrast_in, contrast),
    )
    copies = [pltpu.make_async_copy(here, there, done.at[i]) for i, (here, there) in enumerate(arrays)]
    for copy in copies:
        copy.start()
    lane = lanes_of(ROWS)
    for g in range(GROUPS):
        if g % 3 == 0:
            copies[g // 3].wait()
        planes = background if g == 12 else (field, adjoint, source, adjoint_source)[g // 3].at[g % 3]
        to_right = to_left = None
        for z in range(Z):
            plane = planes[z]
            here_right = turn(plane, 16 * z + 12, 1)
            here_left = turn(plane, 16 * z + 4, 1)
            if z == 0:
                to_right, to_left = here_right, here_left
            else:
                chosen = lane >= 16 * z
                to_right = jnp.where(chosen, here_right, to_right)
                to_left = jnp.where(chosen, here_left, to_left)
        right[g] = to_right
        left[g] = to_left
    for copy in copies[5:]:
        copy.wait()
    right[GROUPS] = density[...]
    left[GROUPS] = density[...]

    col, row = lax.axis_index("gx"), lax.axis_index("gy")
    row24 = rows_of(WRAP)
    tiles_y, tiles_x = design.shape

    def gain_at(first, tile_x):
        tile_y = jnp.clip(first, 0, tiles_y * TILE - 1) // TILE
        tile_x = jnp.clip(tile_x, 0, tiles_x - 1)
        return design[tile_y, tile_x].astype(jnp.float32) * contrast[material[tile_y, tile_x]]

    for k in range(3):
        tile_x = col + (0, 1, -1)[k]
        here = gain_at(row * ROWS, tile_x)
        up = gain_at(row * ROWS + ROWS, tile_x)
        down = gain_at(row * ROWS - HALO, tile_x)
        gains[k] = jnp.where(row24 < 16, here, jnp.where(row24 < 20, up, down))


def rows_kernel(field, adjoint, source, adjoint_source, background, density, sent, up, down):
    low = rows_of(8) < 4
    for g in range(GROUPS):
        planes = background if g == 12 else (field, adjoint, source, adjoint_source)[g // 3].at[g % 3]
        for pair in range(Z // 2):
            k = g * (Z // 2) + pair
            down[k] = jnp.where(low, planes[2 * pair, 0:8], turn(planes[2 * pair + 1, 0:8], 4, 0))
            up[k] = jnp.where(low, turn(planes[2 * pair + 1, 8:16], 4, 0), planes[2 * pair, 8:16])
    for part in range(2):
        up[4 * GROUPS + part] = density[8 * part : 8 * part + 8]
        down[4 * GROUPS + part] = density[8 * part : 8 * part + 8]


def strip_kernel(own_right, own_left, from_left, from_right, strips, side, up, down):
    col = lax.axis_index("gx")
    first, last = col == 0, col == lax.axis_size("gx") - 1
    lane = lanes_of(ROWS)
    within = lane % 16
    half = lane % 32 < 16
    low = rows_of(8) < 4
    for g in range(GROUPS):
        here_right = jnp.where(within >= HALO, jnp.where(last, 0.0, from_right[g]), own_left[g])
        here_left = jnp.where(within < 12, jnp.where(first, 0.0, from_left[g]), own_right[g])
        even = jnp.where(half, here_right, turn(here_left, 16, 1))
        odd = jnp.where(half, turn(here_right, -16, 1), here_left)
        strips[g, 0] = even
        strips[g, 1] = odd
        down[g] = jnp.where(low, even[0:8], turn(odd[0:8], 4, 0))
        up[g] = jnp.where(low, turn(odd[8:16], 4, 0), even[8:16])
    beside = jnp.where(
        lane < 64, jnp.where(last, 0.0, from_right[GROUPS]), jnp.where(first, 0.0, from_left[GROUPS])
    )
    side[...] = beside
    for part in range(2):
        up[GROUPS + part] = beside[8 * part : 8 * part + 8]
        down[GROUPS + part] = beside[8 * part : 8 * part + 8]


def unpack(above, below, low, odd):
    if odd:
        return turn(jnp.where(low, below, above), 4, 0)
    return jnp.where(low, above, below)


def main_kernel(
    gains, field, adjoint, source, adjoint_source, background, density,
    above, below, strips, side, strip_above, strip_below,
    field_out, adjoint_out, local_up, local_down,
    fields, sources, curls, rate, keep, strip_fields, strip_sources, strip_curls, strip_rate, strip_keep, wide,
):
    col, row = lax.axis_index("gx"), lax.axis_index("gy")
    cols, rows = lax.axis_size("gx"), lax.axis_size("gy")
    first_row, last_row = row == 0, row == rows - 1
    low = rows_of(8) < 4
    lane24, row24 = lanes_of(WRAP), rows_of(WRAP)
    outside8 = (low & last_row) | (jnp.logical_not(low) & first_row)
    outside = ((row24 >= 16) & (row24 < 20) & last_row) | ((row24 >= 20) & first_row)
    j = lane24 % 32
    outside_strip = outside | ((j >= HALO) & (j < 16) & (col == cols - 1)) | ((j >= 16) & (j < 28) & (col == 0))
    gain_main, gain_right, gain_left = gains[0], gains[1], gains[2]

    wide[0:8, 0:LANES] = jnp.where(first_row, 0.0, below[52])
    wide[8:16, 0:LANES] = jnp.where(first_row, 0.0, below[53])
    wide[0:8, LANES : 2 * LANES] = jnp.where(first_row, 0.0, strip_below[13])
    wide[8:16, LANES : 2 * LANES] = jnp.where(first_row, 0.0, strip_below[14])
    wide[16:32, 0:LANES] = density[...]
    wide[16:32, LANES : 2 * LANES] = side[...]
    wide[32:40, 0:LANES] = jnp.where(last_row, 0.0, above[52])
    wide[40:48, 0:LANES] = jnp.where(last_row, 0.0, above[53])
    wide[32:40, LANES : 2 * LANES] = jnp.where(last_row, 0.0, strip_above[13])
    wide[40:48, LANES : 2 * LANES] = jnp.where(last_row, 0.0, strip_above[14])
    filtered = cone(lambda a: wide[8 + a : 40 + a], 32)
    low2 = lax.broadcasted_iota(jnp.int32, (8, 2 * LANES), 0) < 4
    filtered = jnp.concatenate(
        [filtered[8:24], jnp.where(low2, filtered[24:32], filtered[0:8])], axis=0
    )
    design_main = gain_main * filtered[:, :LANES]
    beside = filtered[:, LANES:]
    block = filtered[:, :LANES]
    right_side = jnp.where(lane24 < HALO, turn(block, HALO, 1), turn(beside, HALO, 1))
    left_side = jnp.where(lane24 < 28, turn(beside, 28, 1), turn(block, 28, 1))
    quarter = jnp.where(lane24 < 16, right_side * gain_right, left_side * gain_left)
    quarter = jnp.where((lane24 < HALO) | (lane24 >= 28), turn_edges(right_side, left_side, lane24) * gain_main, quarter)
    quarter = jnp.where(lane24 < 32, quarter, 0.0)
    quarter = quarter + turn(quarter, 32, 1)
    design_strip = quarter + turn(quarter, 64, 1)

    def whole(inner, halo):
        return jnp.concatenate([inner, halo], axis=0)

    for z in range(Z):
        k = 48 + z // 2
        halo = unpack(above[k], below[k], low, z % 2)
        step = 0.5 / (4.0 + 0.5 * (whole(background[z], halo) + design_main))
        step = jnp.where(outside, 0.0, step)
        rate[z] = step
        keep[z] = 0.5 + 4.0 * step
    for t in range(2):
        halo = unpack(strip_above[12], strip_below[12], low, t)
        step = 0.5 / (4.0 + 0.5 * (whole(strips[12, t], halo) + design_strip))
        step = jnp.where(outside_strip, 0.0, step)
        strip_rate[t] = step
        strip_keep[t] = 0.5 + 4.0 * step

    starts = (field, adjoint, source, adjoint_source)
    for f in range(4):
        for c in range(3):
            g = 3 * f + c
            for z in range(Z):
                k = 4 * g + z // 2
                halo = unpack(above[k], below[k], low, z % 2)
                if f < 2:
                    fields[f, c, z] = whole(starts[f][c, z], jnp.where(outside8, 0.0, halo))
                else:
                    sources[f - 2, c, z] = whole(starts[f][c, z], halo)
            for t in range(2):
                halo = unpack(strip_above[g], strip_below[g], low, t)
                if f < 2:
                    strip_fields[f, c, t] = whole(strips[g, t], jnp.where(outside8, 0.0, halo))
                else:
                    strip_sources[f - 2, c, t] = whole(strips[g, t], halo)

    at_last, at_first = lane24 == LANES - 1, lane24 == 0

    def ahead_y(value):
        return turn(value, -1, 0)

    def behind_y(value):
        return turn(value, 1, 0)

    def ahead_x(value, strip, z):
        return jnp.where(at_last, turn(strip[z % 2], 123 - 32 * (z // 2), 1), turn(value, -1, 1))

    def behind_x(value, strip, z):
        return jnp.where(at_first, turn(strip[z % 2], -(32 * (z // 2) + 27), 1), turn(value, 1, 1))

    def sweep(_, carry):
        for f in range(2):
            ex, ey, ez = ([strip_fields[f, c, t] for t in range(2)] for c in range(3))
            for t in range(2):
                if t == 0:
                    ex_z, ey_z = ex[1], ey[1]
                else:
                    ex_z = jnp.where(lane24 < 96, turn(ex[0], -32, 1), 0.0)
                    ey_z = jnp.where(lane24 < 96, turn(ey[0], -32, 1), 0.0)
                strip_curls[f, 0, t] = (ahead_y(ez[t]) - ez[t]) - (ey_z - ey[t])
                strip_curls[f, 1, t] = (ex_z - ex[t]) - (turn(ez[t], -1, 1) - ez[t])
                strip_curls[f, 2, t] = (turn(ey[t], -1, 1) - ey[t]) - (ahead_y(ex[t]) - ex[t])
            for z in range(Z):
                ex, ey, ez = (fields[f, c, z] for c in range(3))
                if z < Z - 1:
                    ex_z, ey_z = fields[f, 0, z + 1], fields[f, 1, z + 1]
                else:
                    ex_z = ey_z = jnp.zeros_like(ex)
                curls[f, 0, z] = (ahead_y(ez) - ez) - (ey_z - ey)
                curls[f, 1, z] = (ex_z - ex) - (ahead_x(ez, strip_fields.at[f, 2], z) - ez)
                curls[f, 2, z] = (ahead_x(ey, strip_fields.at[f, 1], z) - ey) - (ahead_y(ex) - ex)
        bottom = lane24 < 32
        for f in range(2):
            for t in range(2):
                ex, ey, ez = (strip_fields[f, c, t] for c in range(3))
                hx, hy, hz = (strip_curls[f, c, t] for c in range(3))
                if t == 1:
                    hx_z, hy_z = strip_curls[f, 0, 0], strip_curls[f, 1, 0]
                else:
                    hx_z = jnp.where(bottom, -ey, turn(strip_curls[f, 0, 1], 32, 1))
                    hy_z = jnp.where(bottom, ex, turn(strip_curls[f, 1, 1], 32, 1))
                curl_x = (hz - behind_y(hz)) - (hy - hy_z)
                curl_y = (hx - hx_z) - (hz - turn(hz, 1, 1))
                curl_z = (hy - turn(hy, 1, 1)) - (hx - behind_y(hx))
                step, kept = strip_rate[t], strip_keep[t]
                strip_fields[f, 0, t] = kept * ex + step * (strip_sources[f, 0, t] - curl_x)
                strip_fields[f, 1, t] = kept * ey + step * (strip_sources[f, 1, t] - curl_y)
                strip_fields[f, 2, t] = kept * ez + step * (strip_sources[f, 2, t] - curl_z)
            for z in range(Z):
                ex, ey, ez = (fields[f, c, z] for c in range(3))
                hx, hy, hz = (curls[f, c, z] for c in range(3))
                if z > 0:
                    hx_z, hy_z = curls[f, 0, z - 1], curls[f, 1, z - 1]
                else:
                    hx_z, hy_z = -ey, ex
                curl_x = (hz - behind_y(hz)) - (hy - hy_z)
                curl_y = (hx - hx_z) - (hz - behind_x(hz, strip_curls.at[f, 2], z))
                curl_z = (hy - behind_x(hy, strip_curls.at[f, 1], z)) - (hx - behind_y(hx))
                step, kept = rate[z], keep[z]
                fields[f, 0, z] = kept * ex + step * (sources[f, 0, z] - curl_x)
                fields[f, 1, z] = kept * ey + step * (sources[f, 1, z] - curl_y)
                fields[f, 2, z] = kept * ez + step * (sources[f, 2, z] - curl_z)
        return carry

    lax.fori_loop(0, ITERS, sweep, 0)

    product = jnp.zeros((ROWS, LANES), jnp.float32)
    strip_product = jnp.zeros((ROWS, LANES), jnp.float32)
    for c in range(3):
        for z in range(Z):
            forward, backward = fields[0, c, z, 0:ROWS], fields[1, c, z, 0:ROWS]
            field_out[c, z] = forward
            adjoint_out[c, z] = backward
            product = product + forward * backward
        for t in range(2):
            strip_product = strip_product + strip_fields[0, c, t, 0:ROWS] * strip_fields[1, c, t, 0:ROWS]
    strip_product = strip_product + turn(strip_product, 64, 1)
    strip_product = strip_product + turn(strip_product, 32, 1)
    local = product * (-0.5 * gain_main[0:ROWS])
    lane = lanes_of(ROWS)
    local_side = jnp.where(
        lane < 64, turn(strip_product, -4, 1) * (-0.5 * gain_right[0:ROWS]),
        turn(strip_product, 100, 1) * (-0.5 * gain_left[0:ROWS]),
    )
    local_down[:, 0:LANES] = local[0:8]
    local_down[:, LANES : 2 * LANES] = local_side[0:8]
    local_up[:, 0:LANES] = local[8:16]
    local_up[:, LANES : 2 * LANES] = local_side[8:16]


def turn_edges(right_side, left_side, lane):
    return jnp.where(lane < 16, right_side, left_side)


def gradient_kernel(own_up, own_down, above, below, gradient, wide):
    row = lax.axis_index("gy")
    wide[0:8] = jnp.where(row == 0, 0.0, below[...])
    wide[8:16] = own_down[...]
    wide[16:24] = own_up[...]
    wide[24:32] = jnp.where(row == lax.axis_size("gy") - 1, 0.0, above[...])
    gradient[...] = cone(lambda a: wide[8 + a : 24 + a], ROWS)[:, :LANES]


def ring(axis, step):
    size = lax.axis_size(axis)
    return [(i, (i + step) % size) for i in range(size)]


def shape(*dims):
    return jax.ShapeDtypeStruct(dims, jnp.float32)


def call(kernel, outs, space=VMEM, scratch=()):
    def run(*operands):
        return pl.pallas_call(
            kernel,
            out_shape=outs,
            in_specs=[pl.BlockSpec(memory_space=space)] * len(operands),
            out_specs=jax.tree.map(lambda _: pl.BlockSpec(memory_space=VMEM), outs),
            scratch_shapes=scratch,
            compiler_params=pltpu.CompilerParams(vmem_limit_bytes=LIMIT),
        )(*operands)

    return run


def room(*dims):
    return pltpu.VMEM(dims, jnp.float32)


def on_device(background, density, design_tiles, material_tiles, contrast, source, adjoint_source, field_start, adjoint_start):
    inner = (field_start, adjoint_start, source, adjoint_source, background, density)
    tiles = (design_tiles, material_tiles, contrast)
    edges = shape(GROUPS + 1, ROWS, LANES)
    right, left, gains = call(
        edge_kernel,
        [edges, edges, shape(3, WRAP, LANES)],
        space=pl.ANY,
        scratch=[pltpu.SMEM(a.shape, a.dtype) for a in tiles]
        + [room(*a.shape) for a in inner]
        + [pltpu.SemaphoreType.DMA((9,))],
    )(*tiles, *inner)
    from_left = lax.ppermute(right, "gx", ring("gx", 1))
    from_right = lax.ppermute(left, "gx", ring("gx", -1))
    rows = shape(4 * GROUPS + 2, 8, LANES)
    up, down = call(rows_kernel, [rows, rows])(*inner, from_left)
    below = lax.ppermute(up, "gy", ring("gy", 1))
    above = lax.ppermute(down, "gy", ring("gy", -1))
    corner = shape(GROUPS + 2, 8, LANES)
    strips, side, strip_up, strip_down = call(
        strip_kernel, [shape(GROUPS, 2, ROWS, LANES), shape(ROWS, LANES), corner, corner]
    )(right, left, from_left, from_right)
    strip_below = lax.ppermute(strip_up, "gy", ring("gy", 1))
    strip_above = lax.ppermute(strip_down, "gy", ring("gy", -1))
    block, part = shape(3, Z, ROWS, LANES), shape(8, 2 * LANES)
    planes, sheets = (2, 3, Z, WRAP, LANES), (2, 3, 2, WRAP, LANES)
    field, adjoint, local_up, local_down = call(
        main_kernel,
        [block, block, part, part],
        scratch=[
            room(*planes), room(*planes), room(*planes), room(Z, WRAP, LANES), room(Z, WRAP, LANES),
            room(*sheets), room(*sheets), room(*sheets), room(2, WRAP, LANES), room(2, WRAP, LANES),
            room(48, 2 * LANES),
        ],
    )(gains, *inner, above, below, strips, side, strip_above, strip_below)
    local_below = lax.ppermute(local_up, "gy", ring("gy", 1))
    local_above = lax.ppermute(local_down, "gy", ring("gy", -1))
    gradient = call(gradient_kernel, shape(ROWS, LANES), scratch=[room(32, 2 * LANES)])(
        local_up, local_down, local_above, local_below
    )
    return (field, adjoint, gradient)


def solution(mesh):
    in_specs = (
        P(None, "gy", "gx"),
        P("gy", "gx"),
        P(),
        P(),
        P(),
        P(None, None, "gy", "gx"),
        P(None, None, "gy", "gx"),
        P(None, None, "gy", "gx"),
        P(None, None, "gy", "gx"),
    )
    out_specs = (P(None, None, "gy", "gx"), P(None, None, "gy", "gx"), P("gy", "gx"))
    return jax.shard_map(on_device, mesh=mesh, in_specs=in_specs, out_specs=out_specs, check_vma=False)
```

```python
import functools
import math

import jax
import jax.numpy as jnp
from jax import lax
from jax.experimental import pallas as pl
from jax.experimental.pallas import tpu as pltpu
from jax.sharding import PartitionSpec as P

ITERS = 4
RADIUS = 8
TILE = 128
Z = 8
ROWS = 16
LANES = 128
HALO = 4
WRAP = ROWS + 8
GROUPS = 13
VMEM = pltpu.VMEM
LIMIT = 48 * 1024 * 1024


def cone_weight(row_shift, col_shift):
    return max(0.0, RADIUS + 1 - math.sqrt(row_shift * row_shift + col_shift * col_shift))


def cone_total():
    span = range(-RADIUS, RADIUS + 1)
    return math.fsum(cone_weight(a, b) for a in span for b in span)


def lanes_of(rows):
    return lax.broadcasted_iota(jnp.int32, (rows, LANES), 1)


def rows_of(rows):
    return lax.broadcasted_iota(jnp.int32, (rows, LANES), 0)


def turn(value, shift, axis):
    size = value.shape[axis]
    return pltpu.roll(value, shift % size, axis)


def cone(rows_at, rows):
    total = cone_total()
    paired = [rows_at(0)]
    for a in range(1, RADIUS + 1):
        paired.append(rows_at(a) + rows_at(-a))
    result = None
    for b in range(RADIUS + 1):
        column = None
        for a in range(RADIUS + 1):
            weight = cone_weight(a, b)
            if weight > 0.0:
                term = paired[a] * (weight / total)
                column = term if column is None else column + term
        if b > 0:
            column = turn(column, b, 1) + turn(column, -b, 1)
        result = column if result is None else result + column
    return result


def pack_kernel(
    design_in, material_in, contrast_in, field_in, adjoint_in, source_in, adjoint_source_in, background_in, density_in,
    right, left, up, down, gains, field, adjoint, source, adjoint_source, background, density,
    design, material, contrast, done,
):
    arrays = (
        (field_in, field), (adjoint_in, adjoint), (source_in, source), (adjoint_source_in, adjoint_source),
        (background_in, background), (density_in, density),
        (design_in, design), (material_in, material), (contrast_in, contrast),
    )
    copies = [pltpu.make_async_copy(here, there, done.at[i]) for i, (here, there) in enumerate(arrays)]
    for copy in copies:
        copy.start()
    lane = lanes_of(ROWS)
    low = rows_of(8) < 4
    for g in range(GROUPS):
        if g % 3 == 0:
            copies[g // 3].wait()
        planes = background if g == 12 else (field, adjoint, source, adjoint_source)[g // 3].at[g % 3]
        to_right = to_left = None
        for z in range(Z):
            plane = planes[z]
            here_right = turn(plane, 16 * z + 12, 1)
            here_left = turn(plane, 16 * z + 4, 1)
            if z == 0:
                to_right, to_left = here_right, here_left
            else:
                chosen = lane >= 16 * z
                to_right = jnp.where(chosen, here_right, to_right)
                to_left = jnp.where(chosen, here_left, to_left)
        right[g] = to_right
        left[g] = to_left
        for pair in range(Z // 2):
            k = g * (Z // 2) + pair
            down[k] = jnp.where(low, planes[2 * pair, 0:8], turn(planes[2 * pair + 1, 0:8], 4, 0))
            up[k] = jnp.where(low, turn(planes[2 * pair + 1, 8:16], 4, 0), planes[2 * pair, 8:16])
    for copy in copies[5:]:
        copy.wait()
    right[GROUPS] = density[...]
    left[GROUPS] = density[...]
    for part in range(2):
        up[4 * GROUPS + part] = density[8 * part : 8 * part + 8]
        down[4 * GROUPS + part] = density[8 * part : 8 * part + 8]

    col, row = lax.axis_index("gx"), lax.axis_index("gy")
    row24 = rows_of(WRAP)
    tiles_y, tiles_x = design.shape

    def gain_at(first, tile_x):
        tile_y = jnp.clip(first, 0, tiles_y * TILE - 1) // TILE
        tile_x = jnp.clip(tile_x, 0, tiles_x - 1)
        return design[tile_y, tile_x].astype(jnp.float32) * contrast[material[tile_y, tile_x]]

    for k in range(3):
        tile_x = col + (0, 1, -1)[k]
        here = gain_at(row * ROWS, tile_x)
        up = gain_at(row * ROWS + ROWS, tile_x)
        down = gain_at(row * ROWS - HALO, tile_x)
        gains[k] = jnp.where(row24 < 16, here, jnp.where(row24 < 20, up, down))


def strip_kernel(own_right, own_left, from_left, from_right, strips, side, up, down):
    col = lax.axis_index("gx")
    first, last = col == 0, col == lax.axis_size("gx") - 1
    lane = lanes_of(ROWS)
    within = lane % 16
    half = lane % 32 < 16
    low = rows_of(8) < 4
    for g in range(GROUPS):
        here_right = jnp.where(within >= HALO, jnp.where(last, 0.0, from_right[g]), own_left[g])
        here_left = jnp.where(within < 12, jnp.where(first, 0.0, from_left[g]), own_right[g])
        even = jnp.where(half, here_right, turn(here_left, 16, 1))
        odd = jnp.where(half, turn(here_right, -16, 1), here_left)
        strips[g, 0] = even
        strips[g, 1] = odd
        down[g] = jnp.where(low, even[0:8], turn(odd[0:8], 4, 0))
        up[g] = jnp.where(low, turn(odd[8:16], 4, 0), even[8:16])
    beside = jnp.where(
        lane < 64, jnp.where(last, 0.0, from_right[GROUPS]), jnp.where(first, 0.0, from_left[GROUPS])
    )
    side[...] = beside
    for part in range(2):
        up[GROUPS + part] = beside[8 * part : 8 * part + 8]
        down[GROUPS + part] = beside[8 * part : 8 * part + 8]


def unpack(above, below, low, odd):
    if odd:
        return turn(jnp.where(low, below, above), 4, 0)
    return jnp.where(low, above, below)


def main_kernel(
    gains, field, adjoint, source, adjoint_source, background, density,
    above, below, strips, side, strip_above, strip_below,
    field_out, adjoint_out, local_up, local_down,
    fields, sources, curls, rate, keep, strip_fields, strip_sources, strip_curls, strip_rate, strip_keep, wide,
):
    col, row = lax.axis_index("gx"), lax.axis_index("gy")
    cols, rows = lax.axis_size("gx"), lax.axis_size("gy")
    first_row, last_row = row == 0, row == rows - 1
    low = rows_of(8) < 4
    lane24, row24 = lanes_of(WRAP), rows_of(WRAP)
    outside8 = (low & last_row) | (jnp.logical_not(low) & first_row)
    outside = ((row24 >= 16) & (row24 < 20) & last_row) | ((row24 >= 20) & first_row)
    j = lane24 % 32
    outside_strip = outside | ((j >= HALO) & (j < 16) & (col == cols - 1)) | ((j >= 16) & (j < 28) & (col == 0))
    gain_main, gain_right, gain_left = gains[0], gains[1], gains[2]

    wide[0:8, 0:LANES] = jnp.where(first_row, 0.0, below[52])
    wide[8:16, 0:LANES] = jnp.where(first_row, 0.0, below[53])
    wide[0:8, LANES : 2 * LANES] = jnp.where(first_row, 0.0, strip_below[13])
    wide[8:16, LANES : 2 * LANES] = jnp.where(first_row, 0.0, strip_below[14])
    wide[16:32, 0:LANES] = density[...]
    wide[16:32, LANES : 2 * LANES] = side[...]
    wide[32:40, 0:LANES] = jnp.where(last_row, 0.0, above[52])
    wide[40:48, 0:LANES] = jnp.where(last_row, 0.0, above[53])
    wide[32:40, LANES : 2 * LANES] = jnp.where(last_row, 0.0, strip_above[13])
    wide[40:48, LANES : 2 * LANES] = jnp.where(last_row, 0.0, strip_above[14])
    filtered = cone(lambda a: wide[8 + a : 40 + a], 32)
    low2 = lax.broadcasted_iota(jnp.int32, (8, 2 * LANES), 0) < 4
    filtered = jnp.concatenate(
        [filtered[8:24], jnp.where(low2, filtered[24:32], filtered[0:8])], axis=0
    )
    design_main = gain_main * filtered[:, :LANES]
    beside = filtered[:, LANES:]
    block = filtered[:, :LANES]
    right_side = jnp.where(lane24 < HALO, turn(block, HALO, 1), turn(beside, HALO, 1))
    left_side = jnp.where(lane24 < 28, turn(beside, 28, 1), turn(block, 28, 1))
    quarter = jnp.where(lane24 < 16, right_side * gain_right, left_side * gain_left)
    quarter = jnp.where((lane24 < HALO) | (lane24 >= 28), turn_edges(right_side, left_side, lane24) * gain_main, quarter)
    quarter = jnp.where(lane24 < 32, quarter, 0.0)
    quarter = quarter + turn(quarter, 32, 1)
    design_strip = quarter + turn(quarter, 64, 1)

    def whole(inner, halo):
        return jnp.concatenate([inner, halo], axis=0)

    for z in range(Z):
        k = 48 + z // 2
        halo = unpack(above[k], below[k], low, z % 2)
        step = 0.5 / (4.0 + 0.5 * (whole(background[z], halo) + design_main))
        step = jnp.where(outside, 0.0, step)
        rate[z] = step
        keep[z] = 0.5 + 4.0 * step
    for t in range(2):
        halo = unpack(strip_above[12], strip_below[12], low, t)
        step = 0.5 / (4.0 + 0.5 * (whole(strips[12, t], halo) + design_strip))
        step = jnp.where(outside_strip, 0.0, step)
        strip_rate[t] = step
        strip_keep[t] = 0.5 + 4.0 * step

    starts = (field, adjoint, source, adjoint_source)
    for f in range(4):
        for c in range(3):
            g = 3 * f + c
            for z in range(Z):
                k = 4 * g + z // 2
                halo = unpack(above[k], below[k], low, z % 2)
                if f < 2:
                    fields[f, c, z] = whole(starts[f][c, z], jnp.where(outside8, 0.0, halo))
                else:
                    sources[f - 2, c, z] = whole(starts[f][c, z], halo)
            for t in range(2):
                halo = unpack(strip_above[g], strip_below[g], low, t)
                if f < 2:
                    strip_fields[f, c, t] = whole(strips[g, t], jnp.where(outside8, 0.0, halo))
                else:
                    strip_sources[f - 2, c, t] = whole(strips[g, t], halo)

    at_last, at_first = lane24 == LANES - 1, lane24 == 0

    def ahead_y(value):
        return turn(value, -1, 0)

    def behind_y(value):
        return turn(value, 1, 0)

    def ahead_x(value, strip, z):
        return jnp.where(at_last, turn(strip[z % 2], 123 - 32 * (z // 2), 1), turn(value, -1, 1))

    def behind_x(value, strip, z):
        return jnp.where(at_first, turn(strip[z % 2], -(32 * (z // 2) + 27), 1), turn(value, 1, 1))

    def sweep(_, carry):
        for f in range(2):
            ex, ey, ez = ([strip_fields[f, c, t] for t in range(2)] for c in range(3))
            for t in range(2):
                if t == 0:
                    ex_z, ey_z = ex[1], ey[1]
                else:
                    ex_z = jnp.where(lane24 < 96, turn(ex[0], -32, 1), 0.0)
                    ey_z = jnp.where(lane24 < 96, turn(ey[0], -32, 1), 0.0)
                strip_curls[f, 0, t] = (ahead_y(ez[t]) - ez[t]) - (ey_z - ey[t])
                strip_curls[f, 1, t] = (ex_z - ex[t]) - (turn(ez[t], -1, 1) - ez[t])
                strip_curls[f, 2, t] = (turn(ey[t], -1, 1) - ey[t]) - (ahead_y(ex[t]) - ex[t])
            for z in range(Z):
                ex, ey, ez = (fields[f, c, z] for c in range(3))
                if z < Z - 1:
                    ex_z, ey_z = fields[f, 0, z + 1], fields[f, 1, z + 1]
                else:
                    ex_z = ey_z = jnp.zeros_like(ex)
                curls[f, 0, z] = (ahead_y(ez) - ez) - (ey_z - ey)
                curls[f, 1, z] = (ex_z - ex) - (ahead_x(ez, strip_fields.at[f, 2], z) - ez)
                curls[f, 2, z] = (ahead_x(ey, strip_fields.at[f, 1], z) - ey) - (ahead_y(ex) - ex)
        bottom = lane24 < 32
        for f in range(2):
            for t in range(2):
                ex, ey, ez = (strip_fields[f, c, t] for c in range(3))
                hx, hy, hz = (strip_curls[f, c, t] for c in range(3))
                if t == 1:
                    hx_z, hy_z = strip_curls[f, 0, 0], strip_curls[f, 1, 0]
                else:
                    hx_z = jnp.where(bottom, -ey, turn(strip_curls[f, 0, 1], 32, 1))
                    hy_z = jnp.where(bottom, ex, turn(strip_curls[f, 1, 1], 32, 1))
                curl_x = (hz - behind_y(hz)) - (hy - hy_z)
                curl_y = (hx - hx_z) - (hz - turn(hz, 1, 1))
                curl_z = (hy - turn(hy, 1, 1)) - (hx - behind_y(hx))
                step, kept = strip_rate[t], strip_keep[t]
                strip_fields[f, 0, t] = kept * ex + step * (strip_sources[f, 0, t] - curl_x)
                strip_fields[f, 1, t] = kept * ey + step * (strip_sources[f, 1, t] - curl_y)
                strip_fields[f, 2, t] = kept * ez + step * (strip_sources[f, 2, t] - curl_z)
            for z in range(Z):
                ex, ey, ez = (fields[f, c, z] for c in range(3))
                hx, hy, hz = (curls[f, c, z] for c in range(3))
                if z > 0:
                    hx_z, hy_z = curls[f, 0, z - 1], curls[f, 1, z - 1]
                else:
                    hx_z, hy_z = -ey, ex
                curl_x = (hz - behind_y(hz)) - (hy - hy_z)
                curl_y = (hx - hx_z) - (hz - behind_x(hz, strip_curls.at[f, 2], z))
                curl_z = (hy - behind_x(hy, strip_curls.at[f, 1], z)) - (hx - behind_y(hx))
                step, kept = rate[z], keep[z]
                fields[f, 0, z] = kept * ex + step * (sources[f, 0, z] - curl_x)
                fields[f, 1, z] = kept * ey + step * (sources[f, 1, z] - curl_y)
                fields[f, 2, z] = kept * ez + step * (sources[f, 2, z] - curl_z)
        return carry

    lax.fori_loop(0, ITERS, sweep, 0)

    product = jnp.zeros((ROWS, LANES), jnp.float32)
    strip_product = jnp.zeros((ROWS, LANES), jnp.float32)
    for c in range(3):
        for z in range(Z):
            forward, backward = fields[0, c, z, 0:ROWS], fields[1, c, z, 0:ROWS]
            field_out[c, z] = forward
            adjoint_out[c, z] = backward
            product = product + forward * backward
        for t in range(2):
            strip_product = strip_product + strip_fields[0, c, t, 0:ROWS] * strip_fields[1, c, t, 0:ROWS]
    strip_product = strip_product + turn(strip_product, 64, 1)
    strip_product = strip_product + turn(strip_product, 32, 1)
    local = product * (-0.5 * gain_main[0:ROWS])
    lane = lanes_of(ROWS)
    local_side = jnp.where(
        lane < 64, turn(strip_product, -4, 1) * (-0.5 * gain_right[0:ROWS]),
        turn(strip_product, 100, 1) * (-0.5 * gain_left[0:ROWS]),
    )
    local_down[:, 0:LANES] = local[0:8]
    local_down[:, LANES : 2 * LANES] = local_side[0:8]
    local_up[:, 0:LANES] = local[8:16]
    local_up[:, LANES : 2 * LANES] = local_side[8:16]


def turn_edges(right_side, left_side, lane):
    return jnp.where(lane < 16, right_side, left_side)


def gradient_kernel(own_up, own_down, above, below, gradient, wide):
    row = lax.axis_index("gy")
    wide[0:8] = jnp.where(row == 0, 0.0, below[...])
    wide[8:16] = own_down[...]
    wide[16:24] = own_up[...]
    wide[24:32] = jnp.where(row == lax.axis_size("gy") - 1, 0.0, above[...])
    gradient[...] = cone(lambda a: wide[8 + a : 24 + a], ROWS)[:, :LANES]


def ring(axis, step):
    size = lax.axis_size(axis)
    return [(i, (i + step) % size) for i in range(size)]


def shape(*dims):
    return jax.ShapeDtypeStruct(dims, jnp.float32)


def call(kernel, outs, space=VMEM, scratch=()):
    def run(*operands):
        return pl.pallas_call(
            kernel,
            out_shape=outs,
            in_specs=[pl.BlockSpec(memory_space=space)] * len(operands),
            out_specs=jax.tree.map(lambda _: pl.BlockSpec(memory_space=VMEM), outs),
            scratch_shapes=scratch,
            compiler_params=pltpu.CompilerParams(vmem_limit_bytes=LIMIT),
        )(*operands)

    return run


def room(*dims):
    return pltpu.VMEM(dims, jnp.float32)


def on_device(background, density, design_tiles, material_tiles, contrast, source, adjoint_source, field_start, adjoint_start):
    inner = (field_start, adjoint_start, source, adjoint_source, background, density)
    tiles = (design_tiles, material_tiles, contrast)
    edges, rows = shape(GROUPS + 1, ROWS, LANES), shape(4 * GROUPS + 2, 8, LANES)
    right, left, up, down, gains, *inner = call(
        pack_kernel,
        [edges, edges, rows, rows, shape(3, WRAP, LANES)] + [shape(*a.shape) for a in inner],
        space=pltpu.HBM,
        scratch=[pltpu.SMEM(a.shape, a.dtype) for a in tiles] + [pltpu.SemaphoreType.DMA((9,))],
    )(*[pltpu.with_memory_space_constraint(a, pltpu.HBM) for a in (*tiles, *inner)])
    from_left = lax.ppermute(right, "gx", ring("gx", 1))
    from_right = lax.ppermute(left, "gx", ring("gx", -1))
    below = lax.ppermute(up, "gy", ring("gy", 1))
    above = lax.ppermute(down, "gy", ring("gy", -1))
    corner = shape(GROUPS + 2, 8, LANES)
    strips, side, strip_up, strip_down = call(
        strip_kernel, [shape(GROUPS, 2, ROWS, LANES), shape(ROWS, LANES), corner, corner]
    )(right, left, from_left, from_right)
    strip_below = lax.ppermute(strip_up, "gy", ring("gy", 1))
    strip_above = lax.ppermute(strip_down, "gy", ring("gy", -1))
    block, part = shape(3, Z, ROWS, LANES), shape(8, 2 * LANES)
    planes, sheets = (2, 3, Z, WRAP, LANES), (2, 3, 2, WRAP, LANES)
    field, adjoint, local_up, local_down = call(
        main_kernel,
        [block, block, part, part],
        scratch=[
            room(*planes), room(*planes), room(*planes), room(Z, WRAP, LANES), room(Z, WRAP, LANES),
            room(*sheets), room(*sheets), room(*sheets), room(2, WRAP, LANES), room(2, WRAP, LANES),
            room(48, 2 * LANES),
        ],
    )(gains, *inner, above, below, strips, side, strip_above, strip_below)
    local_below = lax.ppermute(local_up, "gy", ring("gy", 1))
    local_above = lax.ppermute(local_down, "gy", ring("gy", -1))
    gradient = call(gradient_kernel, shape(ROWS, LANES), scratch=[room(32, 2 * LANES)])(
        local_up, local_down, local_above, local_below
    )
    return (field, adjoint, gradient)


def solution(mesh):
    in_specs = (
        P(None, "gy", "gx"),
        P("gy", "gx"),
        P(),
        P(),
        P(),
        P(None, None, "gy", "gx"),
        P(None, None, "gy", "gx"),
        P(None, None, "gy", "gx"),
        P(None, None, "gy", "gx"),
    )
    out_specs = (P(None, None, "gy", "gx"), P(None, None, "gy", "gx"), P("gy", "gx"))
    return jax.shard_map(on_device, mesh=mesh, in_specs=in_specs, out_specs=out_specs, check_vma=False)
```

```python
import functools
import math

import jax
import jax.numpy as jnp
from jax import lax
from jax.experimental import pallas as pl
from jax.experimental.pallas import tpu as pltpu
from jax.sharding import PartitionSpec as P

ITERS = 4
RADIUS = 8
TILE = 128
Z = 8
ROWS = 16
LANES = 128
HALO = 4
WRAP = ROWS + 8
GROUPS = 13
VMEM = pltpu.VMEM
LIMIT = 48 * 1024 * 1024


def cone_weight(row_shift, col_shift):
    return max(0.0, RADIUS + 1 - math.sqrt(row_shift * row_shift + col_shift * col_shift))


def cone_total():
    span = range(-RADIUS, RADIUS + 1)
    return math.fsum(cone_weight(a, b) for a in span for b in span)


def lanes_of(rows):
    return lax.broadcasted_iota(jnp.int32, (rows, LANES), 1)


def rows_of(rows):
    return lax.broadcasted_iota(jnp.int32, (rows, LANES), 0)


def turn(value, shift, axis):
    size = value.shape[axis]
    return pltpu.roll(value, shift % size, axis)


def cone(rows_at, rows):
    total = cone_total()
    paired = [rows_at(0)]
    for a in range(1, RADIUS + 1):
        paired.append(rows_at(a) + rows_at(-a))
    result = None
    for b in range(RADIUS + 1):
        column = None
        for a in range(RADIUS + 1):
            weight = cone_weight(a, b)
            if weight > 0.0:
                term = paired[a] * (weight / total)
                column = term if column is None else column + term
        if b > 0:
            column = turn(column, b, 1) + turn(column, -b, 1)
        result = column if result is None else result + column
    return result


def pack_kernel(
    design_in, material_in, contrast_in, field_in, adjoint_in, source_in, adjoint_source_in, background_in, density_in,
    first, second, own_right, own_left, up, down, gains, field, adjoint, source, adjoint_source, background, density,
    design, material, contrast, done,
):
    arrays = (
        (field_in, field), (adjoint_in, adjoint), (source_in, source), (adjoint_source_in, adjoint_source),
        (background_in, background), (density_in, density),
        (design_in, design), (material_in, material), (contrast_in, contrast),
    )
    copies = [pltpu.make_async_copy(here, there, done.at[i]) for i, (here, there) in enumerate(arrays)]
    for copy in copies:
        copy.start()
    lane = lanes_of(ROWS)
    rightward = lax.axis_index("gx") % 2 == 0
    low = rows_of(8) < 4
    for g in range(GROUPS):
        if g % 3 == 0:
            copies[g // 3].wait()
        planes = background if g == 12 else (field, adjoint, source, adjoint_source)[g // 3].at[g % 3]
        to_right = to_left = None
        for z in range(Z):
            plane = planes[z]
            here_right = turn(plane, 16 * z + 12, 1)
            here_left = turn(plane, 16 * z + 4, 1)
            if z == 0:
                to_right, to_left = here_right, here_left
            else:
                chosen = lane >= 16 * z
                to_right = jnp.where(chosen, here_right, to_right)
                to_left = jnp.where(chosen, here_left, to_left)
        own_right[g] = to_right
        own_left[g] = to_left
        first[g] = jnp.where(rightward, to_right, to_left)
        second[g] = jnp.where(rightward, to_left, to_right)
        for pair in range(Z // 2):
            k = g * (Z // 2) + pair
            down[k] = jnp.where(low, planes[2 * pair, 0:8], turn(planes[2 * pair + 1, 0:8], 4, 0))
            up[k] = jnp.where(low, turn(planes[2 * pair + 1, 8:16], 4, 0), planes[2 * pair, 8:16])
    for copy in copies[5:]:
        copy.wait()
    first[GROUPS] = density[...]
    second[GROUPS] = density[...]
    for part in range(2):
        up[4 * GROUPS + part] = density[8 * part : 8 * part + 8]
        down[4 * GROUPS + part] = density[8 * part : 8 * part + 8]

    col, row = lax.axis_index("gx"), lax.axis_index("gy")
    row24 = rows_of(WRAP)
    tiles_y, tiles_x = design.shape

    def gain_at(first, tile_x):
        tile_y = jnp.clip(first, 0, tiles_y * TILE - 1) // TILE
        tile_x = jnp.clip(tile_x, 0, tiles_x - 1)
        return design[tile_y, tile_x].astype(jnp.float32) * contrast[material[tile_y, tile_x]]

    for k in range(3):
        tile_x = col + (0, 1, -1)[k]
        here = gain_at(row * ROWS, tile_x)
        up = gain_at(row * ROWS + ROWS, tile_x)
        down = gain_at(row * ROWS - HALO, tile_x)
        gains[k] = jnp.where(row24 < 16, here, jnp.where(row24 < 20, up, down))


def strip_kernel(own_right, own_left, first_got, second_got, strips, side, up, down):
    col = lax.axis_index("gx")
    rightward = col % 2 == 0
    first, last = col == 0, col == lax.axis_size("gx") - 1
    lane = lanes_of(ROWS)
    within = lane % 16
    half = lane % 32 < 16
    low = rows_of(8) < 4

    def sides(g):
        from_right = jnp.where(rightward, first_got[g], second_got[g])
        from_left = jnp.where(rightward, second_got[g], first_got[g])
        return jnp.where(last, 0.0, from_right), jnp.where(first, 0.0, from_left)

    for g in range(GROUPS):
        from_right, from_left = sides(g)
        here_right = jnp.where(within >= HALO, from_right, own_left[g])
        here_left = jnp.where(within < 12, from_left, own_right[g])
        even = jnp.where(half, here_right, turn(here_left, 16, 1))
        odd = jnp.where(half, turn(here_right, -16, 1), here_left)
        strips[g, 0] = even
        strips[g, 1] = odd
        down[g] = jnp.where(low, even[0:8], turn(odd[0:8], 4, 0))
        up[g] = jnp.where(low, turn(odd[8:16], 4, 0), even[8:16])
    from_right, from_left = sides(GROUPS)
    beside = jnp.where(lane < 64, from_right, from_left)
    side[...] = beside
    for part in range(2):
        up[GROUPS + part] = beside[8 * part : 8 * part + 8]
        down[GROUPS + part] = beside[8 * part : 8 * part + 8]


def unpack(above, below, low, odd):
    if odd:
        return turn(jnp.where(low, below, above), 4, 0)
    return jnp.where(low, above, below)


def main_kernel(
    gains, field, adjoint, source, adjoint_source, background, density,
    above, below, strips, side, strip_above, strip_below,
    field_out, adjoint_out, local_up, local_down,
    fields, sources, curls, rate, keep, strip_fields, strip_sources, strip_curls, strip_rate, strip_keep, wide,
):
    col, row = lax.axis_index("gx"), lax.axis_index("gy")
    cols, rows = lax.axis_size("gx"), lax.axis_size("gy")
    first_row, last_row = row == 0, row == rows - 1
    low = rows_of(8) < 4
    lane24, row24 = lanes_of(WRAP), rows_of(WRAP)
    outside8 = (low & last_row) | (jnp.logical_not(low) & first_row)
    outside = ((row24 >= 16) & (row24 < 20) & last_row) | ((row24 >= 20) & first_row)
    j = lane24 % 32
    outside_strip = outside | ((j >= HALO) & (j < 16) & (col == cols - 1)) | ((j >= 16) & (j < 28) & (col == 0))
    gain_main, gain_right, gain_left = gains[0], gains[1], gains[2]

    wide[0:8, 0:LANES] = jnp.where(first_row, 0.0, below[52])
    wide[8:16, 0:LANES] = jnp.where(first_row, 0.0, below[53])
    wide[0:8, LANES : 2 * LANES] = jnp.where(first_row, 0.0, strip_below[13])
    wide[8:16, LANES : 2 * LANES] = jnp.where(first_row, 0.0, strip_below[14])
    wide[16:32, 0:LANES] = density[...]
    wide[16:32, LANES : 2 * LANES] = side[...]
    wide[32:40, 0:LANES] = jnp.where(last_row, 0.0, above[52])
    wide[40:48, 0:LANES] = jnp.where(last_row, 0.0, above[53])
    wide[32:40, LANES : 2 * LANES] = jnp.where(last_row, 0.0, strip_above[13])
    wide[40:48, LANES : 2 * LANES] = jnp.where(last_row, 0.0, strip_above[14])
    filtered = cone(lambda a: wide[8 + a : 40 + a], 32)
    low2 = lax.broadcasted_iota(jnp.int32, (8, 2 * LANES), 0) < 4
    filtered = jnp.concatenate(
        [filtered[8:24], jnp.where(low2, filtered[24:32], filtered[0:8])], axis=0
    )
    design_main = gain_main * filtered[:, :LANES]
    beside = filtered[:, LANES:]
    block = filtered[:, :LANES]
    right_side = jnp.where(lane24 < HALO, turn(block, HALO, 1), turn(beside, HALO, 1))
    left_side = jnp.where(lane24 < 28, turn(beside, 28, 1), turn(block, 28, 1))
    quarter = jnp.where(lane24 < 16, right_side * gain_right, left_side * gain_left)
    quarter = jnp.where((lane24 < HALO) | (lane24 >= 28), turn_edges(right_side, left_side, lane24) * gain_main, quarter)
    quarter = jnp.where(lane24 < 32, quarter, 0.0)
    quarter = quarter + turn(quarter, 32, 1)
    design_strip = quarter + turn(quarter, 64, 1)

    def whole(inner, halo):
        return jnp.concatenate([inner, halo], axis=0)

    for z in range(Z):
        k = 48 + z // 2
        halo = unpack(above[k], below[k], low, z % 2)
        step = 0.5 / (4.0 + 0.5 * (whole(background[z], halo) + design_main))
        step = jnp.where(outside, 0.0, step)
        rate[z] = step
        keep[z] = 0.5 + 4.0 * step
    for t in range(2):
        halo = unpack(strip_above[12], strip_below[12], low, t)
        step = 0.5 / (4.0 + 0.5 * (whole(strips[12, t], halo) + design_strip))
        step = jnp.where(outside_strip, 0.0, step)
        strip_rate[t] = step
        strip_keep[t] = 0.5 + 4.0 * step

    starts = (field, adjoint, source, adjoint_source)
    for f in range(4):
        for c in range(3):
            g = 3 * f + c
            for z in range(Z):
                k = 4 * g + z // 2
                halo = unpack(above[k], below[k], low, z % 2)
                if f < 2:
                    fields[f, c, z] = whole(starts[f][c, z], jnp.where(outside8, 0.0, halo))
                else:
                    sources[f - 2, c, z] = whole(starts[f][c, z], halo)
            for t in range(2):
                halo = unpack(strip_above[g], strip_below[g], low, t)
                if f < 2:
                    strip_fields[f, c, t] = whole(strips[g, t], jnp.where(outside8, 0.0, halo))
                else:
                    strip_sources[f - 2, c, t] = whole(strips[g, t], halo)

    at_last, at_first = lane24 == LANES - 1, lane24 == 0

    def ahead_y(value):
        return turn(value, -1, 0)

    def behind_y(value):
        return turn(value, 1, 0)

    def ahead_x(value, strip, z):
        return jnp.where(at_last, turn(strip[z % 2], 123 - 32 * (z // 2), 1), turn(value, -1, 1))

    def behind_x(value, strip, z):
        return jnp.where(at_first, turn(strip[z % 2], -(32 * (z // 2) + 27), 1), turn(value, 1, 1))

    def sweep(_, carry):
        for f in range(2):
            ex, ey, ez = ([strip_fields[f, c, t] for t in range(2)] for c in range(3))
            for t in range(2):
                if t == 0:
                    ex_z, ey_z = ex[1], ey[1]
                else:
                    ex_z = jnp.where(lane24 < 96, turn(ex[0], -32, 1), 0.0)
                    ey_z = jnp.where(lane24 < 96, turn(ey[0], -32, 1), 0.0)
                strip_curls[f, 0, t] = (ahead_y(ez[t]) - ez[t]) - (ey_z - ey[t])
                strip_curls[f, 1, t] = (ex_z - ex[t]) - (turn(ez[t], -1, 1) - ez[t])
                strip_curls[f, 2, t] = (turn(ey[t], -1, 1) - ey[t]) - (ahead_y(ex[t]) - ex[t])
            for z in range(Z):
                ex, ey, ez = (fields[f, c, z] for c in range(3))
                if z < Z - 1:
                    ex_z, ey_z = fields[f, 0, z + 1], fields[f, 1, z + 1]
                else:
                    ex_z = ey_z = jnp.zeros_like(ex)
                curls[f, 0, z] = (ahead_y(ez) - ez) - (ey_z - ey)
                curls[f, 1, z] = (ex_z - ex) - (ahead_x(ez, strip_fields.at[f, 2], z) - ez)
                curls[f, 2, z] = (ahead_x(ey, strip_fields.at[f, 1], z) - ey) - (ahead_y(ex) - ex)
        bottom = lane24 < 32
        for f in range(2):
            for t in range(2):
                ex, ey, ez = (strip_fields[f, c, t] for c in range(3))
                hx, hy, hz = (strip_curls[f, c, t] for c in range(3))
                if t == 1:
                    hx_z, hy_z = strip_curls[f, 0, 0], strip_curls[f, 1, 0]
                else:
                    hx_z = jnp.where(bottom, -ey, turn(strip_curls[f, 0, 1], 32, 1))
                    hy_z = jnp.where(bottom, ex, turn(strip_curls[f, 1, 1], 32, 1))
                curl_x = (hz - behind_y(hz)) - (hy - hy_z)
                curl_y = (hx - hx_z) - (hz - turn(hz, 1, 1))
                curl_z = (hy - turn(hy, 1, 1)) - (hx - behind_y(hx))
                step, kept = strip_rate[t], strip_keep[t]
                strip_fields[f, 0, t] = kept * ex + step * (strip_sources[f, 0, t] - curl_x)
                strip_fields[f, 1, t] = kept * ey + step * (strip_sources[f, 1, t] - curl_y)
                strip_fields[f, 2, t] = kept * ez + step * (strip_sources[f, 2, t] - curl_z)
            for z in range(Z):
                ex, ey, ez = (fields[f, c, z] for c in range(3))
                hx, hy, hz = (curls[f, c, z] for c in range(3))
                if z > 0:
                    hx_z, hy_z = curls[f, 0, z - 1], curls[f, 1, z - 1]
                else:
                    hx_z, hy_z = -ey, ex
                curl_x = (hz - behind_y(hz)) - (hy - hy_z)
                curl_y = (hx - hx_z) - (hz - behind_x(hz, strip_curls.at[f, 2], z))
                curl_z = (hy - behind_x(hy, strip_curls.at[f, 1], z)) - (hx - behind_y(hx))
                step, kept = rate[z], keep[z]
                fields[f, 0, z] = kept * ex + step * (sources[f, 0, z] - curl_x)
                fields[f, 1, z] = kept * ey + step * (sources[f, 1, z] - curl_y)
                fields[f, 2, z] = kept * ez + step * (sources[f, 2, z] - curl_z)
        return carry

    lax.fori_loop(0, ITERS, sweep, 0)

    product = jnp.zeros((ROWS, LANES), jnp.float32)
    strip_product = jnp.zeros((ROWS, LANES), jnp.float32)
    for c in range(3):
        for z in range(Z):
            forward, backward = fields[0, c, z, 0:ROWS], fields[1, c, z, 0:ROWS]
            field_out[c, z] = forward
            adjoint_out[c, z] = backward
            product = product + forward * backward
        for t in range(2):
            strip_product = strip_product + strip_fields[0, c, t, 0:ROWS] * strip_fields[1, c, t, 0:ROWS]
    strip_product = strip_product + turn(strip_product, 64, 1)
    strip_product = strip_product + turn(strip_product, 32, 1)
    local = product * (-0.5 * gain_main[0:ROWS])
    lane = lanes_of(ROWS)
    local_side = jnp.where(
        lane < 64, turn(strip_product, -4, 1) * (-0.5 * gain_right[0:ROWS]),
        turn(strip_product, 100, 1) * (-0.5 * gain_left[0:ROWS]),
    )
    local_down[:, 0:LANES] = local[0:8]
    local_down[:, LANES : 2 * LANES] = local_side[0:8]
    local_up[:, 0:LANES] = local[8:16]
    local_up[:, LANES : 2 * LANES] = local_side[8:16]


def turn_edges(right_side, left_side, lane):
    return jnp.where(lane < 16, right_side, left_side)


def gradient_kernel(own_up, own_down, above, below, gradient, wide):
    row = lax.axis_index("gy")
    wide[0:8] = jnp.where(row == 0, 0.0, below[...])
    wide[8:16] = own_down[...]
    wide[16:24] = own_up[...]
    wide[24:32] = jnp.where(row == lax.axis_size("gy") - 1, 0.0, above[...])
    gradient[...] = cone(lambda a: wide[8 + a : 24 + a], ROWS)[:, :LANES]


def swaps(axis, start):
    size = lax.axis_size(axis)
    pairs = [(i, i + 1) for i in range(start, size - 1, 2)]
    return sorted(pairs + [(j, i) for i, j in pairs])


def ring(axis, step):
    size = lax.axis_size(axis)
    return [(i, (i + step) % size) for i in range(size)]


def shape(*dims):
    return jax.ShapeDtypeStruct(dims, jnp.float32)


def call(kernel, outs, space=VMEM, scratch=()):
    def run(*operands):
        return pl.pallas_call(
            kernel,
            out_shape=outs,
            in_specs=[pl.BlockSpec(memory_space=space)] * len(operands),
            out_specs=jax.tree.map(lambda _: pl.BlockSpec(memory_space=VMEM), outs),
            scratch_shapes=scratch,
            compiler_params=pltpu.CompilerParams(vmem_limit_bytes=LIMIT),
        )(*operands)

    return run


def room(*dims):
    return pltpu.VMEM(dims, jnp.float32)


def on_device(background, density, design_tiles, material_tiles, contrast, source, adjoint_source, field_start, adjoint_start):
    inner = (field_start, adjoint_start, source, adjoint_source, background, density)
    tiles = (design_tiles, material_tiles, contrast)
    edges, rows = shape(GROUPS + 1, ROWS, LANES), shape(4 * GROUPS + 2, 8, LANES)
    first, second, own_right, own_left, up, down, gains, *inner = call(
        pack_kernel,
        [edges, edges, edges, edges, rows, rows, shape(3, WRAP, LANES)] + [shape(*a.shape) for a in inner],
        space=pltpu.HBM,
        scratch=[pltpu.SMEM(a.shape, a.dtype) for a in tiles] + [pltpu.SemaphoreType.DMA((9,))],
    )(*[pltpu.with_memory_space_constraint(a, pltpu.HBM) for a in (*tiles, *inner)])
    first_got = lax.ppermute(first, "gx", swaps("gx", 0))
    second_got = lax.ppermute(second, "gx", swaps("gx", 1))
    below = lax.ppermute(up, "gy", ring("gy", 1))
    above = lax.ppermute(down, "gy", ring("gy", -1))
    corner = shape(GROUPS + 2, 8, LANES)
    strips, side, strip_up, strip_down = call(
        strip_kernel, [shape(GROUPS, 2, ROWS, LANES), shape(ROWS, LANES), corner, corner]
    )(own_right, own_left, first_got, second_got)
    strip_below = lax.ppermute(strip_up, "gy", ring("gy", 1))
    strip_above = lax.ppermute(strip_down, "gy", ring("gy", -1))
    block, part = shape(3, Z, ROWS, LANES), shape(8, 2 * LANES)
    planes, sheets = (2, 3, Z, WRAP, LANES), (2, 3, 2, WRAP, LANES)
    field, adjoint, local_up, local_down = call(
        main_kernel,
        [block, block, part, part],
        scratch=[
            room(*planes), room(*planes), room(*planes), room(Z, WRAP, LANES), room(Z, WRAP, LANES),
            room(*sheets), room(*sheets), room(*sheets), room(2, WRAP, LANES), room(2, WRAP, LANES),
            room(48, 2 * LANES),
        ],
    )(gains, *inner, above, below, strips, side, strip_above, strip_below)
    local_below = lax.ppermute(local_up, "gy", ring("gy", 1))
    local_above = lax.ppermute(local_down, "gy", ring("gy", -1))
    gradient = call(gradient_kernel, shape(ROWS, LANES), scratch=[room(32, 2 * LANES)])(
        local_up, local_down, local_above, local_below
    )
    return (field, adjoint, gradient)


def solution(mesh):
    in_specs = (
        P(None, "gy", "gx"),
        P("gy", "gx"),
        P(),
        P(),
        P(),
        P(None, None, "gy", "gx"),
        P(None, None, "gy", "gx"),
        P(None, None, "gy", "gx"),
        P(None, None, "gy", "gx"),
    )
    out_specs = (P(None, None, "gy", "gx"), P(None, None, "gy", "gx"), P("gy", "gx"))
    return jax.shard_map(on_device, mesh=mesh, in_specs=in_specs, out_specs=out_specs, check_vma=False)
```

```python
import functools
import math

import jax
import jax.numpy as jnp
from jax import lax
from jax.experimental import pallas as pl
from jax.experimental.pallas import tpu as pltpu
from jax.sharding import PartitionSpec as P

ITERS = 4
RADIUS = 8
TILE = 128
Z = 8
ROWS = 16
LANES = 128
HALO = 4
WRAP = ROWS + 8
GROUPS = 13
VMEM = pltpu.VMEM
LIMIT = 48 * 1024 * 1024


def cone_weight(row_shift, col_shift):
    return max(0.0, RADIUS + 1 - math.sqrt(row_shift * row_shift + col_shift * col_shift))


def cone_total():
    span = range(-RADIUS, RADIUS + 1)
    return math.fsum(cone_weight(a, b) for a in span for b in span)


def lanes_of(rows):
    return lax.broadcasted_iota(jnp.int32, (rows, LANES), 1)


def rows_of(rows):
    return lax.broadcasted_iota(jnp.int32, (rows, LANES), 0)


def turn(value, shift, axis):
    size = value.shape[axis]
    return pltpu.roll(value, shift % size, axis)


def cone(rows_at, rows):
    total = cone_total()
    paired = [rows_at(0)]
    for a in range(1, RADIUS + 1):
        paired.append(rows_at(a) + rows_at(-a))
    result = None
    for b in range(RADIUS + 1):
        column = None
        for a in range(RADIUS + 1):
            weight = cone_weight(a, b)
            if weight > 0.0:
                term = paired[a] * (weight / total)
                column = term if column is None else column + term
        if b > 0:
            column = turn(column, b, 1) + turn(column, -b, 1)
        result = column if result is None else result + column
    return result


def pack_kernel(
    design_in, material_in, contrast_in, field_in, adjoint_in, source_in, adjoint_source_in, background_in, density_in,
    first, second, own_right, own_left, up, down, gains, field, adjoint, source, adjoint_source, background, density,
    design, material, contrast, done,
):
    arrays = (
        (field_in, field), (adjoint_in, adjoint), (source_in, source), (adjoint_source_in, adjoint_source),
        (background_in, background), (density_in, density),
        (design_in, design), (material_in, material), (contrast_in, contrast),
    )
    copies = [pltpu.make_async_copy(here, there, done.at[i]) for i, (here, there) in enumerate(arrays)]
    for copy in copies:
        copy.start()
    lane = lanes_of(ROWS)
    rightward = lax.axis_index("gx") % 2 == 1
    low = rows_of(8) < 4
    for g in range(GROUPS):
        if g % 3 == 0:
            copies[g // 3].wait()
        planes = background if g == 12 else (field, adjoint, source, adjoint_source)[g // 3].at[g % 3]
        to_right = to_left = None
        for z in range(Z):
            plane = planes[z]
            here_right = turn(plane, 16 * z + 12, 1)
            here_left = turn(plane, 16 * z + 4, 1)
            if z == 0:
                to_right, to_left = here_right, here_left
            else:
                chosen = lane >= 16 * z
                to_right = jnp.where(chosen, here_right, to_right)
                to_left = jnp.where(chosen, here_left, to_left)
        own_right[g] = to_right
        own_left[g] = to_left
        first[g] = jnp.where(rightward, to_right, to_left)
        second[g] = jnp.where(rightward, to_left, to_right)
        for pair in range(Z // 2):
            k = g * (Z // 2) + pair
            down[k] = jnp.where(low, planes[2 * pair, 0:8], turn(planes[2 * pair + 1, 0:8], 4, 0))
            up[k] = jnp.where(low, turn(planes[2 * pair + 1, 8:16], 4, 0), planes[2 * pair, 8:16])
    for copy in copies[5:]:
        copy.wait()
    first[GROUPS] = density[...]
    second[GROUPS] = density[...]
    for part in range(2):
        up[4 * GROUPS + part] = density[8 * part : 8 * part + 8]
        down[4 * GROUPS + part] = density[8 * part : 8 * part + 8]

    col, row = lax.axis_index("gx"), lax.axis_index("gy")
    row24 = rows_of(WRAP)
    tiles_y, tiles_x = design.shape

    def gain_at(first, tile_x):
        tile_y = jnp.clip(first, 0, tiles_y * TILE - 1) // TILE
        tile_x = jnp.clip(tile_x, 0, tiles_x - 1)
        return design[tile_y, tile_x].astype(jnp.float32) * contrast[material[tile_y, tile_x]]

    for k in range(3):
        tile_x = col + (0, 1, -1)[k]
        here = gain_at(row * ROWS, tile_x)
        up = gain_at(row * ROWS + ROWS, tile_x)
        down = gain_at(row * ROWS - HALO, tile_x)
        gains[k] = jnp.where(row24 < 16, here, jnp.where(row24 < 20, up, down))


def strip_kernel(own_right, own_left, first_got, second_got, strips, side, up, down):
    col = lax.axis_index("gx")
    rightward = col % 2 == 1
    first, last = col == 0, col == lax.axis_size("gx") - 1
    lane = lanes_of(ROWS)
    within = lane % 16
    half = lane % 32 < 16
    low = rows_of(8) < 4

    def sides(g):
        from_right = jnp.where(rightward, first_got[g], second_got[g])
        from_left = jnp.where(rightward, second_got[g], first_got[g])
        return jnp.where(last, 0.0, from_right), jnp.where(first, 0.0, from_left)

    for g in range(GROUPS):
        from_right, from_left = sides(g)
        here_right = jnp.where(within >= HALO, from_right, own_left[g])
        here_left = jnp.where(within < 12, from_left, own_right[g])
        even = jnp.where(half, here_right, turn(here_left, 16, 1))
        odd = jnp.where(half, turn(here_right, -16, 1), here_left)
        strips[g, 0] = even
        strips[g, 1] = odd
        down[g] = jnp.where(low, even[0:8], turn(odd[0:8], 4, 0))
        up[g] = jnp.where(low, turn(odd[8:16], 4, 0), even[8:16])
    from_right, from_left = sides(GROUPS)
    beside = jnp.where(lane < 64, from_right, from_left)
    side[...] = beside
    for part in range(2):
        up[GROUPS + part] = beside[8 * part : 8 * part + 8]
        down[GROUPS + part] = beside[8 * part : 8 * part + 8]


def unpack(above, below, low, odd):
    if odd:
        return turn(jnp.where(low, below, above), 4, 0)
    return jnp.where(low, above, below)


def main_kernel(
    gains, field, adjoint, source, adjoint_source, background, density,
    above, below, strips, side, strip_above, strip_below,
    field_out, adjoint_out, local_up, local_down,
    fields, sources, curls, rate, keep, strip_fields, strip_sources, strip_curls, strip_rate, strip_keep, wide,
):
    col, row = lax.axis_index("gx"), lax.axis_index("gy")
    cols, rows = lax.axis_size("gx"), lax.axis_size("gy")
    first_row, last_row = row == 0, row == rows - 1
    low = rows_of(8) < 4
    lane24, row24 = lanes_of(WRAP), rows_of(WRAP)
    outside8 = (low & last_row) | (jnp.logical_not(low) & first_row)
    outside = ((row24 >= 16) & (row24 < 20) & last_row) | ((row24 >= 20) & first_row)
    j = lane24 % 32
    outside_strip = outside | ((j >= HALO) & (j < 16) & (col == cols - 1)) | ((j >= 16) & (j < 28) & (col == 0))
    gain_main, gain_right, gain_left = gains[0], gains[1], gains[2]

    wide[0:8, 0:LANES] = jnp.where(first_row, 0.0, below[52])
    wide[8:16, 0:LANES] = jnp.where(first_row, 0.0, below[53])
    wide[0:8, LANES : 2 * LANES] = jnp.where(first_row, 0.0, strip_below[13])
    wide[8:16, LANES : 2 * LANES] = jnp.where(first_row, 0.0, strip_below[14])
    wide[16:32, 0:LANES] = density[...]
    wide[16:32, LANES : 2 * LANES] = side[...]
    wide[32:40, 0:LANES] = jnp.where(last_row, 0.0, above[52])
    wide[40:48, 0:LANES] = jnp.where(last_row, 0.0, above[53])
    wide[32:40, LANES : 2 * LANES] = jnp.where(last_row, 0.0, strip_above[13])
    wide[40:48, LANES : 2 * LANES] = jnp.where(last_row, 0.0, strip_above[14])
    filtered = cone(lambda a: wide[8 + a : 40 + a], 32)
    low2 = lax.broadcasted_iota(jnp.int32, (8, 2 * LANES), 0) < 4
    filtered = jnp.concatenate(
        [filtered[8:24], jnp.where(low2, filtered[24:32], filtered[0:8])], axis=0
    )
    design_main = gain_main * filtered[:, :LANES]
    beside = filtered[:, LANES:]
    block = filtered[:, :LANES]
    right_side = jnp.where(lane24 < HALO, turn(block, HALO, 1), turn(beside, HALO, 1))
    left_side = jnp.where(lane24 < 28, turn(beside, 28, 1), turn(block, 28, 1))
    quarter = jnp.where(lane24 < 16, right_side * gain_right, left_side * gain_left)
    quarter = jnp.where((lane24 < HALO) | (lane24 >= 28), turn_edges(right_side, left_side, lane24) * gain_main, quarter)
    quarter = jnp.where(lane24 < 32, quarter, 0.0)
    quarter = quarter + turn(quarter, 32, 1)
    design_strip = quarter + turn(quarter, 64, 1)

    def whole(inner, halo):
        return jnp.concatenate([inner, halo], axis=0)

    for z in range(Z):
        k = 48 + z // 2
        halo = unpack(above[k], below[k], low, z % 2)
        step = 0.5 / (4.0 + 0.5 * (whole(background[z], halo) + design_main))
        step = jnp.where(outside, 0.0, step)
        rate[z] = step
        keep[z] = 0.5 + 4.0 * step
    for t in range(2):
        halo = unpack(strip_above[12], strip_below[12], low, t)
        step = 0.5 / (4.0 + 0.5 * (whole(strips[12, t], halo) + design_strip))
        step = jnp.where(outside_strip, 0.0, step)
        strip_rate[t] = step
        strip_keep[t] = 0.5 + 4.0 * step

    starts = (field, adjoint, source, adjoint_source)
    for f in range(4):
        for c in range(3):
            g = 3 * f + c
            for z in range(Z):
                k = 4 * g + z // 2
                halo = unpack(above[k], below[k], low, z % 2)
                if f < 2:
                    fields[f, c, z] = whole(starts[f][c, z], jnp.where(outside8, 0.0, halo))
                else:
                    sources[f - 2, c, z] = whole(starts[f][c, z], halo)
            for t in range(2):
                halo = unpack(strip_above[g], strip_below[g], low, t)
                if f < 2:
                    strip_fields[f, c, t] = whole(strips[g, t], jnp.where(outside8, 0.0, halo))
                else:
                    strip_sources[f - 2, c, t] = whole(strips[g, t], halo)

    at_last, at_first = lane24 == LANES - 1, lane24 == 0

    def ahead_y(value):
        return turn(value, -1, 0)

    def behind_y(value):
        return turn(value, 1, 0)

    def ahead_x(value, strip, z):
        return jnp.where(at_last, turn(strip[z % 2], 123 - 32 * (z // 2), 1), turn(value, -1, 1))

    def behind_x(value, strip, z):
        return jnp.where(at_first, turn(strip[z % 2], -(32 * (z // 2) + 27), 1), turn(value, 1, 1))

    def sweep():
        for f in range(2):
            ex, ey, ez = ([strip_fields[f, c, t] for t in range(2)] for c in range(3))
            for t in range(2):
                if t == 0:
                    ex_z, ey_z = ex[1], ey[1]
                else:
                    ex_z = jnp.where(lane24 < 96, turn(ex[0], -32, 1), 0.0)
                    ey_z = jnp.where(lane24 < 96, turn(ey[0], -32, 1), 0.0)
                strip_curls[f, 0, t] = (ahead_y(ez[t]) - ez[t]) - (ey_z - ey[t])
                strip_curls[f, 1, t] = (ex_z - ex[t]) - (turn(ez[t], -1, 1) - ez[t])
                strip_curls[f, 2, t] = (turn(ey[t], -1, 1) - ey[t]) - (ahead_y(ex[t]) - ex[t])
            for z in range(Z):
                ex, ey, ez = (fields[f, c, z] for c in range(3))
                if z < Z - 1:
                    ex_z, ey_z = fields[f, 0, z + 1], fields[f, 1, z + 1]
                else:
                    ex_z = ey_z = jnp.zeros_like(ex)
                curls[f, 0, z] = (ahead_y(ez) - ez) - (ey_z - ey)
                curls[f, 1, z] = (ex_z - ex) - (ahead_x(ez, strip_fields.at[f, 2], z) - ez)
                curls[f, 2, z] = (ahead_x(ey, strip_fields.at[f, 1], z) - ey) - (ahead_y(ex) - ex)
        bottom = lane24 < 32
        for f in range(2):
            for t in range(2):
                ex, ey, ez = (strip_fields[f, c, t] for c in range(3))
                hx, hy, hz = (strip_curls[f, c, t] for c in range(3))
                if t == 1:
                    hx_z, hy_z = strip_curls[f, 0, 0], strip_curls[f, 1, 0]
                else:
                    hx_z = jnp.where(bottom, -ey, turn(strip_curls[f, 0, 1], 32, 1))
                    hy_z = jnp.where(bottom, ex, turn(strip_curls[f, 1, 1], 32, 1))
                curl_x = (hz - behind_y(hz)) - (hy - hy_z)
                curl_y = (hx - hx_z) - (hz - turn(hz, 1, 1))
                curl_z = (hy - turn(hy, 1, 1)) - (hx - behind_y(hx))
                step, kept = strip_rate[t], strip_keep[t]
                strip_fields[f, 0, t] = kept * ex + step * (strip_sources[f, 0, t] - curl_x)
                strip_fields[f, 1, t] = kept * ey + step * (strip_sources[f, 1, t] - curl_y)
                strip_fields[f, 2, t] = kept * ez + step * (strip_sources[f, 2, t] - curl_z)
            for z in range(Z):
                ex, ey, ez = (fields[f, c, z] for c in range(3))
                hx, hy, hz = (curls[f, c, z] for c in range(3))
                if z > 0:
                    hx_z, hy_z = curls[f, 0, z - 1], curls[f, 1, z - 1]
                else:
                    hx_z, hy_z = -ey, ex
                curl_x = (hz - behind_y(hz)) - (hy - hy_z)
                curl_y = (hx - hx_z) - (hz - behind_x(hz, strip_curls.at[f, 2], z))
                curl_z = (hy - behind_x(hy, strip_curls.at[f, 1], z)) - (hx - behind_y(hx))
                step, kept = rate[z], keep[z]
                fields[f, 0, z] = kept * ex + step * (sources[f, 0, z] - curl_x)
                fields[f, 1, z] = kept * ey + step * (sources[f, 1, z] - curl_y)
                fields[f, 2, z] = kept * ez + step * (sources[f, 2, z] - curl_z)
    for _ in range(ITERS):
        sweep()

    product = jnp.zeros((ROWS, LANES), jnp.float32)
    strip_product = jnp.zeros((ROWS, LANES), jnp.float32)
    for c in range(3):
        for z in range(Z):
            forward, backward = fields[0, c, z, 0:ROWS], fields[1, c, z, 0:ROWS]
            field_out[c, z] = forward
            adjoint_out[c, z] = backward
            product = product + forward * backward
        for t in range(2):
            strip_product = strip_product + strip_fields[0, c, t, 0:ROWS] * strip_fields[1, c, t, 0:ROWS]
    strip_product = strip_product + turn(strip_product, 64, 1)
    strip_product = strip_product + turn(strip_product, 32, 1)
    local = product * (-0.5 * gain_main[0:ROWS])
    lane = lanes_of(ROWS)
    local_side = jnp.where(
        lane < 64, turn(strip_product, -4, 1) * (-0.5 * gain_right[0:ROWS]),
        turn(strip_product, 100, 1) * (-0.5 * gain_left[0:ROWS]),
    )
    local_down[:, 0:LANES] = local[0:8]
    local_down[:, LANES : 2 * LANES] = local_side[0:8]
    local_up[:, 0:LANES] = local[8:16]
    local_up[:, LANES : 2 * LANES] = local_side[8:16]


def turn_edges(right_side, left_side, lane):
    return jnp.where(lane < 16, right_side, left_side)


def gradient_kernel(own_up, own_down, above, below, gradient, wide):
    row = lax.axis_index("gy")
    wide[0:8] = jnp.where(row == 0, 0.0, below[...])
    wide[8:16] = own_down[...]
    wide[16:24] = own_up[...]
    wide[24:32] = jnp.where(row == lax.axis_size("gy") - 1, 0.0, above[...])
    gradient[...] = cone(lambda a: wide[8 + a : 24 + a], ROWS)[:, :LANES]


def swaps(axis, start):
    size = lax.axis_size(axis)
    pairs = [(i, i + 1) for i in range(start, size - 1, 2)]
    return sorted(pairs + [(j, i) for i, j in pairs])


def ring(axis, step):
    size = lax.axis_size(axis)
    return [(i, (i + step) % size) for i in range(size)]


def shape(*dims):
    return jax.ShapeDtypeStruct(dims, jnp.float32)


def call(kernel, outs, space=VMEM, scratch=()):
    def run(*operands):
        return pl.pallas_call(
            kernel,
            out_shape=outs,
            in_specs=[pl.BlockSpec(memory_space=space)] * len(operands),
            out_specs=jax.tree.map(lambda _: pl.BlockSpec(memory_space=VMEM), outs),
            scratch_shapes=scratch,
            compiler_params=pltpu.CompilerParams(vmem_limit_bytes=LIMIT),
        )(*operands)

    return run


def room(*dims):
    return pltpu.VMEM(dims, jnp.float32)


def on_device(background, density, design_tiles, material_tiles, contrast, source, adjoint_source, field_start, adjoint_start):
    inner = (field_start, adjoint_start, source, adjoint_source, background, density)
    tiles = (design_tiles, material_tiles, contrast)
    edges, rows = shape(GROUPS + 1, ROWS, LANES), shape(4 * GROUPS + 2, 8, LANES)
    first, second, own_right, own_left, up, down, gains, *inner = call(
        pack_kernel,
        [edges, edges, edges, edges, rows, rows, shape(3, WRAP, LANES)] + [shape(*a.shape) for a in inner],
        space=pltpu.HBM,
        scratch=[pltpu.SMEM(a.shape, a.dtype) for a in tiles] + [pltpu.SemaphoreType.DMA((9,))],
    )(*[pltpu.with_memory_space_constraint(a, pltpu.HBM) for a in (*tiles, *inner)])
    first_got = lax.ppermute(first, "gx", swaps("gx", 1))
    second_got = lax.ppermute(second, "gx", swaps("gx", 0))
    below = lax.ppermute(up, "gy", ring("gy", 1))
    above = lax.ppermute(down, "gy", ring("gy", -1))
    corner = shape(GROUPS + 2, 8, LANES)
    strips, side, strip_up, strip_down = call(
        strip_kernel, [shape(GROUPS, 2, ROWS, LANES), shape(ROWS, LANES), corner, corner]
    )(own_right, own_left, first_got, second_got)
    strip_below = lax.ppermute(strip_up, "gy", ring("gy", 1))
    strip_above = lax.ppermute(strip_down, "gy", ring("gy", -1))
    block, part = shape(3, Z, ROWS, LANES), shape(8, 2 * LANES)
    planes, sheets = (2, 3, Z, WRAP, LANES), (2, 3, 2, WRAP, LANES)
    field, adjoint, local_up, local_down = call(
        main_kernel,
        [block, block, part, part],
        scratch=[
            room(*planes), room(*planes), room(*planes), room(Z, WRAP, LANES), room(Z, WRAP, LANES),
            room(*sheets), room(*sheets), room(*sheets), room(2, WRAP, LANES), room(2, WRAP, LANES),
            room(48, 2 * LANES),
        ],
    )(gains, *inner, above, below, strips, side, strip_above, strip_below)
    local_below = lax.ppermute(local_up, "gy", ring("gy", 1))
    local_above = lax.ppermute(local_down, "gy", ring("gy", -1))
    gradient = call(gradient_kernel, shape(ROWS, LANES), scratch=[room(32, 2 * LANES)])(
        local_up, local_down, local_above, local_below
    )
    return (field, adjoint, gradient)


def solution(mesh):
    in_specs = (
        P(None, "gy", "gx"),
        P("gy", "gx"),
        P(),
        P(),
        P(),
        P(None, None, "gy", "gx"),
        P(None, None, "gy", "gx"),
        P(None, None, "gy", "gx"),
        P(None, None, "gy", "gx"),
    )
    out_specs = (P(None, None, "gy", "gx"), P(None, None, "gy", "gx"), P("gy", "gx"))
    return jax.shard_map(on_device, mesh=mesh, in_specs=in_specs, out_specs=out_specs, check_vma=False)
```

```python
import functools
import math

import jax
import jax.numpy as jnp
from jax import lax
from jax.experimental import pallas as pl
from jax.experimental.pallas import tpu as pltpu
from jax.sharding import PartitionSpec as P

ITERS = 4
RADIUS = 8
TILE = 128
Z = 8
ROWS = 16
LANES = 128
HALO = 4
WRAP = ROWS + 8
GROUPS = 13
VMEM = pltpu.VMEM
LIMIT = 48 * 1024 * 1024


def cone_weight(row_shift, col_shift):
    return max(0.0, RADIUS + 1 - math.sqrt(row_shift * row_shift + col_shift * col_shift))


def cone_total():
    span = range(-RADIUS, RADIUS + 1)
    return math.fsum(cone_weight(a, b) for a in span for b in span)


def lanes_of(rows):
    return lax.broadcasted_iota(jnp.int32, (rows, LANES), 1)


def rows_of(rows):
    return lax.broadcasted_iota(jnp.int32, (rows, LANES), 0)


def turn(value, shift, axis):
    size = value.shape[axis]
    return pltpu.roll(value, shift % size, axis)


def cone(rows_at, rows):
    total = cone_total()
    paired = [rows_at(0)]
    for a in range(1, RADIUS + 1):
        paired.append(rows_at(a) + rows_at(-a))
    result = None
    for b in range(RADIUS + 1):
        column = None
        for a in range(RADIUS + 1):
            weight = cone_weight(a, b)
            if weight > 0.0:
                term = paired[a] * (weight / total)
                column = term if column is None else column + term
        if b > 0:
            column = turn(column, b, 1) + turn(column, -b, 1)
        result = column if result is None else result + column
    return result


def pack_kernel(
    design_in, material_in, contrast_in, field_in, adjoint_in, source_in, adjoint_source_in, background_in, density_in,
    first, second, own_right, own_left, far, near, gains, field, adjoint, source, adjoint_source, background, density,
    design, material, contrast, done,
):
    arrays = (
        (field_in, field), (adjoint_in, adjoint), (source_in, source), (adjoint_source_in, adjoint_source),
        (background_in, background), (density_in, density),
        (design_in, design), (material_in, material), (contrast_in, contrast),
    )
    copies = [pltpu.make_async_copy(here, there, done.at[i]) for i, (here, there) in enumerate(arrays)]
    for copy in copies:
        copy.start()
    lane = lanes_of(ROWS)
    rightward = lax.axis_index("gx") % 2 == 1
    upward = lax.axis_index("gy") % 2 == 1
    low = rows_of(8) < 4
    for g in range(GROUPS):
        if g % 3 == 0:
            copies[g // 3].wait()
        planes = background if g == 12 else (field, adjoint, source, adjoint_source)[g // 3].at[g % 3]
        to_right = to_left = None
        for z in range(Z):
            plane = planes[z]
            here_right = turn(plane, 16 * z + 12, 1)
            here_left = turn(plane, 16 * z + 4, 1)
            if z == 0:
                to_right, to_left = here_right, here_left
            else:
                chosen = lane >= 16 * z
                to_right = jnp.where(chosen, here_right, to_right)
                to_left = jnp.where(chosen, here_left, to_left)
        own_right[g] = to_right
        own_left[g] = to_left
        first[g] = jnp.where(rightward, to_right, to_left)
        second[g] = jnp.where(rightward, to_left, to_right)
        for pair in range(Z // 2):
            k = g * (Z // 2) + pair
            down = jnp.where(low, planes[2 * pair, 0:8], turn(planes[2 * pair + 1, 0:8], 4, 0))
            up = jnp.where(low, turn(planes[2 * pair + 1, 8:16], 4, 0), planes[2 * pair, 8:16])
            far[k] = jnp.where(upward, up, down)
            near[k] = jnp.where(upward, down, up)
    for copy in copies[5:]:
        copy.wait()
    first[GROUPS] = density[...]
    second[GROUPS] = density[...]
    for part in range(2):
        far[4 * GROUPS + part] = density[8 * part : 8 * part + 8]
        near[4 * GROUPS + part] = density[8 * part : 8 * part + 8]

    col, row = lax.axis_index("gx"), lax.axis_index("gy")
    row24 = rows_of(WRAP)
    tiles_y, tiles_x = design.shape

    def gain_at(first, tile_x):
        tile_y = jnp.clip(first, 0, tiles_y * TILE - 1) // TILE
        tile_x = jnp.clip(tile_x, 0, tiles_x - 1)
        return design[tile_y, tile_x].astype(jnp.float32) * contrast[material[tile_y, tile_x]]

    for k in range(3):
        tile_x = col + (0, 1, -1)[k]
        here = gain_at(row * ROWS, tile_x)
        up = gain_at(row * ROWS + ROWS, tile_x)
        down = gain_at(row * ROWS - HALO, tile_x)
        gains[k] = jnp.where(row24 < 16, here, jnp.where(row24 < 20, up, down))


def strip_kernel(own_right, own_left, first_got, second_got, strips, side, far, near):
    col = lax.axis_index("gx")
    rightward = col % 2 == 1
    upward = lax.axis_index("gy") % 2 == 1
    first, last = col == 0, col == lax.axis_size("gx") - 1
    lane = lanes_of(ROWS)
    within = lane % 16
    half = lane % 32 < 16
    low = rows_of(8) < 4

    def sides(g):
        from_right = jnp.where(rightward, first_got[g], second_got[g])
        from_left = jnp.where(rightward, second_got[g], first_got[g])
        return jnp.where(last, 0.0, from_right), jnp.where(first, 0.0, from_left)

    for g in range(GROUPS):
        from_right, from_left = sides(g)
        here_right = jnp.where(within >= HALO, from_right, own_left[g])
        here_left = jnp.where(within < 12, from_left, own_right[g])
        even = jnp.where(half, here_right, turn(here_left, 16, 1))
        odd = jnp.where(half, turn(here_right, -16, 1), here_left)
        strips[g, 0] = even
        strips[g, 1] = odd
        down = jnp.where(low, even[0:8], turn(odd[0:8], 4, 0))
        up = jnp.where(low, turn(odd[8:16], 4, 0), even[8:16])
        far[g] = jnp.where(upward, up, down)
        near[g] = jnp.where(upward, down, up)
    from_right, from_left = sides(GROUPS)
    beside = jnp.where(lane < 64, from_right, from_left)
    side[...] = beside
    for part in range(2):
        far[GROUPS + part] = beside[8 * part : 8 * part + 8]
        near[GROUPS + part] = beside[8 * part : 8 * part + 8]


def unpack(far, near, pick, second):
    if second:
        return turn(jnp.where(pick, near, far), 4, 0)
    return jnp.where(pick, far, near)


def main_kernel(
    gains, field, adjoint, source, adjoint_source, background, density,
    far, near, strips, side, strip_far, strip_near,
    field_out, adjoint_out, local_far, local_near,
    fields, sources, curls, rate, keep, strip_fields, strip_sources, strip_curls, strip_rate, strip_keep, wide,
):
    col, row = lax.axis_index("gx"), lax.axis_index("gy")
    cols, rows = lax.axis_size("gx"), lax.axis_size("gy")
    first_row, last_row = row == 0, row == rows - 1
    low = rows_of(8) < 4
    upward = row % 2 == 1
    pick = jnp.where(upward, rows_of(8), 7 - rows_of(8)) < 4
    lane24, row24 = lanes_of(WRAP), rows_of(WRAP)
    outside8 = (low & last_row) | (jnp.logical_not(low) & first_row)
    outside = ((row24 >= 16) & (row24 < 20) & last_row) | ((row24 >= 20) & first_row)
    j = lane24 % 32
    outside_strip = outside | ((j >= HALO) & (j < 16) & (col == cols - 1)) | ((j >= 16) & (j < 28) & (col == 0))
    gain_main, gain_right, gain_left = gains[0], gains[1], gains[2]

    wide[16:32, 0:LANES] = density[...]
    wide[16:32, LANES : 2 * LANES] = side[...]
    for part in range(2):
        k, rows8 = 4 * GROUPS + part, slice(8 * part, 8 * part + 8)
        wide[rows8, 0:LANES] = jnp.where(first_row, 0.0, jnp.where(upward, near[k], far[k]))
        rows8 = slice(32 + 8 * part, 40 + 8 * part)
        wide[rows8, 0:LANES] = jnp.where(last_row, 0.0, jnp.where(upward, far[k], near[k]))
        k, rows8 = GROUPS + part, slice(8 * part, 8 * part + 8)
        wide[rows8, LANES : 2 * LANES] = jnp.where(first_row, 0.0, jnp.where(upward, strip_near[k], strip_far[k]))
        rows8 = slice(32 + 8 * part, 40 + 8 * part)
        wide[rows8, LANES : 2 * LANES] = jnp.where(last_row, 0.0, jnp.where(upward, strip_far[k], strip_near[k]))
    filtered = cone(lambda a: wide[8 + a : 40 + a], 32)
    low2 = lax.broadcasted_iota(jnp.int32, (8, 2 * LANES), 0) < 4
    filtered = jnp.concatenate(
        [filtered[8:24], jnp.where(low2, filtered[24:32], filtered[0:8])], axis=0
    )
    design_main = gain_main * filtered[:, :LANES]
    beside = filtered[:, LANES:]
    block = filtered[:, :LANES]
    right_side = jnp.where(lane24 < HALO, turn(block, HALO, 1), turn(beside, HALO, 1))
    left_side = jnp.where(lane24 < 28, turn(beside, 28, 1), turn(block, 28, 1))
    quarter = jnp.where(lane24 < 16, right_side * gain_right, left_side * gain_left)
    quarter = jnp.where((lane24 < HALO) | (lane24 >= 28), turn_edges(right_side, left_side, lane24) * gain_main, quarter)
    quarter = jnp.where(lane24 < 32, quarter, 0.0)
    quarter = quarter + turn(quarter, 32, 1)
    design_strip = quarter + turn(quarter, 64, 1)

    def whole(inner, halo):
        return jnp.concatenate([inner, halo], axis=0)

    for z in range(Z):
        k = 48 + z // 2
        halo = unpack(far[k], near[k], pick, z % 2)
        step = 0.5 / (4.0 + 0.5 * (whole(background[z], halo) + design_main))
        step = jnp.where(outside, 0.0, step)
        rate[z] = step
        keep[z] = 0.5 + 4.0 * step
    for t in range(2):
        halo = unpack(strip_far[12], strip_near[12], pick, t)
        step = 0.5 / (4.0 + 0.5 * (whole(strips[12, t], halo) + design_strip))
        step = jnp.where(outside_strip, 0.0, step)
        strip_rate[t] = step
        strip_keep[t] = 0.5 + 4.0 * step

    starts = (field, adjoint, source, adjoint_source)
    for f in range(4):
        for c in range(3):
            g = 3 * f + c
            for z in range(Z):
                k = 4 * g + z // 2
                halo = unpack(far[k], near[k], pick, z % 2)
                if f < 2:
                    fields[f, c, z] = whole(starts[f][c, z], jnp.where(outside8, 0.0, halo))
                else:
                    sources[f - 2, c, z] = whole(starts[f][c, z], halo)
            for t in range(2):
                halo = unpack(strip_far[g], strip_near[g], pick, t)
                if f < 2:
                    strip_fields[f, c, t] = whole(strips[g, t], jnp.where(outside8, 0.0, halo))
                else:
                    strip_sources[f - 2, c, t] = whole(strips[g, t], halo)

    at_last, at_first = lane24 == LANES - 1, lane24 == 0

    def ahead_y(value):
        return turn(value, -1, 0)

    def behind_y(value):
        return turn(value, 1, 0)

    def ahead_x(value, strip, z):
        return jnp.where(at_last, turn(strip[z % 2], 123 - 32 * (z // 2), 1), turn(value, -1, 1))

    def behind_x(value, strip, z):
        return jnp.where(at_first, turn(strip[z % 2], -(32 * (z // 2) + 27), 1), turn(value, 1, 1))

    def sweep():
        for f in range(2):
            ex, ey, ez = ([strip_fields[f, c, t] for t in range(2)] for c in range(3))
            for t in range(2):
                if t == 0:
                    ex_z, ey_z = ex[1], ey[1]
                else:
                    ex_z = jnp.where(lane24 < 96, turn(ex[0], -32, 1), 0.0)
                    ey_z = jnp.where(lane24 < 96, turn(ey[0], -32, 1), 0.0)
                strip_curls[f, 0, t] = (ahead_y(ez[t]) - ez[t]) - (ey_z - ey[t])
                strip_curls[f, 1, t] = (ex_z - ex[t]) - (turn(ez[t], -1, 1) - ez[t])
                strip_curls[f, 2, t] = (turn(ey[t], -1, 1) - ey[t]) - (ahead_y(ex[t]) - ex[t])
            for z in range(Z):
                ex, ey, ez = (fields[f, c, z] for c in range(3))
                if z < Z - 1:
                    ex_z, ey_z = fields[f, 0, z + 1], fields[f, 1, z + 1]
                else:
                    ex_z = ey_z = jnp.zeros_like(ex)
                curls[f, 0, z] = (ahead_y(ez) - ez) - (ey_z - ey)
                curls[f, 1, z] = (ex_z - ex) - (ahead_x(ez, strip_fields.at[f, 2], z) - ez)
                curls[f, 2, z] = (ahead_x(ey, strip_fields.at[f, 1], z) - ey) - (ahead_y(ex) - ex)
        bottom = lane24 < 32
        for f in range(2):
            for t in range(2):
                ex, ey, ez = (strip_fields[f, c, t] for c in range(3))
                hx, hy, hz = (strip_curls[f, c, t] for c in range(3))
                if t == 1:
                    hx_z, hy_z = strip_curls[f, 0, 0], strip_curls[f, 1, 0]
                else:
                    hx_z = jnp.where(bottom, -ey, turn(strip_curls[f, 0, 1], 32, 1))
                    hy_z = jnp.where(bottom, ex, turn(strip_curls[f, 1, 1], 32, 1))
                curl_x = (hz - behind_y(hz)) - (hy - hy_z)
                curl_y = (hx - hx_z) - (hz - turn(hz, 1, 1))
                curl_z = (hy - turn(hy, 1, 1)) - (hx - behind_y(hx))
                step, kept = strip_rate[t], strip_keep[t]
                strip_fields[f, 0, t] = kept * ex + step * (strip_sources[f, 0, t] - curl_x)
                strip_fields[f, 1, t] = kept * ey + step * (strip_sources[f, 1, t] - curl_y)
                strip_fields[f, 2, t] = kept * ez + step * (strip_sources[f, 2, t] - curl_z)
            for z in range(Z):
                ex, ey, ez = (fields[f, c, z] for c in range(3))
                hx, hy, hz = (curls[f, c, z] for c in range(3))
                if z > 0:
                    hx_z, hy_z = curls[f, 0, z - 1], curls[f, 1, z - 1]
                else:
                    hx_z, hy_z = -ey, ex
                curl_x = (hz - behind_y(hz)) - (hy - hy_z)
                curl_y = (hx - hx_z) - (hz - behind_x(hz, strip_curls.at[f, 2], z))
                curl_z = (hy - behind_x(hy, strip_curls.at[f, 1], z)) - (hx - behind_y(hx))
                step, kept = rate[z], keep[z]
                fields[f, 0, z] = kept * ex + step * (sources[f, 0, z] - curl_x)
                fields[f, 1, z] = kept * ey + step * (sources[f, 1, z] - curl_y)
                fields[f, 2, z] = kept * ez + step * (sources[f, 2, z] - curl_z)
    for _ in range(ITERS):
        sweep()

    product = jnp.zeros((ROWS, LANES), jnp.float32)
    strip_product = jnp.zeros((ROWS, LANES), jnp.float32)
    for c in range(3):
        for z in range(Z):
            forward, backward = fields[0, c, z, 0:ROWS], fields[1, c, z, 0:ROWS]
            field_out[c, z] = forward
            adjoint_out[c, z] = backward
            product = product + forward * backward
        for t in range(2):
            strip_product = strip_product + strip_fields[0, c, t, 0:ROWS] * strip_fields[1, c, t, 0:ROWS]
    strip_product = strip_product + turn(strip_product, 64, 1)
    strip_product = strip_product + turn(strip_product, 32, 1)
    local = product * (-0.5 * gain_main[0:ROWS])
    lane = lanes_of(ROWS)
    local_side = jnp.where(
        lane < 64, turn(strip_product, -4, 1) * (-0.5 * gain_right[0:ROWS]),
        turn(strip_product, 100, 1) * (-0.5 * gain_left[0:ROWS]),
    )
    for out, value in ((slice(0, LANES), local), (slice(LANES, 2 * LANES), local_side)):
        local_far[:, out] = jnp.where(upward, value[8:16], value[0:8])
        local_near[:, out] = jnp.where(upward, value[0:8], value[8:16])


def turn_edges(right_side, left_side, lane):
    return jnp.where(lane < 16, right_side, left_side)


def gradient_kernel(own_far, own_near, far, near, gradient, wide):
    row = lax.axis_index("gy")
    upward = row % 2 == 1
    wide[0:8] = jnp.where(row == 0, 0.0, jnp.where(upward, near[...], far[...]))
    wide[8:16] = jnp.where(upward, own_near[...], own_far[...])
    wide[16:24] = jnp.where(upward, own_far[...], own_near[...])
    wide[24:32] = jnp.where(row == lax.axis_size("gy") - 1, 0.0, jnp.where(upward, far[...], near[...]))
    gradient[...] = cone(lambda a: wide[8 + a : 24 + a], ROWS)[:, :LANES]


def swaps(axis, start):
    size = lax.axis_size(axis)
    pairs = [(i, i + 1) for i in range(start, size - 1, 2)]
    return sorted(pairs + [(j, i) for i, j in pairs])


def swap_rows(far, near):
    return lax.ppermute(far, "gy", swaps("gy", 1)), lax.ppermute(near, "gy", swaps("gy", 0))


def shape(*dims):
    return jax.ShapeDtypeStruct(dims, jnp.float32)


def call(kernel, outs, space=VMEM, scratch=()):
    def run(*operands):
        return pl.pallas_call(
            kernel,
            out_shape=outs,
            in_specs=[pl.BlockSpec(memory_space=space)] * len(operands),
            out_specs=jax.tree.map(lambda _: pl.BlockSpec(memory_space=VMEM), outs),
            scratch_shapes=scratch,
            compiler_params=pltpu.CompilerParams(vmem_limit_bytes=LIMIT),
        )(*operands)

    return run


def room(*dims):
    return pltpu.VMEM(dims, jnp.float32)


def on_device(background, density, design_tiles, material_tiles, contrast, source, adjoint_source, field_start, adjoint_start):
    inner = (field_start, adjoint_start, source, adjoint_source, background, density)
    tiles = (design_tiles, material_tiles, contrast)
    edges, rows = shape(GROUPS + 1, ROWS, LANES), shape(4 * GROUPS + 2, 8, LANES)
    first, second, own_right, own_left, far, near, gains, *inner = call(
        pack_kernel,
        [edges, edges, edges, edges, rows, rows, shape(3, WRAP, LANES)] + [shape(*a.shape) for a in inner],
        space=pltpu.HBM,
        scratch=[pltpu.SMEM(a.shape, a.dtype) for a in tiles] + [pltpu.SemaphoreType.DMA((9,))],
    )(*[pltpu.with_memory_space_constraint(a, pltpu.HBM) for a in (*tiles, *inner)])
    first_got = lax.ppermute(first, "gx", swaps("gx", 1))
    second_got = lax.ppermute(second, "gx", swaps("gx", 0))
    far_got, near_got = swap_rows(far, near)
    corner = shape(GROUPS + 2, 8, LANES)
    strips, side, strip_far, strip_near = call(
        strip_kernel, [shape(GROUPS, 2, ROWS, LANES), shape(ROWS, LANES), corner, corner]
    )(own_right, own_left, first_got, second_got)
    strip_far_got, strip_near_got = swap_rows(strip_far, strip_near)
    block, part = shape(3, Z, ROWS, LANES), shape(8, 2 * LANES)
    planes, sheets = (2, 3, Z, WRAP, LANES), (2, 3, 2, WRAP, LANES)
    field, adjoint, local_far, local_near = call(
        main_kernel,
        [block, block, part, part],
        scratch=[
            room(*planes), room(*planes), room(*planes), room(Z, WRAP, LANES), room(Z, WRAP, LANES),
            room(*sheets), room(*sheets), room(*sheets), room(2, WRAP, LANES), room(2, WRAP, LANES),
            room(48, 2 * LANES),
        ],
    )(gains, *inner, far_got, near_got, strips, side, strip_far_got, strip_near_got)
    local_far_got, local_near_got = swap_rows(local_far, local_near)
    gradient = call(gradient_kernel, shape(ROWS, LANES), scratch=[room(32, 2 * LANES)])(
        local_far, local_near, local_far_got, local_near_got
    )
    return (field, adjoint, gradient)


def solution(mesh):
    in_specs = (
        P(None, "gy", "gx"),
        P("gy", "gx"),
        P(),
        P(),
        P(),
        P(None, None, "gy", "gx"),
        P(None, None, "gy", "gx"),
        P(None, None, "gy", "gx"),
        P(None, None, "gy", "gx"),
    )
    out_specs = (P(None, None, "gy", "gx"), P(None, None, "gy", "gx"), P("gy", "gx"))
    return jax.shard_map(on_device, mesh=mesh, in_specs=in_specs, out_specs=out_specs, check_vma=False)
```

```python
import functools
import math

import jax
import jax.numpy as jnp
from jax import lax
from jax.experimental import pallas as pl
from jax.experimental.pallas import tpu as pltpu
from jax.sharding import PartitionSpec as P

ITERS = 4
RADIUS = 8
TILE = 128
Z = 8
ROWS = 16
LANES = 128
HALO = 4
WRAP = ROWS + 8
GROUPS = 13
PACKED = 4 * GROUPS + 2
VMEM = pltpu.VMEM
LIMIT = 48 * 1024 * 1024


def cone_weight(row_shift, col_shift):
    return max(0.0, RADIUS + 1 - math.sqrt(row_shift * row_shift + col_shift * col_shift))


def cone_total():
    span = range(-RADIUS, RADIUS + 1)
    return math.fsum(cone_weight(a, b) for a in span for b in span)


def lanes_of(rows):
    return lax.broadcasted_iota(jnp.int32, (rows, LANES), 1)


def rows_of(rows):
    return lax.broadcasted_iota(jnp.int32, (rows, LANES), 0)


def turn(value, shift, axis):
    size = value.shape[axis]
    return pltpu.roll(value, shift % size, axis)


def cone(rows_at, rows):
    total = cone_total()
    paired = [rows_at(0)]
    for a in range(1, RADIUS + 1):
        paired.append(rows_at(a) + rows_at(-a))
    result = None
    for b in range(RADIUS + 1):
        column = None
        for a in range(RADIUS + 1):
            weight = cone_weight(a, b)
            if weight > 0.0:
                term = paired[a] * (weight / total)
                column = term if column is None else column + term
        if b > 0:
            column = turn(column, b, 1) + turn(column, -b, 1)
        result = column if result is None else result + column
    return result


def pack_kernel(
    design_in, material_in, contrast_in, field_in, adjoint_in, source_in, adjoint_source_in, background_in, density_in,
    first, second, own_right, own_left, far, near, gains, field, adjoint, source, adjoint_source, background, density,
    design, material, contrast, done,
):
    arrays = (
        (field_in, field), (adjoint_in, adjoint), (source_in, source), (adjoint_source_in, adjoint_source),
        (background_in, background), (density_in, density),
        (design_in, design), (material_in, material), (contrast_in, contrast),
    )
    copies = [pltpu.make_async_copy(here, there, done.at[i]) for i, (here, there) in enumerate(arrays)]
    for copy in copies:
        copy.start()
    lane = lanes_of(ROWS)
    rightward = lax.axis_index("gx") % 2 == 1
    upward = lax.axis_index("gy") % 2 == 1
    low = rows_of(8) < 4
    for g in range(GROUPS):
        if g % 3 == 0:
            copies[g // 3].wait()
        planes = background if g == 12 else (field, adjoint, source, adjoint_source)[g // 3].at[g % 3]
        to_right = to_left = None
        for z in range(Z):
            plane = planes[z]
            here_right = turn(plane, 16 * z + 12, 1)
            here_left = turn(plane, 16 * z + 4, 1)
            if z == 0:
                to_right, to_left = here_right, here_left
            else:
                chosen = lane >= 16 * z
                to_right = jnp.where(chosen, here_right, to_right)
                to_left = jnp.where(chosen, here_left, to_left)
        own_right[g] = to_right
        own_left[g] = to_left
        first[g] = jnp.where(rightward, to_right, to_left)
        second[g] = jnp.where(rightward, to_left, to_right)
        for pair in range(Z // 2):
            k = g * (Z // 2) + pair
            down = jnp.where(low, planes[2 * pair, 0:8], turn(planes[2 * pair + 1, 0:8], 4, 0))
            up = jnp.where(low, turn(planes[2 * pair + 1, 8:16], 4, 0), planes[2 * pair, 8:16])
            far[k] = jnp.where(upward, up, down)
            near[k] = jnp.where(upward, down, up)
    for copy in copies[5:]:
        copy.wait()
    first[GROUPS] = density[...]
    second[GROUPS] = density[...]
    for part in range(2):
        far[4 * GROUPS + part] = density[8 * part : 8 * part + 8]
        near[4 * GROUPS + part] = density[8 * part : 8 * part + 8]

    col, row = lax.axis_index("gx"), lax.axis_index("gy")
    row24 = rows_of(WRAP)
    tiles_y, tiles_x = design.shape

    def gain_at(first, tile_x):
        tile_y = jnp.clip(first, 0, tiles_y * TILE - 1) // TILE
        tile_x = jnp.clip(tile_x, 0, tiles_x - 1)
        return design[tile_y, tile_x].astype(jnp.float32) * contrast[material[tile_y, tile_x]]

    for k in range(3):
        tile_x = col + (0, 1, -1)[k]
        here = gain_at(row * ROWS, tile_x)
        up = gain_at(row * ROWS + ROWS, tile_x)
        down = gain_at(row * ROWS - HALO, tile_x)
        gains[k] = jnp.where(row24 < 16, here, jnp.where(row24 < 20, up, down))


def strip_kernel(own_right, own_left, far_rows, near_rows, first_got, second_got, strips, side, far, near):
    col = lax.axis_index("gx")
    rightward = col % 2 == 1
    upward = lax.axis_index("gy") % 2 == 1
    first, last = col == 0, col == lax.axis_size("gx") - 1
    lane = lanes_of(ROWS)
    within = lane % 16
    half = lane % 32 < 16
    low = rows_of(8) < 4

    far[0:PACKED] = far_rows[...]
    near[0:PACKED] = near_rows[...]

    def sides(g):
        from_right = jnp.where(rightward, first_got[g], second_got[g])
        from_left = jnp.where(rightward, second_got[g], first_got[g])
        return jnp.where(last, 0.0, from_right), jnp.where(first, 0.0, from_left)

    for g in range(GROUPS):
        from_right, from_left = sides(g)
        here_right = jnp.where(within >= HALO, from_right, own_left[g])
        here_left = jnp.where(within < 12, from_left, own_right[g])
        even = jnp.where(half, here_right, turn(here_left, 16, 1))
        odd = jnp.where(half, turn(here_right, -16, 1), here_left)
        strips[g, 0] = even
        strips[g, 1] = odd
        down = jnp.where(low, even[0:8], turn(odd[0:8], 4, 0))
        up = jnp.where(low, turn(odd[8:16], 4, 0), even[8:16])
        far[PACKED + g] = jnp.where(upward, up, down)
        near[PACKED + g] = jnp.where(upward, down, up)
    from_right, from_left = sides(GROUPS)
    beside = jnp.where(lane < 64, from_right, from_left)
    side[...] = beside
    for part in range(2):
        far[PACKED + GROUPS + part] = beside[8 * part : 8 * part + 8]
        near[PACKED + GROUPS + part] = beside[8 * part : 8 * part + 8]


def unpack(far, near, pick, second):
    if second:
        return turn(jnp.where(pick, near, far), 4, 0)
    return jnp.where(pick, far, near)


def main_kernel(
    gains, field, adjoint, source, adjoint_source, background, density,
    far, near, strips, side,
    field_out, adjoint_out, local_far, local_near,
    fields, sources, curls, rate, keep, strip_fields, strip_sources, strip_curls, strip_rate, strip_keep, wide,
):
    col, row = lax.axis_index("gx"), lax.axis_index("gy")
    cols, rows = lax.axis_size("gx"), lax.axis_size("gy")
    first_row, last_row = row == 0, row == rows - 1
    low = rows_of(8) < 4
    upward = row % 2 == 1
    pick = jnp.where(upward, rows_of(8), 7 - rows_of(8)) < 4
    lane24, row24 = lanes_of(WRAP), rows_of(WRAP)
    outside8 = (low & last_row) | (jnp.logical_not(low) & first_row)
    outside = ((row24 >= 16) & (row24 < 20) & last_row) | ((row24 >= 20) & first_row)
    j = lane24 % 32
    outside_strip = outside | ((j >= HALO) & (j < 16) & (col == cols - 1)) | ((j >= 16) & (j < 28) & (col == 0))
    gain_main, gain_right, gain_left = gains[0], gains[1], gains[2]

    wide[16:32, 0:LANES] = density[...]
    wide[16:32, LANES : 2 * LANES] = side[...]
    for part in range(2):
        k, rows8 = 4 * GROUPS + part, slice(8 * part, 8 * part + 8)
        wide[rows8, 0:LANES] = jnp.where(first_row, 0.0, jnp.where(upward, near[k], far[k]))
        rows8 = slice(32 + 8 * part, 40 + 8 * part)
        wide[rows8, 0:LANES] = jnp.where(last_row, 0.0, jnp.where(upward, far[k], near[k]))
        k, rows8 = PACKED + GROUPS + part, slice(8 * part, 8 * part + 8)
        wide[rows8, LANES : 2 * LANES] = jnp.where(first_row, 0.0, jnp.where(upward, near[k], far[k]))
        rows8 = slice(32 + 8 * part, 40 + 8 * part)
        wide[rows8, LANES : 2 * LANES] = jnp.where(last_row, 0.0, jnp.where(upward, far[k], near[k]))
    filtered = cone(lambda a: wide[8 + a : 40 + a], 32)
    low2 = lax.broadcasted_iota(jnp.int32, (8, 2 * LANES), 0) < 4
    filtered = jnp.concatenate(
        [filtered[8:24], jnp.where(low2, filtered[24:32], filtered[0:8])], axis=0
    )
    design_main = gain_main * filtered[:, :LANES]
    beside = filtered[:, LANES:]
    block = filtered[:, :LANES]
    right_side = jnp.where(lane24 < HALO, turn(block, HALO, 1), turn(beside, HALO, 1))
    left_side = jnp.where(lane24 < 28, turn(beside, 28, 1), turn(block, 28, 1))
    quarter = jnp.where(lane24 < 16, right_side * gain_right, left_side * gain_left)
    quarter = jnp.where((lane24 < HALO) | (lane24 >= 28), turn_edges(right_side, left_side, lane24) * gain_main, quarter)
    quarter = jnp.where(lane24 < 32, quarter, 0.0)
    quarter = quarter + turn(quarter, 32, 1)
    design_strip = quarter + turn(quarter, 64, 1)

    def whole(inner, halo):
        return jnp.concatenate([inner, halo], axis=0)

    for z in range(Z):
        k = 48 + z // 2
        halo = unpack(far[k], near[k], pick, z % 2)
        step = 0.5 / (4.0 + 0.5 * (whole(background[z], halo) + design_main))
        step = jnp.where(outside, 0.0, step)
        rate[z] = step
        keep[z] = 0.5 + 4.0 * step
    for t in range(2):
        halo = unpack(far[PACKED + 12], near[PACKED + 12], pick, t)
        step = 0.5 / (4.0 + 0.5 * (whole(strips[12, t], halo) + design_strip))
        step = jnp.where(outside_strip, 0.0, step)
        strip_rate[t] = step
        strip_keep[t] = 0.5 + 4.0 * step

    starts = (field, adjoint, source, adjoint_source)
    for f in range(4):
        for c in range(3):
            g = 3 * f + c
            for z in range(Z):
                k = 4 * g + z // 2
                halo = unpack(far[k], near[k], pick, z % 2)
                if f < 2:
                    fields[f, c, z] = whole(starts[f][c, z], jnp.where(outside8, 0.0, halo))
                else:
                    sources[f - 2, c, z] = whole(starts[f][c, z], halo)
            for t in range(2):
                halo = unpack(far[PACKED + g], near[PACKED + g], pick, t)
                if f < 2:
                    strip_fields[f, c, t] = whole(strips[g, t], jnp.where(outside8, 0.0, halo))
                else:
                    strip_sources[f - 2, c, t] = whole(strips[g, t], halo)

    at_last, at_first = lane24 == LANES - 1, lane24 == 0

    def ahead_y(value):
        return turn(value, -1, 0)

    def behind_y(value):
        return turn(value, 1, 0)

    def ahead_x(value, strip, z):
        return jnp.where(at_last, turn(strip[z % 2], 123 - 32 * (z // 2), 1), turn(value, -1, 1))

    def behind_x(value, strip, z):
        return jnp.where(at_first, turn(strip[z % 2], -(32 * (z // 2) + 27), 1), turn(value, 1, 1))

    def sweep():
        for f in range(2):
            ex, ey, ez = ([strip_fields[f, c, t] for t in range(2)] for c in range(3))
            for t in range(2):
                if t == 0:
                    ex_z, ey_z = ex[1], ey[1]
                else:
                    ex_z = jnp.where(lane24 < 96, turn(ex[0], -32, 1), 0.0)
                    ey_z = jnp.where(lane24 < 96, turn(ey[0], -32, 1), 0.0)
                strip_curls[f, 0, t] = (ahead_y(ez[t]) - ez[t]) - (ey_z - ey[t])
                strip_curls[f, 1, t] = (ex_z - ex[t]) - (turn(ez[t], -1, 1) - ez[t])
                strip_curls[f, 2, t] = (turn(ey[t], -1, 1) - ey[t]) - (ahead_y(ex[t]) - ex[t])
            for z in range(Z):
                ex, ey, ez = (fields[f, c, z] for c in range(3))
                if z < Z - 1:
                    ex_z, ey_z = fields[f, 0, z + 1], fields[f, 1, z + 1]
                else:
                    ex_z = ey_z = jnp.zeros_like(ex)
                curls[f, 0, z] = (ahead_y(ez) - ez) - (ey_z - ey)
                curls[f, 1, z] = (ex_z - ex) - (ahead_x(ez, strip_fields.at[f, 2], z) - ez)
                curls[f, 2, z] = (ahead_x(ey, strip_fields.at[f, 1], z) - ey) - (ahead_y(ex) - ex)
        bottom = lane24 < 32
        for f in range(2):
            for t in range(2):
                ex, ey, ez = (strip_fields[f, c, t] for c in range(3))
                hx, hy, hz = (strip_curls[f, c, t] for c in range(3))
                if t == 1:
                    hx_z, hy_z = strip_curls[f, 0, 0], strip_curls[f, 1, 0]
                else:
                    hx_z = jnp.where(bottom, -ey, turn(strip_curls[f, 0, 1], 32, 1))
                    hy_z = jnp.where(bottom, ex, turn(strip_curls[f, 1, 1], 32, 1))
                curl_x = (hz - behind_y(hz)) - (hy - hy_z)
                curl_y = (hx - hx_z) - (hz - turn(hz, 1, 1))
                curl_z = (hy - turn(hy, 1, 1)) - (hx - behind_y(hx))
                step, kept = strip_rate[t], strip_keep[t]
                strip_fields[f, 0, t] = kept * ex + step * (strip_sources[f, 0, t] - curl_x)
                strip_fields[f, 1, t] = kept * ey + step * (strip_sources[f, 1, t] - curl_y)
                strip_fields[f, 2, t] = kept * ez + step * (strip_sources[f, 2, t] - curl_z)
            for z in range(Z):
                ex, ey, ez = (fields[f, c, z] for c in range(3))
                hx, hy, hz = (curls[f, c, z] for c in range(3))
                if z > 0:
                    hx_z, hy_z = curls[f, 0, z - 1], curls[f, 1, z - 1]
                else:
                    hx_z, hy_z = -ey, ex
                curl_x = (hz - behind_y(hz)) - (hy - hy_z)
                curl_y = (hx - hx_z) - (hz - behind_x(hz, strip_curls.at[f, 2], z))
                curl_z = (hy - behind_x(hy, strip_curls.at[f, 1], z)) - (hx - behind_y(hx))
                step, kept = rate[z], keep[z]
                fields[f, 0, z] = kept * ex + step * (sources[f, 0, z] - curl_x)
                fields[f, 1, z] = kept * ey + step * (sources[f, 1, z] - curl_y)
                fields[f, 2, z] = kept * ez + step * (sources[f, 2, z] - curl_z)
    for _ in range(ITERS):
        sweep()

    product = jnp.zeros((ROWS, LANES), jnp.float32)
    strip_product = jnp.zeros((ROWS, LANES), jnp.float32)
    for c in range(3):
        for z in range(Z):
            forward, backward = fields[0, c, z, 0:ROWS], fields[1, c, z, 0:ROWS]
            field_out[c, z] = forward
            adjoint_out[c, z] = backward
            product = product + forward * backward
        for t in range(2):
            strip_product = strip_product + strip_fields[0, c, t, 0:ROWS] * strip_fields[1, c, t, 0:ROWS]
    strip_product = strip_product + turn(strip_product, 64, 1)
    strip_product = strip_product + turn(strip_product, 32, 1)
    local = product * (-0.5 * gain_main[0:ROWS])
    lane = lanes_of(ROWS)
    local_side = jnp.where(
        lane < 64, turn(strip_product, -4, 1) * (-0.5 * gain_right[0:ROWS]),
        turn(strip_product, 100, 1) * (-0.5 * gain_left[0:ROWS]),
    )
    for out, value in ((slice(0, LANES), local), (slice(LANES, 2 * LANES), local_side)):
        local_far[:, out] = jnp.where(upward, value[8:16], value[0:8])
        local_near[:, out] = jnp.where(upward, value[0:8], value[8:16])


def turn_edges(right_side, left_side, lane):
    return jnp.where(lane < 16, right_side, left_side)


def gradient_kernel(own_far, own_near, far, near, gradient, wide):
    row = lax.axis_index("gy")
    upward = row % 2 == 1
    wide[0:8] = jnp.where(row == 0, 0.0, jnp.where(upward, near[...], far[...]))
    wide[8:16] = jnp.where(upward, own_near[...], own_far[...])
    wide[16:24] = jnp.where(upward, own_far[...], own_near[...])
    wide[24:32] = jnp.where(row == lax.axis_size("gy") - 1, 0.0, jnp.where(upward, far[...], near[...]))
    gradient[...] = cone(lambda a: wide[8 + a : 24 + a], ROWS)[:, :LANES]


def swaps(axis, start):
    size = lax.axis_size(axis)
    pairs = [(i, i + 1) for i in range(start, size - 1, 2)]
    return sorted(pairs + [(j, i) for i, j in pairs])


def swap_rows(far, near):
    return lax.ppermute(far, "gy", swaps("gy", 1)), lax.ppermute(near, "gy", swaps("gy", 0))


def shape(*dims):
    return jax.ShapeDtypeStruct(dims, jnp.float32)


def call(kernel, outs, space=VMEM, scratch=()):
    def run(*operands):
        return pl.pallas_call(
            kernel,
            out_shape=outs,
            in_specs=[pl.BlockSpec(memory_space=space)] * len(operands),
            out_specs=jax.tree.map(lambda _: pl.BlockSpec(memory_space=VMEM), outs),
            scratch_shapes=scratch,
            compiler_params=pltpu.CompilerParams(vmem_limit_bytes=LIMIT),
        )(*operands)

    return run


def room(*dims):
    return pltpu.VMEM(dims, jnp.float32)


def on_device(background, density, design_tiles, material_tiles, contrast, source, adjoint_source, field_start, adjoint_start):
    inner = (field_start, adjoint_start, source, adjoint_source, background, density)
    tiles = (design_tiles, material_tiles, contrast)
    edges, rows, packed = shape(GROUPS + 1, ROWS, LANES), shape(PACKED, 8, LANES), shape(PACKED + GROUPS + 2, 8, LANES)
    first, second, own_right, own_left, far, near, gains, *inner = call(
        pack_kernel,
        [edges, edges, edges, edges, rows, rows, shape(3, WRAP, LANES)] + [shape(*a.shape) for a in inner],
        space=pltpu.HBM,
        scratch=[pltpu.SMEM(a.shape, a.dtype) for a in tiles] + [pltpu.SemaphoreType.DMA((9,))],
    )(*[pltpu.with_memory_space_constraint(a, pltpu.HBM) for a in (*tiles, *inner)])
    first_got = lax.ppermute(first, "gx", swaps("gx", 1))
    second_got = lax.ppermute(second, "gx", swaps("gx", 0))
    strips, side, far, near = call(strip_kernel, [shape(GROUPS, 2, ROWS, LANES), shape(ROWS, LANES), packed, packed])(
        own_right, own_left, far, near, first_got, second_got
    )
    far_got, near_got = swap_rows(far, near)
    block, part = shape(3, Z, ROWS, LANES), shape(8, 2 * LANES)
    planes, sheets = (2, 3, Z, WRAP, LANES), (2, 3, 2, WRAP, LANES)
    field, adjoint, local_far, local_near = call(
        main_kernel,
        [block, block, part, part],
        scratch=[
            room(*planes), room(*planes), room(*planes), room(Z, WRAP, LANES), room(Z, WRAP, LANES),
            room(*sheets), room(*sheets), room(*sheets), room(2, WRAP, LANES), room(2, WRAP, LANES),
            room(48, 2 * LANES),
        ],
    )(gains, *inner, far_got, near_got, strips, side)
    local_far_got, local_near_got = swap_rows(local_far, local_near)
    gradient = call(gradient_kernel, shape(ROWS, LANES), scratch=[room(32, 2 * LANES)])(
        local_far, local_near, local_far_got, local_near_got
    )
    return (field, adjoint, gradient)


def solution(mesh):
    in_specs = (
        P(None, "gy", "gx"),
        P("gy", "gx"),
        P(),
        P(),
        P(),
        P(None, None, "gy", "gx"),
        P(None, None, "gy", "gx"),
        P(None, None, "gy", "gx"),
        P(None, None, "gy", "gx"),
    )
    out_specs = (P(None, None, "gy", "gx"), P(None, None, "gy", "gx"), P("gy", "gx"))
    return jax.shard_map(on_device, mesh=mesh, in_specs=in_specs, out_specs=out_specs, check_vma=False)
```

```python
import functools
import math

import jax
import jax.numpy as jnp
from jax import lax
from jax.experimental import pallas as pl
from jax.experimental.pallas import tpu as pltpu
from jax.sharding import PartitionSpec as P

ITERS = 4
RADIUS = 8
TILE = 128
Z = 8
ROWS = 16
LANES = 128
HALO = 4
WRAP = ROWS + 8
GROUPS = 13
PACKED = 4 * GROUPS + 2
VMEM = pltpu.VMEM
LIMIT = 48 * 1024 * 1024


def cone_weight(row_shift, col_shift):
    return max(0.0, RADIUS + 1 - math.sqrt(row_shift * row_shift + col_shift * col_shift))


def cone_total():
    span = range(-RADIUS, RADIUS + 1)
    return math.fsum(cone_weight(a, b) for a in span for b in span)


def lanes_of(rows):
    return lax.broadcasted_iota(jnp.int32, (rows, LANES), 1)


def rows_of(rows):
    return lax.broadcasted_iota(jnp.int32, (rows, LANES), 0)


def turn(value, shift, axis):
    size = value.shape[axis]
    return pltpu.roll(value, shift % size, axis)


def cone(rows_at, rows):
    total = cone_total()
    paired = [rows_at(0)]
    for a in range(1, RADIUS + 1):
        paired.append(rows_at(a) + rows_at(-a))
    result = None
    for b in range(RADIUS + 1):
        column = None
        for a in range(RADIUS + 1):
            weight = cone_weight(a, b)
            if weight > 0.0:
                term = paired[a] * (weight / total)
                column = term if column is None else column + term
        if b > 0:
            column = turn(column, b, 1) + turn(column, -b, 1)
        result = column if result is None else result + column
    return result


def pack_kernel(
    design_in, material_in, contrast_in, field_in, adjoint_in, source_in, adjoint_source_in, background_in, density_in,
    first, second, own_right, own_left, far, near, gains, field, adjoint, source, adjoint_source, background, density,
    design, material, contrast, done,
):
    arrays = (
        (field_in, field), (adjoint_in, adjoint), (source_in, source), (adjoint_source_in, adjoint_source),
        (background_in, background), (density_in, density),
        (design_in, design), (material_in, material), (contrast_in, contrast),
    )
    copies = [pltpu.make_async_copy(here, there, done.at[i]) for i, (here, there) in enumerate(arrays)]
    for copy in copies:
        copy.start()
    lane = lanes_of(ROWS)
    rightward = lax.axis_index("gx") % 2 == 1
    upward = lax.axis_index("gy") % 2 == 1
    low = rows_of(8) < 4
    for g in range(GROUPS):
        if g % 3 == 0:
            copies[g // 3].wait()
        planes = background if g == 12 else (field, adjoint, source, adjoint_source)[g // 3].at[g % 3]
        windows = []
        for t in range(2):
            window = None
            for q in range(Z // 2):
                here = turn(planes[2 * q + t], 32 * q + 12, 1)
                window = here if q == 0 else jnp.where(lane >= 32 * q, here, window)
            windows.append(window)
        half = lane % 32 < 16
        to_right = jnp.where(half, windows[0], turn(windows[1], 16, 1))
        to_left = jnp.where(half, turn(windows[0], -8, 1), turn(windows[1], 8, 1))
        own_right[g] = to_right
        own_left[g] = to_left
        first[g] = jnp.where(rightward, to_right, to_left)
        second[g] = jnp.where(rightward, to_left, to_right)
        for pair in range(Z // 2):
            k = g * (Z // 2) + pair
            down = jnp.where(low, planes[2 * pair, 0:8], turn(planes[2 * pair + 1, 0:8], 4, 0))
            up = jnp.where(low, turn(planes[2 * pair + 1, 8:16], 4, 0), planes[2 * pair, 8:16])
            far[k] = jnp.where(upward, up, down)
            near[k] = jnp.where(upward, down, up)
    for copy in copies[5:]:
        copy.wait()
    first[GROUPS] = density[...]
    second[GROUPS] = density[...]
    for part in range(2):
        far[4 * GROUPS + part] = density[8 * part : 8 * part + 8]
        near[4 * GROUPS + part] = density[8 * part : 8 * part + 8]

    col, row = lax.axis_index("gx"), lax.axis_index("gy")
    row24 = rows_of(WRAP)
    tiles_y, tiles_x = design.shape

    def gain_at(first, tile_x):
        tile_y = jnp.clip(first, 0, tiles_y * TILE - 1) // TILE
        tile_x = jnp.clip(tile_x, 0, tiles_x - 1)
        return design[tile_y, tile_x].astype(jnp.float32) * contrast[material[tile_y, tile_x]]

    for k in range(3):
        tile_x = col + (0, 1, -1)[k]
        here = gain_at(row * ROWS, tile_x)
        up = gain_at(row * ROWS + ROWS, tile_x)
        down = gain_at(row * ROWS - HALO, tile_x)
        gains[k] = jnp.where(row24 < 16, here, jnp.where(row24 < 20, up, down))


def strip_kernel(own_right, own_left, far_rows, near_rows, first_got, second_got, strips, side, far, near):
    col = lax.axis_index("gx")
    rightward = col % 2 == 1
    upward = lax.axis_index("gy") % 2 == 1
    first, last = col == 0, col == lax.axis_size("gx") - 1
    lane = lanes_of(ROWS)
    within = lane % 16
    half = lane % 32 < 16
    low = rows_of(8) < 4

    far[0:PACKED] = far_rows[...]
    near[0:PACKED] = near_rows[...]

    def sides(g):
        from_right = jnp.where(rightward, first_got[g], second_got[g])
        from_left = jnp.where(rightward, second_got[g], first_got[g])
        return jnp.where(last, 0.0, from_right), jnp.where(first, 0.0, from_left)

    for g in range(GROUPS):
        from_right, from_left = sides(g)
        here_right = jnp.where(within >= HALO, from_right, own_left[g])
        here_left = jnp.where(within < 12, from_left, own_right[g])
        even = jnp.where(half, here_right, turn(here_left, 16, 1))
        odd = jnp.where(half, turn(here_right, -16, 1), here_left)
        strips[g, 0] = even
        strips[g, 1] = odd
        down = jnp.where(low, even[0:8], turn(odd[0:8], 4, 0))
        up = jnp.where(low, turn(odd[8:16], 4, 0), even[8:16])
        far[PACKED + g] = jnp.where(upward, up, down)
        near[PACKED + g] = jnp.where(upward, down, up)
    from_right, from_left = sides(GROUPS)
    beside = jnp.where(lane < 64, from_right, from_left)
    side[...] = beside
    for part in range(2):
        far[PACKED + GROUPS + part] = beside[8 * part : 8 * part + 8]
        near[PACKED + GROUPS + part] = beside[8 * part : 8 * part + 8]


def unpack(far, near, pick, second):
    if second:
        return turn(jnp.where(pick, near, far), 4, 0)
    return jnp.where(pick, far, near)


def main_kernel(
    gains, field, adjoint, source, adjoint_source, background, density,
    far, near, strips, side,
    fields, local_far, local_near,
    sources, curls, rate, keep, strip_fields, strip_sources, strip_curls, strip_rate, strip_keep, wide,
):
    col, row = lax.axis_index("gx"), lax.axis_index("gy")
    cols, rows = lax.axis_size("gx"), lax.axis_size("gy")
    first_row, last_row = row == 0, row == rows - 1
    low = rows_of(8) < 4
    upward = row % 2 == 1
    pick = jnp.where(upward, rows_of(8), 7 - rows_of(8)) < 4
    lane24, row24 = lanes_of(WRAP), rows_of(WRAP)
    outside8 = (low & last_row) | (jnp.logical_not(low) & first_row)
    outside = ((row24 >= 16) & (row24 < 20) & last_row) | ((row24 >= 20) & first_row)
    j = lane24 % 32
    outside_strip = outside | ((j >= HALO) & (j < 16) & (col == cols - 1)) | ((j >= 16) & (j < 28) & (col == 0))
    gain_main, gain_right, gain_left = gains[0], gains[1], gains[2]

    wide[16:32, 0:LANES] = density[...]
    wide[16:32, LANES : 2 * LANES] = side[...]
    for part in range(2):
        k, rows8 = 4 * GROUPS + part, slice(8 * part, 8 * part + 8)
        wide[rows8, 0:LANES] = jnp.where(first_row, 0.0, jnp.where(upward, near[k], far[k]))
        rows8 = slice(32 + 8 * part, 40 + 8 * part)
        wide[rows8, 0:LANES] = jnp.where(last_row, 0.0, jnp.where(upward, far[k], near[k]))
        k, rows8 = PACKED + GROUPS + part, slice(8 * part, 8 * part + 8)
        wide[rows8, LANES : 2 * LANES] = jnp.where(first_row, 0.0, jnp.where(upward, near[k], far[k]))
        rows8 = slice(32 + 8 * part, 40 + 8 * part)
        wide[rows8, LANES : 2 * LANES] = jnp.where(last_row, 0.0, jnp.where(upward, far[k], near[k]))
    filtered = cone(lambda a: wide[8 + a : 40 + a], 32)
    low2 = lax.broadcasted_iota(jnp.int32, (8, 2 * LANES), 0) < 4
    filtered = jnp.concatenate(
        [filtered[8:24], jnp.where(low2, filtered[24:32], filtered[0:8])], axis=0
    )
    design_main = gain_main * filtered[:, :LANES]
    beside = filtered[:, LANES:]
    block = filtered[:, :LANES]
    right_side = jnp.where(lane24 < HALO, turn(block, HALO, 1), turn(beside, HALO, 1))
    left_side = jnp.where(lane24 < 28, turn(beside, 28, 1), turn(block, 28, 1))
    quarter = jnp.where(lane24 < 16, right_side * gain_right, left_side * gain_left)
    quarter = jnp.where((lane24 < HALO) | (lane24 >= 28), turn_edges(right_side, left_side, lane24) * gain_main, quarter)
    quarter = jnp.where(lane24 < 32, quarter, 0.0)
    quarter = quarter + turn(quarter, 32, 1)
    design_strip = quarter + turn(quarter, 64, 1)

    def whole(inner, halo):
        return jnp.concatenate([inner, halo], axis=0)

    for z in range(Z):
        k = 48 + z // 2
        halo = unpack(far[k], near[k], pick, z % 2)
        step = 0.5 / (4.0 + 0.5 * (whole(background[z], halo) + design_main))
        step = jnp.where(outside, 0.0, step)
        rate[z] = step
        keep[z] = 0.5 + 4.0 * step
    for t in range(2):
        halo = unpack(far[PACKED + 12], near[PACKED + 12], pick, t)
        step = 0.5 / (4.0 + 0.5 * (whole(strips[12, t], halo) + design_strip))
        step = jnp.where(outside_strip, 0.0, step)
        strip_rate[t] = step
        strip_keep[t] = 0.5 + 4.0 * step

    starts = (field, adjoint, source, adjoint_source)
    for f in range(4):
        for c in range(3):
            g = 3 * f + c
            for z in range(Z):
                k = 4 * g + z // 2
                halo = unpack(far[k], near[k], pick, z % 2)
                if f < 2:
                    fields[f, c, z] = whole(starts[f][c, z], jnp.where(outside8, 0.0, halo))
                else:
                    sources[f - 2, c, z] = whole(starts[f][c, z], halo)
            for t in range(2):
                halo = unpack(far[PACKED + g], near[PACKED + g], pick, t)
                if f < 2:
                    strip_fields[f, c, t] = whole(strips[g, t], jnp.where(outside8, 0.0, halo))
                else:
                    strip_sources[f - 2, c, t] = whole(strips[g, t], halo)

    at_last, at_first = lane24 == LANES - 1, lane24 == 0

    def ahead_y(value):
        return turn(value, -1, 0)

    def behind_y(value):
        return turn(value, 1, 0)

    def ahead_x(value, strip, z):
        return jnp.where(at_last, turn(strip[z % 2], 123 - 32 * (z // 2), 1), turn(value, -1, 1))

    def behind_x(value, strip, z):
        return jnp.where(at_first, turn(strip[z % 2], -(32 * (z // 2) + 27), 1), turn(value, 1, 1))

    def sweep(kept_rows):
        for f in range(2):
            ex, ey, ez = ([strip_fields[f, c, t] for t in range(2)] for c in range(3))
            for t in range(2):
                if t == 0:
                    ex_z, ey_z = ex[1], ey[1]
                else:
                    ex_z = jnp.where(lane24 < 96, turn(ex[0], -32, 1), 0.0)
                    ey_z = jnp.where(lane24 < 96, turn(ey[0], -32, 1), 0.0)
                strip_curls[f, 0, t] = (ahead_y(ez[t]) - ez[t]) - (ey_z - ey[t])
                strip_curls[f, 1, t] = (ex_z - ex[t]) - (turn(ez[t], -1, 1) - ez[t])
                strip_curls[f, 2, t] = (turn(ey[t], -1, 1) - ey[t]) - (ahead_y(ex[t]) - ex[t])
            for z in range(Z):
                ex, ey, ez = (fields[f, c, z] for c in range(3))
                if z < Z - 1:
                    ex_z, ey_z = fields[f, 0, z + 1], fields[f, 1, z + 1]
                else:
                    ex_z = ey_z = jnp.zeros_like(ex)
                curls[f, 0, z] = (ahead_y(ez) - ez) - (ey_z - ey)
                curls[f, 1, z] = (ex_z - ex) - (ahead_x(ez, strip_fields.at[f, 2], z) - ez)
                curls[f, 2, z] = (ahead_x(ey, strip_fields.at[f, 1], z) - ey) - (ahead_y(ex) - ex)
        bottom = lane24 < 32
        for f in range(2):
            for t in range(2):
                ex, ey, ez = (strip_fields[f, c, t] for c in range(3))
                hx, hy, hz = (strip_curls[f, c, t] for c in range(3))
                if t == 1:
                    hx_z, hy_z = strip_curls[f, 0, 0], strip_curls[f, 1, 0]
                else:
                    hx_z = jnp.where(bottom, -ey, turn(strip_curls[f, 0, 1], 32, 1))
                    hy_z = jnp.where(bottom, ex, turn(strip_curls[f, 1, 1], 32, 1))
                curl_x = (hz - behind_y(hz)) - (hy - hy_z)
                curl_y = (hx - hx_z) - (hz - turn(hz, 1, 1))
                curl_z = (hy - turn(hy, 1, 1)) - (hx - behind_y(hx))
                step, kept = strip_rate[t], strip_keep[t]
                strip_fields[f, 0, t] = kept * ex + step * (strip_sources[f, 0, t] - curl_x)
                strip_fields[f, 1, t] = kept * ey + step * (strip_sources[f, 1, t] - curl_y)
                strip_fields[f, 2, t] = kept * ez + step * (strip_sources[f, 2, t] - curl_z)
            for z in range(Z):
                ex, ey, ez = (fields[f, c, z] for c in range(3))
                hx, hy, hz = (curls[f, c, z] for c in range(3))
                if z > 0:
                    hx_z, hy_z = curls[f, 0, z - 1], curls[f, 1, z - 1]
                else:
                    hx_z, hy_z = -ey, ex
                curl_x = (hz - behind_y(hz)) - (hy - hy_z)
                curl_y = (hx - hx_z) - (hz - behind_x(hz, strip_curls.at[f, 2], z))
                curl_z = (hy - behind_x(hy, strip_curls.at[f, 1], z)) - (hx - behind_y(hx))
                step, kept = rate[z], keep[z]
                fields[f, 0, z, 0:kept_rows] = (kept * ex + step * (sources[f, 0, z] - curl_x))[0:kept_rows]
                fields[f, 1, z, 0:kept_rows] = (kept * ey + step * (sources[f, 1, z] - curl_y))[0:kept_rows]
                fields[f, 2, z, 0:kept_rows] = (kept * ez + step * (sources[f, 2, z] - curl_z))[0:kept_rows]
    for number in range(ITERS):
        sweep(WRAP if number < ITERS - 1 else ROWS)

    product = jnp.zeros((ROWS, LANES), jnp.float32)
    strip_product = jnp.zeros((ROWS, LANES), jnp.float32)
    for c in range(3):
        for z in range(Z):
            product = product + fields[0, c, z, 0:ROWS] * fields[1, c, z, 0:ROWS]
        for t in range(2):
            strip_product = strip_product + strip_fields[0, c, t, 0:ROWS] * strip_fields[1, c, t, 0:ROWS]
    strip_product = strip_product + turn(strip_product, 64, 1)
    strip_product = strip_product + turn(strip_product, 32, 1)
    local = product * (-0.5 * gain_main[0:ROWS])
    lane = lanes_of(ROWS)
    local_side = jnp.where(
        lane < 64, turn(strip_product, -4, 1) * (-0.5 * gain_right[0:ROWS]),
        turn(strip_product, 100, 1) * (-0.5 * gain_left[0:ROWS]),
    )
    for out, value in ((slice(0, LANES), local), (slice(LANES, 2 * LANES), local_side)):
        local_far[:, out] = jnp.where(upward, value[8:16], value[0:8])
        local_near[:, out] = jnp.where(upward, value[0:8], value[8:16])


def turn_edges(right_side, left_side, lane):
    return jnp.where(lane < 16, right_side, left_side)


def last_kernel(fields, own_far, own_near, far, near, field, adjoint, gradient, wide, done):
    copies = [
        pltpu.make_async_copy(fields.at[f, :, :, pl.ds(0, ROWS)], out, done.at[f])
        for f, out in enumerate((field, adjoint))
    ]
    for copy in copies:
        copy.start()
    row = lax.axis_index("gy")
    upward = row % 2 == 1
    wide[0:8] = jnp.where(row == 0, 0.0, jnp.where(upward, near[...], far[...]))
    wide[8:16] = jnp.where(upward, own_near[...], own_far[...])
    wide[16:24] = jnp.where(upward, own_far[...], own_near[...])
    wide[24:32] = jnp.where(row == lax.axis_size("gy") - 1, 0.0, jnp.where(upward, far[...], near[...]))
    gradient[...] = cone(lambda a: wide[8 + a : 24 + a], ROWS)[:, :LANES]
    for copy in copies:
        copy.wait()


def swaps(axis, start):
    size = lax.axis_size(axis)
    pairs = [(i, i + 1) for i in range(start, size - 1, 2)]
    return sorted(pairs + [(j, i) for i, j in pairs])


def swap_rows(far, near):
    return lax.ppermute(far, "gy", swaps("gy", 1)), lax.ppermute(near, "gy", swaps("gy", 0))


def shape(*dims):
    return jax.ShapeDtypeStruct(dims, jnp.float32)


def call(kernel, outs, space=VMEM, scratch=(), places=None):
    def run(*operands):
        return pl.pallas_call(
            kernel,
            out_shape=outs,
            in_specs=[pl.BlockSpec(memory_space=space)] * len(operands),
            out_specs=[pl.BlockSpec(memory_space=place) for place in places or [VMEM] * len(outs)],
            scratch_shapes=scratch,
            compiler_params=pltpu.CompilerParams(vmem_limit_bytes=LIMIT),
        )(*operands)

    return run


def room(*dims):
    return pltpu.VMEM(dims, jnp.float32)


def on_device(background, density, design_tiles, material_tiles, contrast, source, adjoint_source, field_start, adjoint_start):
    inner = (field_start, adjoint_start, source, adjoint_source, background, density)
    tiles = (design_tiles, material_tiles, contrast)
    edges, rows, packed = shape(GROUPS + 1, ROWS, LANES), shape(PACKED, 8, LANES), shape(PACKED + GROUPS + 2, 8, LANES)
    first, second, own_right, own_left, far, near, gains, *inner = call(
        pack_kernel,
        [edges, edges, edges, edges, rows, rows, shape(3, WRAP, LANES)] + [shape(*a.shape) for a in inner],
        space=pltpu.HBM,
        scratch=[pltpu.SMEM(a.shape, a.dtype) for a in tiles] + [pltpu.SemaphoreType.DMA((9,))],
    )(*[pltpu.with_memory_space_constraint(a, pltpu.HBM) for a in (*tiles, *inner)])
    first_got = lax.ppermute(first, "gx", swaps("gx", 1))
    second_got = lax.ppermute(second, "gx", swaps("gx", 0))
    strips, side, far, near = call(strip_kernel, [shape(GROUPS, 2, ROWS, LANES), shape(ROWS, LANES), packed, packed])(
        own_right, own_left, far, near, first_got, second_got
    )
    far_got, near_got = swap_rows(far, near)
    block, part = shape(3, Z, ROWS, LANES), shape(8, 2 * LANES)
    planes, sheets = (2, 3, Z, WRAP, LANES), (2, 3, 2, WRAP, LANES)
    fields, local_far, local_near = call(
        main_kernel,
        [room(*planes), part, part],
        scratch=[
            room(*planes), room(*planes), room(Z, WRAP, LANES), room(Z, WRAP, LANES),
            room(*sheets), room(*sheets), room(*sheets), room(2, WRAP, LANES), room(2, WRAP, LANES),
            room(48, 2 * LANES),
        ],
    )(gains, *inner, far_got, near_got, strips, side)
    local_far_got, local_near_got = swap_rows(local_far, local_near)
    field, adjoint, gradient = call(
        last_kernel,
        [block, block, shape(ROWS, LANES)],
        places=(pltpu.HBM, pltpu.HBM, VMEM),
        scratch=[room(32, 2 * LANES), pltpu.SemaphoreType.DMA((2,))],
    )(fields, local_far, local_near, local_far_got, local_near_got)
    return (field, adjoint, gradient)


def solution(mesh):
    in_specs = (
        P(None, "gy", "gx"),
        P("gy", "gx"),
        P(),
        P(),
        P(),
        P(None, None, "gy", "gx"),
        P(None, None, "gy", "gx"),
        P(None, None, "gy", "gx"),
        P(None, None, "gy", "gx"),
    )
    out_specs = (P(None, None, "gy", "gx"), P(None, None, "gy", "gx"), P("gy", "gx"))
    return jax.shard_map(on_device, mesh=mesh, in_specs=in_specs, out_specs=out_specs, check_vma=False)
```

```python
import functools
import math

import jax
import jax.numpy as jnp
from jax import lax
from jax.experimental import pallas as pl
from jax.experimental.pallas import tpu as pltpu
from jax.sharding import PartitionSpec as P

ITERS = 4
RADIUS = 8
TILE = 128
Z = 8
ROWS = 16
LANES = 128
HALO = 4
WRAP = ROWS + 8
GROUPS = 13
PACKED = 4 * GROUPS + 2
VMEM = pltpu.VMEM
LIMIT = 48 * 1024 * 1024


def cone_weight(row_shift, col_shift):
    return max(0.0, RADIUS + 1 - math.sqrt(row_shift * row_shift + col_shift * col_shift))


def cone_total():
    span = range(-RADIUS, RADIUS + 1)
    return math.fsum(cone_weight(a, b) for a in span for b in span)


def lanes_of(rows):
    return lax.broadcasted_iota(jnp.int32, (rows, LANES), 1)


def rows_of(rows):
    return lax.broadcasted_iota(jnp.int32, (rows, LANES), 0)


def turn(value, shift, axis):
    size = value.shape[axis]
    return pltpu.roll(value, shift % size, axis)


def cone(rows_at, rows):
    total = cone_total()
    paired = [rows_at(0)]
    for a in range(1, RADIUS + 1):
        paired.append(rows_at(a) + rows_at(-a))
    result = None
    for b in range(RADIUS + 1):
        column = None
        for a in range(RADIUS + 1):
            weight = cone_weight(a, b)
            if weight > 0.0:
                term = paired[a] * (weight / total)
                column = term if column is None else column + term
        if b > 0:
            column = turn(column, b, 1) + turn(column, -b, 1)
        result = column if result is None else result + column
    return result


def pack_kernel(
    design_in, material_in, contrast_in, field_in, adjoint_in, source_in, adjoint_source_in, background_in, density_in,
    first, second, own_right, own_left, far, near, gains, field, adjoint, source, adjoint_source, background, density,
    design, material, contrast, done,
):
    arrays = (
        (field_in, field), (adjoint_in, adjoint), (source_in, source), (adjoint_source_in, adjoint_source),
        (background_in, background), (density_in, density),
        (design_in, design), (material_in, material), (contrast_in, contrast),
    )
    copies = [pltpu.make_async_copy(here, there, done.at[i]) for i, (here, there) in enumerate(arrays)]
    for copy in copies:
        copy.start()
    lane = lanes_of(ROWS)
    rightward = lax.axis_index("gx") % 2 == 0
    upward = lax.axis_index("gy") % 2 == 1
    low = rows_of(8) < 4
    for g in range(GROUPS):
        if g % 3 == 0:
            copies[g // 3].wait()
        planes = background if g == 12 else (field, adjoint, source, adjoint_source)[g // 3].at[g % 3]
        windows = []
        for t in range(2):
            window = None
            for q in range(Z // 2):
                here = turn(planes[2 * q + t], 32 * q + 12, 1)
                window = here if q == 0 else jnp.where(lane >= 32 * q, here, window)
            windows.append(window)
        half = lane % 32 < 16
        to_right = jnp.where(half, windows[0], turn(windows[1], 16, 1))
        to_left = jnp.where(half, turn(windows[0], -8, 1), turn(windows[1], 8, 1))
        own_right[g] = to_right
        own_left[g] = to_left
        first[g] = jnp.where(rightward, to_right, to_left)
        second[g] = jnp.where(rightward, to_left, to_right)
        for pair in range(Z // 2):
            k = g * (Z // 2) + pair
            down = jnp.where(low, planes[2 * pair, 0:8], turn(planes[2 * pair + 1, 0:8], 4, 0))
            up = jnp.where(low, turn(planes[2 * pair + 1, 8:16], 4, 0), planes[2 * pair, 8:16])
            far[k] = jnp.where(upward, up, down)
            near[k] = jnp.where(upward, down, up)
    for copy in copies[5:]:
        copy.wait()
    first[GROUPS] = density[...]
    second[GROUPS] = density[...]
    for part in range(2):
        far[4 * GROUPS + part] = density[8 * part : 8 * part + 8]
        near[4 * GROUPS + part] = density[8 * part : 8 * part + 8]

    col, row = lax.axis_index("gx"), lax.axis_index("gy")
    row24 = rows_of(WRAP)
    tiles_y, tiles_x = design.shape

    def gain_at(first, tile_x):
        tile_y = jnp.clip(first, 0, tiles_y * TILE - 1) // TILE
        tile_x = jnp.clip(tile_x, 0, tiles_x - 1)
        return design[tile_y, tile_x].astype(jnp.float32) * contrast[material[tile_y, tile_x]]

    for k in range(3):
        tile_x = col + (0, 1, -1)[k]
        here = gain_at(row * ROWS, tile_x)
        up = gain_at(row * ROWS + ROWS, tile_x)
        down = gain_at(row * ROWS - HALO, tile_x)
        gains[k] = jnp.where(row24 < 16, here, jnp.where(row24 < 20, up, down))


def strip_kernel(own_right, own_left, far_rows, near_rows, first_got, second_got, strips, side, far, near):
    col = lax.axis_index("gx")
    rightward = col % 2 == 0
    upward = lax.axis_index("gy") % 2 == 1
    first, last = col == 0, col == lax.axis_size("gx") - 1
    lane = lanes_of(ROWS)
    within = lane % 16
    half = lane % 32 < 16
    low = rows_of(8) < 4

    far[0:PACKED] = far_rows[...]
    near[0:PACKED] = near_rows[...]

    def sides(g):
        from_right = jnp.where(rightward, first_got[g], second_got[g])
        from_left = jnp.where(rightward, second_got[g], first_got[g])
        return jnp.where(last, 0.0, from_right), jnp.where(first, 0.0, from_left)

    for g in range(GROUPS):
        from_right, from_left = sides(g)
        here_right = jnp.where(within >= HALO, from_right, own_left[g])
        here_left = jnp.where(within < 12, from_left, own_right[g])
        even = jnp.where(half, here_right, turn(here_left, 16, 1))
        odd = jnp.where(half, turn(here_right, -16, 1), here_left)
        strips[g, 0] = even
        strips[g, 1] = odd
        down = jnp.where(low, even[0:8], turn(odd[0:8], 4, 0))
        up = jnp.where(low, turn(odd[8:16], 4, 0), even[8:16])
        far[PACKED + g] = jnp.where(upward, up, down)
        near[PACKED + g] = jnp.where(upward, down, up)
    from_right, from_left = sides(GROUPS)
    beside = jnp.where(lane < 64, from_right, from_left)
    side[...] = beside
    for part in range(2):
        far[PACKED + GROUPS + part] = beside[8 * part : 8 * part + 8]
        near[PACKED + GROUPS + part] = beside[8 * part : 8 * part + 8]


def unpack(far, near, pick, second):
    if second:
        return turn(jnp.where(pick, near, far), 4, 0)
    return jnp.where(pick, far, near)


def main_kernel(
    gains, field, adjoint, source, adjoint_source, background, density,
    far, near, strips, side,
    fields, local_far, local_near,
    sources, curls, rate, keep, strip_fields, strip_sources, strip_curls, strip_rate, strip_keep, wide,
):
    col, row = lax.axis_index("gx"), lax.axis_index("gy")
    cols, rows = lax.axis_size("gx"), lax.axis_size("gy")
    first_row, last_row = row == 0, row == rows - 1
    low = rows_of(8) < 4
    upward = row % 2 == 1
    pick = jnp.where(upward, rows_of(8), 7 - rows_of(8)) < 4
    lane24, row24 = lanes_of(WRAP), rows_of(WRAP)
    outside8 = (low & last_row) | (jnp.logical_not(low) & first_row)
    outside = ((row24 >= 16) & (row24 < 20) & last_row) | ((row24 >= 20) & first_row)
    j = lane24 % 32
    outside_strip = outside | ((j >= HALO) & (j < 16) & (col == cols - 1)) | ((j >= 16) & (j < 28) & (col == 0))
    gain_main, gain_right, gain_left = gains[0], gains[1], gains[2]

    wide[16:32, 0:LANES] = density[...]
    wide[16:32, LANES : 2 * LANES] = side[...]
    for part in range(2):
        k, rows8 = 4 * GROUPS + part, slice(8 * part, 8 * part + 8)
        wide[rows8, 0:LANES] = jnp.where(first_row, 0.0, jnp.where(upward, near[k], far[k]))
        rows8 = slice(32 + 8 * part, 40 + 8 * part)
        wide[rows8, 0:LANES] = jnp.where(last_row, 0.0, jnp.where(upward, far[k], near[k]))
        k, rows8 = PACKED + GROUPS + part, slice(8 * part, 8 * part + 8)
        wide[rows8, LANES : 2 * LANES] = jnp.where(first_row, 0.0, jnp.where(upward, near[k], far[k]))
        rows8 = slice(32 + 8 * part, 40 + 8 * part)
        wide[rows8, LANES : 2 * LANES] = jnp.where(last_row, 0.0, jnp.where(upward, far[k], near[k]))
    filtered = cone(lambda a: wide[8 + a : 40 + a], 32)
    low2 = lax.broadcasted_iota(jnp.int32, (8, 2 * LANES), 0) < 4
    filtered = jnp.concatenate(
        [filtered[8:24], jnp.where(low2, filtered[24:32], filtered[0:8])], axis=0
    )
    design_main = gain_main * filtered[:, :LANES]
    beside = filtered[:, LANES:]
    block = filtered[:, :LANES]
    right_side = jnp.where(lane24 < HALO, turn(block, HALO, 1), turn(beside, HALO, 1))
    left_side = jnp.where(lane24 < 28, turn(beside, 28, 1), turn(block, 28, 1))
    quarter = jnp.where(lane24 < 16, right_side * gain_right, left_side * gain_left)
    quarter = jnp.where((lane24 < HALO) | (lane24 >= 28), turn_edges(right_side, left_side, lane24) * gain_main, quarter)
    quarter = jnp.where(lane24 < 32, quarter, 0.0)
    quarter = quarter + turn(quarter, 32, 1)
    design_strip = quarter + turn(quarter, 64, 1)

    def whole(inner, halo):
        return jnp.concatenate([inner, halo], axis=0)

    for z in range(Z):
        k = 48 + z // 2
        halo = unpack(far[k], near[k], pick, z % 2)
        step = 0.5 / (4.0 + 0.5 * (whole(background[z], halo) + design_main))
        step = jnp.where(outside, 0.0, step)
        rate[z] = step
        keep[z] = 0.5 + 4.0 * step
    for t in range(2):
        halo = unpack(far[PACKED + 12], near[PACKED + 12], pick, t)
        step = 0.5 / (4.0 + 0.5 * (whole(strips[12, t], halo) + design_strip))
        step = jnp.where(outside_strip, 0.0, step)
        strip_rate[t] = step
        strip_keep[t] = 0.5 + 4.0 * step

    starts = (field, adjoint, source, adjoint_source)
    for f in range(4):
        for c in range(3):
            g = 3 * f + c
            for z in range(Z):
                k = 4 * g + z // 2
                halo = unpack(far[k], near[k], pick, z % 2)
                if f < 2:
                    fields[f, c, z] = whole(starts[f][c, z], jnp.where(outside8, 0.0, halo))
                else:
                    sources[f - 2, c, z] = whole(starts[f][c, z], halo)
            for t in range(2):
                halo = unpack(far[PACKED + g], near[PACKED + g], pick, t)
                if f < 2:
                    strip_fields[f, c, t] = whole(strips[g, t], jnp.where(outside8, 0.0, halo))
                else:
                    strip_sources[f - 2, c, t] = whole(strips[g, t], halo)

    at_last, at_first = lane24 == LANES - 1, lane24 == 0

    def ahead_y(value):
        return turn(value, -1, 0)

    def behind_y(value):
        return turn(value, 1, 0)

    def ahead_x(value, strip, z):
        return jnp.where(at_last, turn(strip[z % 2], 123 - 32 * (z // 2), 1), turn(value, -1, 1))

    def behind_x(value, strip, z):
        return jnp.where(at_first, turn(strip[z % 2], -(32 * (z // 2) + 27), 1), turn(value, 1, 1))

    def sweep(kept_rows):
        for f in range(2):
            ex, ey, ez = ([strip_fields[f, c, t] for t in range(2)] for c in range(3))
            for t in range(2):
                if t == 0:
                    ex_z, ey_z = ex[1], ey[1]
                else:
                    ex_z = jnp.where(lane24 < 96, turn(ex[0], -32, 1), 0.0)
                    ey_z = jnp.where(lane24 < 96, turn(ey[0], -32, 1), 0.0)
                strip_curls[f, 0, t] = (ahead_y(ez[t]) - ez[t]) - (ey_z - ey[t])
                strip_curls[f, 1, t] = (ex_z - ex[t]) - (turn(ez[t], -1, 1) - ez[t])
                strip_curls[f, 2, t] = (turn(ey[t], -1, 1) - ey[t]) - (ahead_y(ex[t]) - ex[t])
            for z in range(Z):
                ex, ey, ez = (fields[f, c, z] for c in range(3))
                if z < Z - 1:
                    ex_z, ey_z = fields[f, 0, z + 1], fields[f, 1, z + 1]
                else:
                    ex_z = ey_z = jnp.zeros_like(ex)
                curls[f, 0, z] = (ahead_y(ez) - ez) - (ey_z - ey)
                curls[f, 1, z] = (ex_z - ex) - (ahead_x(ez, strip_fields.at[f, 2], z) - ez)
                curls[f, 2, z] = (ahead_x(ey, strip_fields.at[f, 1], z) - ey) - (ahead_y(ex) - ex)
        bottom = lane24 < 32
        for f in range(2):
            for t in range(2):
                ex, ey, ez = (strip_fields[f, c, t] for c in range(3))
                hx, hy, hz = (strip_curls[f, c, t] for c in range(3))
                if t == 1:
                    hx_z, hy_z = strip_curls[f, 0, 0], strip_curls[f, 1, 0]
                else:
                    hx_z = jnp.where(bottom, -ey, turn(strip_curls[f, 0, 1], 32, 1))
                    hy_z = jnp.where(bottom, ex, turn(strip_curls[f, 1, 1], 32, 1))
                curl_x = (hz - behind_y(hz)) - (hy - hy_z)
                curl_y = (hx - hx_z) - (hz - turn(hz, 1, 1))
                curl_z = (hy - turn(hy, 1, 1)) - (hx - behind_y(hx))
                step, kept = strip_rate[t], strip_keep[t]
                strip_fields[f, 0, t] = kept * ex + step * (strip_sources[f, 0, t] - curl_x)
                strip_fields[f, 1, t] = kept * ey + step * (strip_sources[f, 1, t] - curl_y)
                strip_fields[f, 2, t] = kept * ez + step * (strip_sources[f, 2, t] - curl_z)
            for z in range(Z):
                ex, ey, ez = (fields[f, c, z] for c in range(3))
                hx, hy, hz = (curls[f, c, z] for c in range(3))
                if z > 0:
                    hx_z, hy_z = curls[f, 0, z - 1], curls[f, 1, z - 1]
                else:
                    hx_z, hy_z = -ey, ex
                curl_x = (hz - behind_y(hz)) - (hy - hy_z)
                curl_y = (hx - hx_z) - (hz - behind_x(hz, strip_curls.at[f, 2], z))
                curl_z = (hy - behind_x(hy, strip_curls.at[f, 1], z)) - (hx - behind_y(hx))
                step, kept = rate[z], keep[z]
                fields[f, 0, z, 0:kept_rows] = (kept * ex + step * (sources[f, 0, z] - curl_x))[0:kept_rows]
                fields[f, 1, z, 0:kept_rows] = (kept * ey + step * (sources[f, 1, z] - curl_y))[0:kept_rows]
                fields[f, 2, z, 0:kept_rows] = (kept * ez + step * (sources[f, 2, z] - curl_z))[0:kept_rows]
    for number in range(ITERS):
        sweep(WRAP if number < ITERS - 1 else ROWS)

    product = jnp.zeros((ROWS, LANES), jnp.float32)
    strip_product = jnp.zeros((ROWS, LANES), jnp.float32)
    for c in range(3):
        for z in range(Z):
            product = product + fields[0, c, z, 0:ROWS] * fields[1, c, z, 0:ROWS]
        for t in range(2):
            strip_product = strip_product + strip_fields[0, c, t, 0:ROWS] * strip_fields[1, c, t, 0:ROWS]
    strip_product = strip_product + turn(strip_product, 64, 1)
    strip_product = strip_product + turn(strip_product, 32, 1)
    local = product * (-0.5 * gain_main[0:ROWS])
    lane = lanes_of(ROWS)
    local_side = jnp.where(
        lane < 64, turn(strip_product, -4, 1) * (-0.5 * gain_right[0:ROWS]),
        turn(strip_product, 100, 1) * (-0.5 * gain_left[0:ROWS]),
    )
    for out, value in ((slice(0, LANES), local), (slice(LANES, 2 * LANES), local_side)):
        local_far[:, out] = jnp.where(upward, value[8:16], value[0:8])
        local_near[:, out] = jnp.where(upward, value[0:8], value[8:16])


def turn_edges(right_side, left_side, lane):
    return jnp.where(lane < 16, right_side, left_side)


def last_kernel(fields, own_far, own_near, far, near, field, adjoint, gradient, wide, result, done):
    copies = [
        pltpu.make_async_copy(fields.at[f, :, :, pl.ds(0, ROWS)], out, done.at[f])
        for f, out in enumerate((field, adjoint))
    ]
    for copy in copies:
        copy.start()
    row = lax.axis_index("gy")
    upward = row % 2 == 1
    wide[0:8] = jnp.where(row == 0, 0.0, jnp.where(upward, near[...], far[...]))
    wide[8:16] = jnp.where(upward, own_near[...], own_far[...])
    wide[16:24] = jnp.where(upward, own_far[...], own_near[...])
    wide[24:32] = jnp.where(row == lax.axis_size("gy") - 1, 0.0, jnp.where(upward, far[...], near[...]))
    result[...] = cone(lambda a: wide[8 + a : 24 + a], ROWS)[:, :LANES]
    copies.append(pltpu.make_async_copy(result, gradient, done.at[2]))
    copies[2].start()
    for copy in copies:
        copy.wait()


def swaps(axis, start):
    size = lax.axis_size(axis)
    pairs = [(i, i + 1) for i in range(start, size - 1, 2)]
    return sorted(pairs + [(j, i) for i, j in pairs])


def swap_rows(far, near):
    return lax.ppermute(far, "gy", swaps("gy", 1)), lax.ppermute(near, "gy", swaps("gy", 0))


def shape(*dims):
    return jax.ShapeDtypeStruct(dims, jnp.float32)


def call(kernel, outs, space=VMEM, scratch=(), places=None):
    def run(*operands):
        return pl.pallas_call(
            kernel,
            out_shape=outs,
            in_specs=[pl.BlockSpec(memory_space=space)] * len(operands),
            out_specs=[pl.BlockSpec(memory_space=place) for place in places or [VMEM] * len(outs)],
            scratch_shapes=scratch,
            compiler_params=pltpu.CompilerParams(vmem_limit_bytes=LIMIT),
        )(*operands)

    return run


def room(*dims):
    return pltpu.VMEM(dims, jnp.float32)


def on_device(background, density, design_tiles, material_tiles, contrast, source, adjoint_source, field_start, adjoint_start):
    inner = (field_start, adjoint_start, source, adjoint_source, background, density)
    tiles = (design_tiles, material_tiles, contrast)
    edges, rows, packed = shape(GROUPS + 1, ROWS, LANES), shape(PACKED, 8, LANES), shape(PACKED + GROUPS + 2, 8, LANES)
    first, second, own_right, own_left, far, near, gains, *inner = call(
        pack_kernel,
        [edges, edges, edges, edges, rows, rows, shape(3, WRAP, LANES)] + [shape(*a.shape) for a in inner],
        space=pltpu.HBM,
        scratch=[pltpu.SMEM(a.shape, a.dtype) for a in tiles] + [pltpu.SemaphoreType.DMA((9,))],
    )(*[pltpu.with_memory_space_constraint(a, pltpu.HBM) for a in (*tiles, *inner)])
    first_got = lax.ppermute(first, "gx", swaps("gx", 0))
    second_got = lax.ppermute(second, "gx", swaps("gx", 1))
    strips, side, far, near = call(strip_kernel, [shape(GROUPS, 2, ROWS, LANES), shape(ROWS, LANES), packed, packed])(
        own_right, own_left, far, near, first_got, second_got
    )
    far_got, near_got = swap_rows(far, near)
    block, part = shape(3, Z, ROWS, LANES), shape(8, 2 * LANES)
    planes, sheets = (2, 3, Z, WRAP, LANES), (2, 3, 2, WRAP, LANES)
    fields, local_far, local_near = call(
        main_kernel,
        [room(*planes), part, part],
        scratch=[
            room(*planes), room(*planes), room(Z, WRAP, LANES), room(Z, WRAP, LANES),
            room(*sheets), room(*sheets), room(*sheets), room(2, WRAP, LANES), room(2, WRAP, LANES),
            room(48, 2 * LANES),
        ],
    )(gains, *inner, far_got, near_got, strips, side)
    local_far_got, local_near_got = swap_rows(local_far, local_near)
    field, adjoint, gradient = call(
        last_kernel,
        [block, block, shape(ROWS, LANES)],
        places=(pltpu.HBM,) * 3,
        scratch=[room(32, 2 * LANES), room(ROWS, LANES), pltpu.SemaphoreType.DMA((3,))],
    )(fields, local_far, local_near, local_far_got, local_near_got)
    return (field, adjoint, gradient)


def solution(mesh):
    in_specs = (
        P(None, "gy", "gx"),
        P("gy", "gx"),
        P(),
        P(),
        P(),
        P(None, None, "gy", "gx"),
        P(None, None, "gy", "gx"),
        P(None, None, "gy", "gx"),
        P(None, None, "gy", "gx"),
    )
    out_specs = (P(None, None, "gy", "gx"), P(None, None, "gy", "gx"), P("gy", "gx"))
    return jax.shard_map(on_device, mesh=mesh, in_specs=in_specs, out_specs=out_specs, check_vma=False)
```

```python
import functools
import math

import jax
import jax.numpy as jnp
from jax import lax
from jax.experimental import pallas as pl
from jax.experimental.pallas import tpu as pltpu
from jax.sharding import PartitionSpec as P

ITERS = 4
RADIUS = 8
TILE = 128
Z = 8
ROWS = 16
LANES = 128
HALO = 4
WRAP = ROWS + 8
GROUPS = 13
PACKED = 4 * GROUPS + 2
VMEM = pltpu.VMEM
LIMIT = 48 * 1024 * 1024


def cone_weight(row_shift, col_shift):
    return max(0.0, RADIUS + 1 - math.sqrt(row_shift * row_shift + col_shift * col_shift))


def cone_total():
    span = range(-RADIUS, RADIUS + 1)
    return math.fsum(cone_weight(a, b) for a in span for b in span)


def lanes_of(rows):
    return lax.broadcasted_iota(jnp.int32, (rows, LANES), 1)


def rows_of(rows):
    return lax.broadcasted_iota(jnp.int32, (rows, LANES), 0)


def turn(value, shift, axis):
    size = value.shape[axis]
    return pltpu.roll(value, shift % size, axis)


def cone(rows_at, rows):
    total = cone_total()
    paired = [rows_at(0)]
    for a in range(1, RADIUS + 1):
        paired.append(rows_at(a) + rows_at(-a))
    result = None
    for b in range(RADIUS + 1):
        column = None
        for a in range(RADIUS + 1):
            weight = cone_weight(a, b)
            if weight > 0.0:
                term = paired[a] * (weight / total)
                column = term if column is None else column + term
        if b > 0:
            column = turn(column, b, 1) + turn(column, -b, 1)
        result = column if result is None else result + column
    return result


def pack_kernel(
    design_in, material_in, contrast_in, field_in, adjoint_in, source_in, adjoint_source_in, background_in, density_in,
    first, second, own_right, own_left, far, near, gains, field, adjoint, source, adjoint_source, background, density,
    design, material, contrast, done,
):
    arrays = (
        (field_in, field), (adjoint_in, adjoint), (source_in, source), (adjoint_source_in, adjoint_source),
        (background_in, background), (density_in, density),
        (design_in, design), (material_in, material), (contrast_in, contrast),
    )
    copies = [pltpu.make_async_copy(here, there, done.at[i]) for i, (here, there) in enumerate(arrays)]
    for copy in copies:
        copy.start()
    lane = lanes_of(ROWS)
    rightward = lax.axis_index("gx") % 2 == 1
    upward = lax.axis_index("gy") % 2 == 1
    low = rows_of(8) < 4
    for g in range(GROUPS):
        if g % 3 == 0:
            copies[g // 3].wait()
        planes = background if g == 12 else (field, adjoint, source, adjoint_source)[g // 3].at[g % 3]
        windows = []
        for t in range(2):
            window = None
            for q in range(Z // 2):
                here = turn(planes[2 * q + t], 32 * q + 12, 1)
                window = here if q == 0 else jnp.where(lane >= 32 * q, here, window)
            windows.append(window)
        half = lane % 32 < 16
        to_right = jnp.where(half, windows[0], turn(windows[1], 16, 1))
        to_left = jnp.where(half, turn(windows[0], -8, 1), turn(windows[1], 8, 1))
        own_right[g] = to_right
        own_left[g] = to_left
        first[g] = jnp.where(rightward, to_right, to_left)
        second[g] = jnp.where(rightward, to_left, to_right)
        for pair in range(Z // 2):
            k = g * (Z // 2) + pair
            down = jnp.where(low, planes[2 * pair, 0:8], turn(planes[2 * pair + 1, 0:8], 4, 0))
            up = jnp.where(low, turn(planes[2 * pair + 1, 8:16], 4, 0), planes[2 * pair, 8:16])
            far[k] = jnp.where(upward, up, down)
            near[k] = jnp.where(upward, down, up)
    for copy in copies[5:]:
        copy.wait()
    first[GROUPS] = density[...]
    second[GROUPS] = density[...]
    for part in range(2):
        far[4 * GROUPS + part] = density[8 * part : 8 * part + 8]
        near[4 * GROUPS + part] = density[8 * part : 8 * part + 8]

    col, row = lax.axis_index("gx"), lax.axis_index("gy")
    row24 = rows_of(WRAP)
    tiles_y, tiles_x = design.shape

    def gain_at(first, tile_x):
        tile_y = jnp.clip(first, 0, tiles_y * TILE - 1) // TILE
        tile_x = jnp.clip(tile_x, 0, tiles_x - 1)
        return design[tile_y, tile_x].astype(jnp.float32) * contrast[material[tile_y, tile_x]]

    for k in range(3):
        tile_x = col + (0, 1, -1)[k]
        here = gain_at(row * ROWS, tile_x)
        up = gain_at(row * ROWS + ROWS, tile_x)
        down = gain_at(row * ROWS - HALO, tile_x)
        gains[k] = jnp.where(row24 < 16, here, jnp.where(row24 < 20, up, down))


def strip_kernel(own_right, own_left, far_rows, near_rows, first_got, second_got, strips, side, far, near):
    col = lax.axis_index("gx")
    rightward = col % 2 == 1
    upward = lax.axis_index("gy") % 2 == 1
    first, last = col == 0, col == lax.axis_size("gx") - 1
    lane = lanes_of(ROWS)
    within = lane % 16
    half = lane % 32 < 16
    low = rows_of(8) < 4

    far[0:PACKED] = far_rows[...]
    near[0:PACKED] = near_rows[...]

    def sides(g):
        from_right = jnp.where(rightward, first_got[g], second_got[g])
        from_left = jnp.where(rightward, second_got[g], first_got[g])
        return jnp.where(last, 0.0, from_right), jnp.where(first, 0.0, from_left)

    for g in range(GROUPS):
        from_right, from_left = sides(g)
        here_right = jnp.where(within >= HALO, from_right, own_left[g])
        here_left = jnp.where(within < 12, from_left, own_right[g])
        even = jnp.where(half, here_right, turn(here_left, 16, 1))
        odd = jnp.where(half, turn(here_right, -16, 1), here_left)
        strips[g, 0] = even
        strips[g, 1] = odd
        down = jnp.where(low, even[0:8], turn(odd[0:8], 4, 0))
        up = jnp.where(low, turn(odd[8:16], 4, 0), even[8:16])
        far[PACKED + g] = jnp.where(upward, up, down)
        near[PACKED + g] = jnp.where(upward, down, up)
    from_right, from_left = sides(GROUPS)
    beside = jnp.where(lane < 64, from_right, from_left)
    side[...] = beside
    for part in range(2):
        far[PACKED + GROUPS + part] = beside[8 * part : 8 * part + 8]
        near[PACKED + GROUPS + part] = beside[8 * part : 8 * part + 8]


def unpack(far, near, pick, second):
    if second:
        return turn(jnp.where(pick, near, far), 4, 0)
    return jnp.where(pick, far, near)


def main_kernel(
    gains, field, adjoint, source, adjoint_source, background, density,
    far, near, strips, side,
    fields, local_far, local_near,
    sources, curls, rate, keep, strip_fields, strip_sources, strip_curls, strip_rate, strip_keep, wide,
):
    col, row = lax.axis_index("gx"), lax.axis_index("gy")
    cols, rows = lax.axis_size("gx"), lax.axis_size("gy")
    first_row, last_row = row == 0, row == rows - 1
    low = rows_of(8) < 4
    upward = row % 2 == 1
    pick = jnp.where(upward, rows_of(8), 7 - rows_of(8)) < 4
    lane24, row24 = lanes_of(WRAP), rows_of(WRAP)
    outside8 = (low & last_row) | (jnp.logical_not(low) & first_row)
    outside = ((row24 >= 16) & (row24 < 20) & last_row) | ((row24 >= 20) & first_row)
    j = lane24 % 32
    outside_strip = outside | ((j >= HALO) & (j < 16) & (col == cols - 1)) | ((j >= 16) & (j < 28) & (col == 0))
    gain_main, gain_right, gain_left = gains[0], gains[1], gains[2]

    wide[16:32, 0:LANES] = density[...]
    wide[16:32, LANES : 2 * LANES] = side[...]
    for part in range(2):
        k, rows8 = 4 * GROUPS + part, slice(8 * part, 8 * part + 8)
        wide[rows8, 0:LANES] = jnp.where(first_row, 0.0, jnp.where(upward, near[k], far[k]))
        rows8 = slice(32 + 8 * part, 40 + 8 * part)
        wide[rows8, 0:LANES] = jnp.where(last_row, 0.0, jnp.where(upward, far[k], near[k]))
        k, rows8 = PACKED + GROUPS + part, slice(8 * part, 8 * part + 8)
        wide[rows8, LANES : 2 * LANES] = jnp.where(first_row, 0.0, jnp.where(upward, near[k], far[k]))
        rows8 = slice(32 + 8 * part, 40 + 8 * part)
        wide[rows8, LANES : 2 * LANES] = jnp.where(last_row, 0.0, jnp.where(upward, far[k], near[k]))
    filtered = cone(lambda a: wide[8 + a : 40 + a], 32)
    low2 = lax.broadcasted_iota(jnp.int32, (8, 2 * LANES), 0) < 4
    filtered = jnp.concatenate(
        [filtered[8:24], jnp.where(low2, filtered[24:32], filtered[0:8])], axis=0
    )
    design_main = gain_main * filtered[:, :LANES]
    beside = filtered[:, LANES:]
    block = filtered[:, :LANES]
    right_side = jnp.where(lane24 < HALO, turn(block, HALO, 1), turn(beside, HALO, 1))
    left_side = jnp.where(lane24 < 28, turn(beside, 28, 1), turn(block, 28, 1))
    quarter = jnp.where(lane24 < 16, right_side * gain_right, left_side * gain_left)
    quarter = jnp.where((lane24 < HALO) | (lane24 >= 28), turn_edges(right_side, left_side, lane24) * gain_main, quarter)
    quarter = jnp.where(lane24 < 32, quarter, 0.0)
    quarter = quarter + turn(quarter, 32, 1)
    design_strip = quarter + turn(quarter, 64, 1)

    def whole(inner, halo):
        return jnp.concatenate([inner, halo], axis=0)

    for z in range(Z):
        k = 48 + z // 2
        halo = unpack(far[k], near[k], pick, z % 2)
        step = 0.5 / (4.0 + 0.5 * (whole(background[z], halo) + design_main))
        step = jnp.where(outside, 0.0, step)
        rate[z] = step
        keep[z] = 0.5 + 4.0 * step
    for t in range(2):
        halo = unpack(far[PACKED + 12], near[PACKED + 12], pick, t)
        step = 0.5 / (4.0 + 0.5 * (whole(strips[12, t], halo) + design_strip))
        step = jnp.where(outside_strip, 0.0, step)
        strip_rate[t] = step
        strip_keep[t] = 0.5 + 4.0 * step

    starts = (field, adjoint, source, adjoint_source)
    for f in range(4):
        for c in range(3):
            g = 3 * f + c
            for z in range(Z):
                k = 4 * g + z // 2
                halo = unpack(far[k], near[k], pick, z % 2)
                if f < 2:
                    fields[f, c, z] = whole(starts[f][c, z], jnp.where(outside8, 0.0, halo))
                else:
                    sources[f - 2, c, z] = whole(starts[f][c, z], halo)
            for t in range(2):
                halo = unpack(far[PACKED + g], near[PACKED + g], pick, t)
                if f < 2:
                    strip_fields[f, c, t] = whole(strips[g, t], jnp.where(outside8, 0.0, halo))
                else:
                    strip_sources[f - 2, c, t] = whole(strips[g, t], halo)

    at_last, at_first = lane24 == LANES - 1, lane24 == 0

    def ahead_y(value):
        return turn(value, -1, 0)

    def behind_y(value):
        return turn(value, 1, 0)

    def ahead_x(value, strip, z):
        return jnp.where(at_last, turn(strip[z % 2], 123 - 32 * (z // 2), 1), turn(value, -1, 1))

    def behind_x(value, strip, z):
        return jnp.where(at_first, turn(strip[z % 2], -(32 * (z // 2) + 27), 1), turn(value, 1, 1))

    def sweep(kept_rows):
        for f in range(2):
            ex, ey, ez = ([strip_fields[f, c, t] for t in range(2)] for c in range(3))
            for t in range(2):
                if t == 0:
                    ex_z, ey_z = ex[1], ey[1]
                else:
                    ex_z = jnp.where(lane24 < 96, turn(ex[0], -32, 1), 0.0)
                    ey_z = jnp.where(lane24 < 96, turn(ey[0], -32, 1), 0.0)
                strip_curls[f, 0, t] = (ahead_y(ez[t]) - ez[t]) - (ey_z - ey[t])
                strip_curls[f, 1, t] = (ex_z - ex[t]) - (turn(ez[t], -1, 1) - ez[t])
                strip_curls[f, 2, t] = (turn(ey[t], -1, 1) - ey[t]) - (ahead_y(ex[t]) - ex[t])
            for z in range(Z):
                ex, ey, ez = (fields[f, c, z] for c in range(3))
                if z < Z - 1:
                    ex_z, ey_z = fields[f, 0, z + 1], fields[f, 1, z + 1]
                else:
                    ex_z = ey_z = jnp.zeros_like(ex)
                curls[f, 0, z] = (ahead_y(ez) - ez) - (ey_z - ey)
                curls[f, 1, z] = (ex_z - ex) - (ahead_x(ez, strip_fields.at[f, 2], z) - ez)
                curls[f, 2, z] = (ahead_x(ey, strip_fields.at[f, 1], z) - ey) - (ahead_y(ex) - ex)
        bottom = lane24 < 32
        for f in range(2):
            for t in range(2):
                ex, ey, ez = (strip_fields[f, c, t] for c in range(3))
                hx, hy, hz = (strip_curls[f, c, t] for c in range(3))
                if t == 1:
                    hx_z, hy_z = strip_curls[f, 0, 0], strip_curls[f, 1, 0]
                else:
                    hx_z = jnp.where(bottom, -ey, turn(strip_curls[f, 0, 1], 32, 1))
                    hy_z = jnp.where(bottom, ex, turn(strip_curls[f, 1, 1], 32, 1))
                curl_x = (hz - behind_y(hz)) - (hy - hy_z)
                curl_y = (hx - hx_z) - (hz - turn(hz, 1, 1))
                curl_z = (hy - turn(hy, 1, 1)) - (hx - behind_y(hx))
                step, kept = strip_rate[t], strip_keep[t]
                strip_fields[f, 0, t] = kept * ex + step * (strip_sources[f, 0, t] - curl_x)
                strip_fields[f, 1, t] = kept * ey + step * (strip_sources[f, 1, t] - curl_y)
                strip_fields[f, 2, t] = kept * ez + step * (strip_sources[f, 2, t] - curl_z)
            for z in range(Z):
                ex, ey, ez = (fields[f, c, z] for c in range(3))
                hx, hy, hz = (curls[f, c, z] for c in range(3))
                if z > 0:
                    hx_z, hy_z = curls[f, 0, z - 1], curls[f, 1, z - 1]
                else:
                    hx_z, hy_z = -ey, ex
                curl_x = (hz - behind_y(hz)) - (hy - hy_z)
                curl_y = (hx - hx_z) - (hz - behind_x(hz, strip_curls.at[f, 2], z))
                curl_z = (hy - behind_x(hy, strip_curls.at[f, 1], z)) - (hx - behind_y(hx))
                step, kept = rate[z], keep[z]
                fields[f, 0, z, 0:kept_rows] = (kept * ex + step * (sources[f, 0, z] - curl_x))[0:kept_rows]
                fields[f, 1, z, 0:kept_rows] = (kept * ey + step * (sources[f, 1, z] - curl_y))[0:kept_rows]
                fields[f, 2, z, 0:kept_rows] = (kept * ez + step * (sources[f, 2, z] - curl_z))[0:kept_rows]
    for number in range(ITERS):
        sweep(WRAP if number < ITERS - 1 else ROWS)

    product = jnp.zeros((ROWS, LANES), jnp.float32)
    strip_product = jnp.zeros((ROWS, LANES), jnp.float32)
    for c in range(3):
        for z in range(Z):
            product = product + fields[0, c, z, 0:ROWS] * fields[1, c, z, 0:ROWS]
        for t in range(2):
            strip_product = strip_product + strip_fields[0, c, t, 0:ROWS] * strip_fields[1, c, t, 0:ROWS]
    strip_product = strip_product + turn(strip_product, 64, 1)
    strip_product = strip_product + turn(strip_product, 32, 1)
    local = product * (-0.5 * gain_main[0:ROWS])
    lane = lanes_of(ROWS)
    local_side = jnp.where(
        lane < 64, turn(strip_product, -4, 1) * (-0.5 * gain_right[0:ROWS]),
        turn(strip_product, 100, 1) * (-0.5 * gain_left[0:ROWS]),
    )
    for out, value in ((slice(0, LANES), local), (slice(LANES, 2 * LANES), local_side)):
        local_far[:, out] = jnp.where(upward, value[8:16], value[0:8])
        local_near[:, out] = jnp.where(upward, value[0:8], value[8:16])


def turn_edges(right_side, left_side, lane):
    return jnp.where(lane < 16, right_side, left_side)


def last_kernel(fields, own_far, own_near, far, near, field, adjoint, gradient, wide, result, done):
    copies = [
        pltpu.make_async_copy(fields.at[f, :, :, pl.ds(0, ROWS)], out, done.at[f])
        for f, out in enumerate((field, adjoint))
    ]
    for copy in copies:
        copy.start()
    row = lax.axis_index("gy")
    upward = row % 2 == 1
    wide[0:8] = jnp.where(row == 0, 0.0, jnp.where(upward, near[...], far[...]))
    wide[8:16] = jnp.where(upward, own_near[...], own_far[...])
    wide[16:24] = jnp.where(upward, own_far[...], own_near[...])
    wide[24:32] = jnp.where(row == lax.axis_size("gy") - 1, 0.0, jnp.where(upward, far[...], near[...]))
    result[...] = cone(lambda a: wide[8 + a : 24 + a], ROWS)[:, :LANES]
    copies.append(pltpu.make_async_copy(result, gradient, done.at[2]))
    copies[2].start()
    for copy in copies:
        copy.wait()


def swaps(axis, start):
    size = lax.axis_size(axis)
    pairs = [(i, i + 1) for i in range(start, size - 1, 2)]
    return sorted(pairs + [(j, i) for i, j in pairs])


def swap_rows(far, near):
    return lax.ppermute(far, "gy", swaps("gy", 1)), lax.ppermute(near, "gy", swaps("gy", 0))


def shape(*dims):
    return jax.ShapeDtypeStruct(dims, jnp.float32)


def call(kernel, outs, space=VMEM, scratch=(), places=None):
    def run(*operands):
        return pl.pallas_call(
            kernel,
            out_shape=outs,
            in_specs=[pl.BlockSpec(memory_space=space)] * len(operands),
            out_specs=[pl.BlockSpec(memory_space=place) for place in places or [VMEM] * len(outs)],
            scratch_shapes=scratch,
            compiler_params=pltpu.CompilerParams(vmem_limit_bytes=LIMIT),
        )(*operands)

    return run


def room(*dims):
    return pltpu.VMEM(dims, jnp.float32)


def on_device(background, density, design_tiles, material_tiles, contrast, source, adjoint_source, field_start, adjoint_start):
    inner = (field_start, adjoint_start, source, adjoint_source, background, density)
    tiles = (design_tiles, material_tiles, contrast)
    edges, rows, packed = shape(GROUPS + 1, ROWS, LANES), shape(PACKED, 8, LANES), shape(PACKED + GROUPS + 2, 8, LANES)
    first, second, own_right, own_left, far, near, gains, *inner = call(
        pack_kernel,
        [edges, edges, edges, edges, rows, rows, shape(3, WRAP, LANES)] + [shape(*a.shape) for a in inner],
        space=pltpu.HBM,
        scratch=[pltpu.SMEM(a.shape, a.dtype) for a in tiles] + [pltpu.SemaphoreType.DMA((9,))],
    )(*[pltpu.with_memory_space_constraint(a, pltpu.HBM) for a in (*tiles, *inner)])
    first_got = lax.ppermute(first, "gx", swaps("gx", 1))
    second_got = lax.ppermute(second, "gx", swaps("gx", 0))
    strips, side, far, near = call(strip_kernel, [shape(GROUPS, 2, ROWS, LANES), shape(ROWS, LANES), packed, packed])(
        own_right, own_left, far, near, first_got, second_got
    )
    far_got, near_got = swap_rows(far, near)
    block, part = shape(3, Z, ROWS, LANES), shape(8, 2 * LANES)
    planes, sheets = (2, 3, Z, WRAP, LANES), (2, 3, 2, WRAP, LANES)
    fields, local_far, local_near = call(
        main_kernel,
        [room(*planes), part, part],
        scratch=[
            room(*planes), room(*planes), room(Z, WRAP, LANES), room(Z, WRAP, LANES),
            room(*sheets), room(*sheets), room(*sheets), room(2, WRAP, LANES), room(2, WRAP, LANES),
            room(48, 2 * LANES),
        ],
    )(gains, *inner, far_got, near_got, strips, side)
    local_far_got, local_near_got = swap_rows(local_far, local_near)
    field, adjoint, gradient = call(
        last_kernel,
        [block, block, shape(ROWS, LANES)],
        places=(pltpu.HBM,) * 3,
        scratch=[room(32, 2 * LANES), room(ROWS, LANES), pltpu.SemaphoreType.DMA((3,))],
    )(fields, local_far, local_near, local_far_got, local_near_got)
    return (field, adjoint, gradient)


def solution(mesh):
    in_specs = (
        P(None, "gy", "gx"),
        P("gy", "gx"),
        P(),
        P(),
        P(),
        P(None, None, "gy", "gx"),
        P(None, None, "gy", "gx"),
        P(None, None, "gy", "gx"),
        P(None, None, "gy", "gx"),
    )
    out_specs = (P(None, None, "gy", "gx"), P(None, None, "gy", "gx"), P("gy", "gx"))
    return jax.shard_map(on_device, mesh=mesh, in_specs=in_specs, out_specs=out_specs, check_vma=False)
```

```python
import functools
import math

import jax
import jax.numpy as jnp
from jax import lax
from jax.experimental import pallas as pl
from jax.experimental.pallas import tpu as pltpu
from jax.sharding import PartitionSpec as P

ITERS = 4
RADIUS = 8
TILE = 128
Z = 8
ROWS = 16
LANES = 128
HALO = 4
WRAP = ROWS + 8
GROUPS = 13
PACKED = 4 * GROUPS + 2
VMEM = pltpu.VMEM
LIMIT = 48 * 1024 * 1024


def cone_weight(row_shift, col_shift):
    return max(0.0, RADIUS + 1 - math.sqrt(row_shift * row_shift + col_shift * col_shift))


def cone_total():
    span = range(-RADIUS, RADIUS + 1)
    return math.fsum(cone_weight(a, b) for a in span for b in span)


def lanes_of(rows):
    return lax.broadcasted_iota(jnp.int32, (rows, LANES), 1)


def rows_of(rows):
    return lax.broadcasted_iota(jnp.int32, (rows, LANES), 0)


def turn(value, shift, axis):
    size = value.shape[axis]
    return pltpu.roll(value, shift % size, axis)


def cone(rows_at, rows):
    total = cone_total()
    paired = [rows_at(0)]
    for a in range(1, RADIUS + 1):
        paired.append(rows_at(a) + rows_at(-a))
    result = None
    for b in range(RADIUS + 1):
        column = None
        for a in range(RADIUS + 1):
            weight = cone_weight(a, b)
            if weight > 0.0:
                term = paired[a] * (weight / total)
                column = term if column is None else column + term
        if b > 0:
            column = turn(column, b, 1) + turn(column, -b, 1)
        result = column if result is None else result + column
    return result


def pack_kernel(
    field_in, adjoint_in, source_in, adjoint_source_in, background_in, density_in,
    first, second, own_right, own_left, far, near, field, adjoint, source, adjoint_source, background, density,
    done,
):
    arrays = (
        (field_in, field), (adjoint_in, adjoint), (source_in, source), (adjoint_source_in, adjoint_source),
        (background_in, background), (density_in, density),
    )
    copies = [pltpu.make_async_copy(here, there, done.at[i]) for i, (here, there) in enumerate(arrays)]
    for copy in copies:
        copy.start()
    lane = lanes_of(ROWS)
    rightward = lax.axis_index("gx") % 2 == 1
    upward = lax.axis_index("gy") % 2 == 1
    low = rows_of(8) < 4
    for g in range(GROUPS):
        if g % 3 == 0:
            copies[g // 3].wait()
        planes = background if g == 12 else (field, adjoint, source, adjoint_source)[g // 3].at[g % 3]
        windows = []
        for t in range(2):
            window = None
            for q in range(Z // 2):
                here = turn(planes[2 * q + t], 32 * q + 12, 1)
                window = here if q == 0 else jnp.where(lane >= 32 * q, here, window)
            windows.append(window)
        half = lane % 32 < 16
        to_right = jnp.where(half, windows[0], turn(windows[1], 16, 1))
        to_left = jnp.where(half, turn(windows[0], -8, 1), turn(windows[1], 8, 1))
        own_right[g] = to_right
        own_left[g] = to_left
        first[g] = jnp.where(rightward, to_right, to_left)
        second[g] = jnp.where(rightward, to_left, to_right)
        for pair in range(Z // 2):
            k = g * (Z // 2) + pair
            down = jnp.where(low, planes[2 * pair, 0:8], turn(planes[2 * pair + 1, 0:8], 4, 0))
            up = jnp.where(low, turn(planes[2 * pair + 1, 8:16], 4, 0), planes[2 * pair, 8:16])
            far[k] = jnp.where(upward, up, down)
            near[k] = jnp.where(upward, down, up)
    for copy in copies[5:]:
        copy.wait()
    first[GROUPS] = density[...]
    second[GROUPS] = density[...]
    for part in range(2):
        far[4 * GROUPS + part] = density[8 * part : 8 * part + 8]
        near[4 * GROUPS + part] = density[8 * part : 8 * part + 8]


def gain_planes(design, material, contrast):
    chosen = material[:, :, None] == jnp.arange(contrast.shape[0], dtype=jnp.int32)
    tile_gain = design.astype(jnp.float32) * jnp.sum(jnp.where(chosen, contrast, 0.0), axis=2)
    tiles_y, tiles_x = design.shape
    place = jnp.arange(WRAP, dtype=jnp.int32)
    place = lax.axis_index("gy") * ROWS + jnp.where(place < 20, place, place - WRAP)
    tile_y = jnp.clip(place, 0, tiles_y * TILE - 1) // TILE
    tile_x = jnp.clip(lax.axis_index("gx") + jnp.array([0, 1, -1], jnp.int32), 0, tiles_x - 1)
    by_row = tile_y[:, None] == jnp.arange(tiles_y, dtype=jnp.int32)
    by_col = tile_x[:, None] == jnp.arange(tiles_x, dtype=jnp.int32)
    picked = by_row[None, :, :, None] & by_col[:, None, None, :]
    gains = jnp.sum(jnp.where(picked, tile_gain[None, None], 0.0), axis=(2, 3))
    return jnp.broadcast_to(gains[:, :, None], (3, WRAP, LANES))


def strip_kernel(own_right, own_left, far_rows, near_rows, first_got, second_got, strips, side, far, near):
    col = lax.axis_index("gx")
    rightward = col % 2 == 1
    upward = lax.axis_index("gy") % 2 == 1
    first, last = col == 0, col == lax.axis_size("gx") - 1
    lane = lanes_of(ROWS)
    within = lane % 16
    half = lane % 32 < 16
    low = rows_of(8) < 4

    far[0:PACKED] = far_rows[...]
    near[0:PACKED] = near_rows[...]

    def sides(g):
        from_right = jnp.where(rightward, first_got[g], second_got[g])
        from_left = jnp.where(rightward, second_got[g], first_got[g])
        return jnp.where(last, 0.0, from_right), jnp.where(first, 0.0, from_left)

    for g in range(GROUPS):
        from_right, from_left = sides(g)
        here_right = jnp.where(within >= HALO, from_right, own_left[g])
        here_left = jnp.where(within < 12, from_left, own_right[g])
        even = jnp.where(half, here_right, turn(here_left, 16, 1))
        odd = jnp.where(half, turn(here_right, -16, 1), here_left)
        strips[g, 0] = even
        strips[g, 1] = odd
        down = jnp.where(low, even[0:8], turn(odd[0:8], 4, 0))
        up = jnp.where(low, turn(odd[8:16], 4, 0), even[8:16])
        far[PACKED + g] = jnp.where(upward, up, down)
        near[PACKED + g] = jnp.where(upward, down, up)
    from_right, from_left = sides(GROUPS)
    beside = jnp.where(lane < 64, from_right, from_left)
    side[...] = beside
    for part in range(2):
        far[PACKED + GROUPS + part] = beside[8 * part : 8 * part + 8]
        near[PACKED + GROUPS + part] = beside[8 * part : 8 * part + 8]


def unpack(far, near, pick, second):
    if second:
        return turn(jnp.where(pick, near, far), 4, 0)
    return jnp.where(pick, far, near)


def main_kernel(
    gains, field, adjoint, source, adjoint_source, background, density,
    far, near, strips, side,
    fields, local_far, local_near,
    sources, curls, rate, keep, strip_fields, strip_sources, strip_curls, strip_rate, strip_keep, wide,
):
    col, row = lax.axis_index("gx"), lax.axis_index("gy")
    cols, rows = lax.axis_size("gx"), lax.axis_size("gy")
    first_row, last_row = row == 0, row == rows - 1
    low = rows_of(8) < 4
    upward = row % 2 == 1
    pick = jnp.where(upward, rows_of(8), 7 - rows_of(8)) < 4
    lane24, row24 = lanes_of(WRAP), rows_of(WRAP)
    outside8 = (low & last_row) | (jnp.logical_not(low) & first_row)
    outside = ((row24 >= 16) & (row24 < 20) & last_row) | ((row24 >= 20) & first_row)
    j = lane24 % 32
    outside_strip = outside | ((j >= HALO) & (j < 16) & (col == cols - 1)) | ((j >= 16) & (j < 28) & (col == 0))
    gain_main, gain_right, gain_left = gains[0], gains[1], gains[2]

    wide[16:32, 0:LANES] = density[...]
    wide[16:32, LANES : 2 * LANES] = side[...]
    for part in range(2):
        k, rows8 = 4 * GROUPS + part, slice(8 * part, 8 * part + 8)
        wide[rows8, 0:LANES] = jnp.where(first_row, 0.0, jnp.where(upward, near[k], far[k]))
        rows8 = slice(32 + 8 * part, 40 + 8 * part)
        wide[rows8, 0:LANES] = jnp.where(last_row, 0.0, jnp.where(upward, far[k], near[k]))
        k, rows8 = PACKED + GROUPS + part, slice(8 * part, 8 * part + 8)
        wide[rows8, LANES : 2 * LANES] = jnp.where(first_row, 0.0, jnp.where(upward, near[k], far[k]))
        rows8 = slice(32 + 8 * part, 40 + 8 * part)
        wide[rows8, LANES : 2 * LANES] = jnp.where(last_row, 0.0, jnp.where(upward, far[k], near[k]))
    filtered = cone(lambda a: wide[8 + a : 40 + a], 32)
    low2 = lax.broadcasted_iota(jnp.int32, (8, 2 * LANES), 0) < 4
    filtered = jnp.concatenate(
        [filtered[8:24], jnp.where(low2, filtered[24:32], filtered[0:8])], axis=0
    )
    design_main = gain_main * filtered[:, :LANES]
    beside = filtered[:, LANES:]
    block = filtered[:, :LANES]
    right_side = jnp.where(lane24 < HALO, turn(block, HALO, 1), turn(beside, HALO, 1))
    left_side = jnp.where(lane24 < 28, turn(beside, 28, 1), turn(block, 28, 1))
    quarter = jnp.where(lane24 < 16, right_side * gain_right, left_side * gain_left)
    quarter = jnp.where((lane24 < HALO) | (lane24 >= 28), turn_edges(right_side, left_side, lane24) * gain_main, quarter)
    quarter = jnp.where(lane24 < 32, quarter, 0.0)
    quarter = quarter + turn(quarter, 32, 1)
    design_strip = quarter + turn(quarter, 64, 1)

    def whole(inner, halo):
        return jnp.concatenate([inner, halo], axis=0)

    for z in range(Z):
        k = 48 + z // 2
        halo = unpack(far[k], near[k], pick, z % 2)
        step = 0.5 / (4.0 + 0.5 * (whole(background[z], halo) + design_main))
        step = jnp.where(outside, 0.0, step)
        rate[z] = step
        keep[z] = 0.5 + 4.0 * step
    for t in range(2):
        halo = unpack(far[PACKED + 12], near[PACKED + 12], pick, t)
        step = 0.5 / (4.0 + 0.5 * (whole(strips[12, t], halo) + design_strip))
        step = jnp.where(outside_strip, 0.0, step)
        strip_rate[t] = step
        strip_keep[t] = 0.5 + 4.0 * step

    starts = (field, adjoint, source, adjoint_source)
    for f in range(4):
        for c in range(3):
            g = 3 * f + c
            for z in range(Z):
                k = 4 * g + z // 2
                halo = unpack(far[k], near[k], pick, z % 2)
                if f < 2:
                    fields[f, c, z] = whole(starts[f][c, z], jnp.where(outside8, 0.0, halo))
                else:
                    sources[f - 2, c, z] = whole(starts[f][c, z], halo)
            for t in range(2):
                halo = unpack(far[PACKED + g], near[PACKED + g], pick, t)
                if f < 2:
                    strip_fields[f, c, t] = whole(strips[g, t], jnp.where(outside8, 0.0, halo))
                else:
                    strip_sources[f - 2, c, t] = whole(strips[g, t], halo)

    at_last, at_first = lane24 == LANES - 1, lane24 == 0

    def ahead_y(value):
        return turn(value, -1, 0)

    def behind_y(value):
        return turn(value, 1, 0)

    def ahead_x(value, strip, z):
        return jnp.where(at_last, turn(strip[z % 2], 123 - 32 * (z // 2), 1), turn(value, -1, 1))

    def behind_x(value, strip, z):
        return jnp.where(at_first, turn(strip[z % 2], -(32 * (z // 2) + 27), 1), turn(value, 1, 1))

    def sweep(kept_rows):
        for f in range(2):
            ex, ey, ez = ([strip_fields[f, c, t] for t in range(2)] for c in range(3))
            for t in range(2):
                if t == 0:
                    ex_z, ey_z = ex[1], ey[1]
                else:
                    ex_z = jnp.where(lane24 < 96, turn(ex[0], -32, 1), 0.0)
                    ey_z = jnp.where(lane24 < 96, turn(ey[0], -32, 1), 0.0)
                strip_curls[f, 0, t] = (ahead_y(ez[t]) - ez[t]) - (ey_z - ey[t])
                strip_curls[f, 1, t] = (ex_z - ex[t]) - (turn(ez[t], -1, 1) - ez[t])
                strip_curls[f, 2, t] = (turn(ey[t], -1, 1) - ey[t]) - (ahead_y(ex[t]) - ex[t])
            for z in range(Z):
                ex, ey, ez = (fields[f, c, z] for c in range(3))
                if z < Z - 1:
                    ex_z, ey_z = fields[f, 0, z + 1], fields[f, 1, z + 1]
                else:
                    ex_z = ey_z = jnp.zeros_like(ex)
                curls[f, 0, z] = (ahead_y(ez) - ez) - (ey_z - ey)
                curls[f, 1, z] = (ex_z - ex) - (ahead_x(ez, strip_fields.at[f, 2], z) - ez)
                curls[f, 2, z] = (ahead_x(ey, strip_fields.at[f, 1], z) - ey) - (ahead_y(ex) - ex)
        bottom = lane24 < 32
        for f in range(2):
            for t in range(2):
                ex, ey, ez = (strip_fields[f, c, t] for c in range(3))
                hx, hy, hz = (strip_curls[f, c, t] for c in range(3))
                if t == 1:
                    hx_z, hy_z = strip_curls[f, 0, 0], strip_curls[f, 1, 0]
                else:
                    hx_z = jnp.where(bottom, -ey, turn(strip_curls[f, 0, 1], 32, 1))
                    hy_z = jnp.where(bottom, ex, turn(strip_curls[f, 1, 1], 32, 1))
                curl_x = (hz - behind_y(hz)) - (hy - hy_z)
                curl_y = (hx - hx_z) - (hz - turn(hz, 1, 1))
                curl_z = (hy - turn(hy, 1, 1)) - (hx - behind_y(hx))
                step, kept = strip_rate[t], strip_keep[t]
                strip_fields[f, 0, t] = kept * ex + step * (strip_sources[f, 0, t] - curl_x)
                strip_fields[f, 1, t] = kept * ey + step * (strip_sources[f, 1, t] - curl_y)
                strip_fields[f, 2, t] = kept * ez + step * (strip_sources[f, 2, t] - curl_z)
            for z in range(Z):
                ex, ey, ez = (fields[f, c, z] for c in range(3))
                hx, hy, hz = (curls[f, c, z] for c in range(3))
                if z > 0:
                    hx_z, hy_z = curls[f, 0, z - 1], curls[f, 1, z - 1]
                else:
                    hx_z, hy_z = -ey, ex
                curl_x = (hz - behind_y(hz)) - (hy - hy_z)
                curl_y = (hx - hx_z) - (hz - behind_x(hz, strip_curls.at[f, 2], z))
                curl_z = (hy - behind_x(hy, strip_curls.at[f, 1], z)) - (hx - behind_y(hx))
                step, kept = rate[z], keep[z]
                fields[f, 0, z, 0:kept_rows] = (kept * ex + step * (sources[f, 0, z] - curl_x))[0:kept_rows]
                fields[f, 1, z, 0:kept_rows] = (kept * ey + step * (sources[f, 1, z] - curl_y))[0:kept_rows]
                fields[f, 2, z, 0:kept_rows] = (kept * ez + step * (sources[f, 2, z] - curl_z))[0:kept_rows]
    for number in range(ITERS):
        sweep(WRAP if number < ITERS - 1 else ROWS)

    product = jnp.zeros((ROWS, LANES), jnp.float32)
    strip_product = jnp.zeros((ROWS, LANES), jnp.float32)
    for c in range(3):
        for z in range(Z):
            product = product + fields[0, c, z, 0:ROWS] * fields[1, c, z, 0:ROWS]
        for t in range(2):
            strip_product = strip_product + strip_fields[0, c, t, 0:ROWS] * strip_fields[1, c, t, 0:ROWS]
    strip_product = strip_product + turn(strip_product, 64, 1)
    strip_product = strip_product + turn(strip_product, 32, 1)
    local = product * (-0.5 * gain_main[0:ROWS])
    lane = lanes_of(ROWS)
    local_side = jnp.where(
        lane < 64, turn(strip_product, -4, 1) * (-0.5 * gain_right[0:ROWS]),
        turn(strip_product, 100, 1) * (-0.5 * gain_left[0:ROWS]),
    )
    for out, value in ((slice(0, LANES), local), (slice(LANES, 2 * LANES), local_side)):
        local_far[:, out] = jnp.where(upward, value[8:16], value[0:8])
        local_near[:, out] = jnp.where(upward, value[0:8], value[8:16])


def turn_edges(right_side, left_side, lane):
    return jnp.where(lane < 16, right_side, left_side)


def last_kernel(fields, own_far, own_near, far, near, field, adjoint, gradient, wide, result, done):
    copies = [
        pltpu.make_async_copy(fields.at[f, :, :, pl.ds(0, ROWS)], out, done.at[f])
        for f, out in enumerate((field, adjoint))
    ]
    for copy in copies:
        copy.start()
    row = lax.axis_index("gy")
    upward = row % 2 == 1
    wide[0:8] = jnp.where(row == 0, 0.0, jnp.where(upward, near[...], far[...]))
    wide[8:16] = jnp.where(upward, own_near[...], own_far[...])
    wide[16:24] = jnp.where(upward, own_far[...], own_near[...])
    wide[24:32] = jnp.where(row == lax.axis_size("gy") - 1, 0.0, jnp.where(upward, far[...], near[...]))
    result[...] = cone(lambda a: wide[8 + a : 24 + a], ROWS)[:, :LANES]
    copies.append(pltpu.make_async_copy(result, gradient, done.at[2]))
    copies[2].start()
    for copy in copies:
        copy.wait()


def swaps(axis, start):
    size = lax.axis_size(axis)
    pairs = [(i, i + 1) for i in range(start, size - 1, 2)]
    return sorted(pairs + [(j, i) for i, j in pairs])


def swap_rows(far, near):
    return lax.ppermute(far, "gy", swaps("gy", 1)), lax.ppermute(near, "gy", swaps("gy", 0))


def shape(*dims):
    return jax.ShapeDtypeStruct(dims, jnp.float32)


def call(kernel, outs, space=VMEM, scratch=(), places=None):
    def run(*operands):
        return pl.pallas_call(
            kernel,
            out_shape=outs,
            in_specs=[pl.BlockSpec(memory_space=space)] * len(operands),
            out_specs=[pl.BlockSpec(memory_space=place) for place in places or [VMEM] * len(outs)],
            scratch_shapes=scratch,
            compiler_params=pltpu.CompilerParams(vmem_limit_bytes=LIMIT),
        )(*operands)

    return run


def room(*dims):
    return pltpu.VMEM(dims, jnp.float32)


def on_device(background, density, design_tiles, material_tiles, contrast, source, adjoint_source, field_start, adjoint_start):
    inner = (field_start, adjoint_start, source, adjoint_source, background, density)
    gains = gain_planes(design_tiles, material_tiles, contrast)
    edges, rows, packed = shape(GROUPS + 1, ROWS, LANES), shape(PACKED, 8, LANES), shape(PACKED + GROUPS + 2, 8, LANES)
    first, second, own_right, own_left, far, near, *inner = call(
        pack_kernel,
        [edges, edges, edges, edges, rows, rows] + [shape(*a.shape) for a in inner],
        space=pltpu.HBM,
        scratch=[pltpu.SemaphoreType.DMA((6,))],
    )(*[pltpu.with_memory_space_constraint(a, pltpu.HBM) for a in inner])
    first_got = lax.ppermute(first, "gx", swaps("gx", 1))
    second_got = lax.ppermute(second, "gx", swaps("gx", 0))
    strips, side, far, near = call(strip_kernel, [shape(GROUPS, 2, ROWS, LANES), shape(ROWS, LANES), packed, packed])(
        own_right, own_left, far, near, first_got, second_got
    )
    far_got, near_got = swap_rows(far, near)
    block, part = shape(3, Z, ROWS, LANES), shape(8, 2 * LANES)
    planes, sheets = (2, 3, Z, WRAP, LANES), (2, 3, 2, WRAP, LANES)
    fields, local_far, local_near = call(
        main_kernel,
        [room(*planes), part, part],
        scratch=[
            room(*planes), room(*planes), room(Z, WRAP, LANES), room(Z, WRAP, LANES),
            room(*sheets), room(*sheets), room(*sheets), room(2, WRAP, LANES), room(2, WRAP, LANES),
            room(48, 2 * LANES),
        ],
    )(gains, *inner, far_got, near_got, strips, side)
    local_far_got, local_near_got = swap_rows(local_far, local_near)
    field, adjoint, gradient = call(
        last_kernel,
        [block, block, shape(ROWS, LANES)],
        places=(pltpu.HBM,) * 3,
        scratch=[room(32, 2 * LANES), room(ROWS, LANES), pltpu.SemaphoreType.DMA((3,))],
    )(fields, local_far, local_near, local_far_got, local_near_got)
    return (field, adjoint, gradient)


def solution(mesh):
    in_specs = (
        P(None, "gy", "gx"),
        P("gy", "gx"),
        P(),
        P(),
        P(),
        P(None, None, "gy", "gx"),
        P(None, None, "gy", "gx"),
        P(None, None, "gy", "gx"),
        P(None, None, "gy", "gx"),
    )
    out_specs = (P(None, None, "gy", "gx"), P(None, None, "gy", "gx"), P("gy", "gx"))
    return jax.shard_map(on_device, mesh=mesh, in_specs=in_specs, out_specs=out_specs, check_vma=False)
```
